32 devices in a mesh: stream: 2 (over x), page: 16 (over z, y, core).
Axes of the slice: x: 2, y: 2, z: 4, core: 2. Of those that a mesh axis runs over, the one named last changes fastest.
Arguments:
- states: bfloat16 [2, 16, 640, 768], P('stream', 'page'), may hold values from -6 to 6
- counts: int32 [2, 16], P(None, 'page'), may hold values from 160 to 640, as said below
- box_x: int32 [16, 640], P('page'), may hold values from 0 to 63
- box_y: int32 [16, 640], P('page'), may hold values from 0 to 63
- ln1_gain: float32 [2, 768], P('stream'), may hold values from 0.5 to 1.5
- ln2_gain: float32 [2, 768], P('stream'), may hold values from 0.5 to 1.5
- box_table: float32 [2, 128, 24], P('stream'), may hold values from -4 to 4
- w_qkv: bfloat16 [2, 768, 2304], P('stream'), may hold values from -0.21875 to 0.21875
- w_out: bfloat16 [2, 768, 768], P('stream'), may hold values from -0.875 to 0.875
- w_cq: bfloat16 [2, 768, 768], P('stream'), may hold values from -0.21875 to 0.21875
- w_ckv: bfloat16 [2, 768, 1536], P('stream'), may hold values from -0.21875 to 0.21875
- w_cout: bfloat16 [2, 768, 768], P('stream'), may hold values from -0.875 to 0.875
- w_up: bfloat16 [2, 768, 3072], P('stream'), may hold values from -0.21875 to 0.21875
- w_down: bfloat16 [2, 3072, 768], P('stream'), may hold values from -0.109375 to 0.109375
- cotangent: bfloat16 [2, 16, 640, 768], P('stream', 'page'), may hold values from -6 to 6
Outputs:
- result: bfloat16 [2, 16, 640, 768], P('stream', 'page')
- states_grad: float32 [2, 16, 640, 768], P('stream', 'page')
- ln1_gain_grad: float32 [2, 768], P('stream', 'page')
- ln2_gain_grad: float32 [2, 768], P('stream', 'page')
- box_table_grad: float32 [2, 128, 24], P('stream', 'page')
- w_qkv_grad: float32 [2, 768, 2304], P('stream', 'page')
- w_out_grad: float32 [2, 768, 768], P('stream', 'page')
- w_cq_grad: float32 [2, 768, 768], P('stream', 'page')
- w_ckv_grad: float32 [2, 768, 1536], P('stream', 'page')
- w_cout_grad: float32 [2, 768, 768], P('stream', 'page')
- w_up_grad: float32 [2, 768, 3072], P('stream', 'page')
- w_down_grad: float32 [2, 3072, 768], P('stream', 'page')
The draws below stay inside these ranges and needn't reach their ends.
Inputs may be any that keep to these rules, and one draw needn't show every extreme that they name: counts[0] holds each page's text tokens, 640 on some page; counts[1] holds each page's patches, 256 for a 512-pixel page and 576 for a 768-pixel page.
All inputs are finite; a program needn't handle non-finite values.
Results may differ from the reference program's by a relative error of at most 0.015.
Values may be sent and summed in bfloat16 or wider, within the bound.
A program may use at most 256 MiB of HBM per device.

```python
import jax
import jax.numpy as jnp
from jax import lax

D = 768
H = 12
HD = 64
FF = 3072
L = 640
BOX = 64
GRID_SMALL = 16
GRID_LARGE = 24
PAGES = 16


def draw_counts(key, part):
    key = jax.random.fold_in(key, 11)
    text_key, top_key, group_key = jax.random.split(key, 3)
    text = jax.random.randint(text_key, (PAGES,), L // 4, L + 1).astype(jnp.int32)
    fullest = jax.random.randint(top_key, (), 0, PAGES)
    text = jnp.where(jnp.arange(PAGES) == fullest, L, text).astype(jnp.int32)
    group = jax.random.randint(group_key, (PAGES,), 0, 2)
    vision = jnp.where(group == 1, GRID_LARGE * GRID_LARGE, GRID_SMALL * GRID_SMALL).astype(jnp.int32)
    return jnp.stack((text, vision)).astype(jnp.int32)


def plant(result, stream_key, least, largest):
    longest = result.shape.index(max(result.shape))
    spots = []
    for shift in (0, 1):
        where = [jax.random.randint(jax.random.fold_in(stream_key, axis), (), 0, length) for axis, length in enumerate(result.shape)]
        where[longest] = (where[longest] + shift) % result.shape[longest]
        spots.append(tuple(where))
    return result.at[spots[0]].set(least).at[spots[1]].set(largest)


def shard_levels(own_key, extent, shards, least, high):
    gain = 1.0
    for dim, blocks in shards:
        heights = jax.random.uniform(jax.random.fold_in(jax.random.fold_in(own_key, 6), dim), (blocks,), jnp.float32, least / len(shards), high / len(shards))
        gain = gain * jnp.repeat(jnp.exp(heights), extent[dim] // blocks).reshape((-1,) + (1,) * (len(extent) - 1 - dim))
    return gain


def gaussian(rng, shape, deviation, most, cuts=(), dtype=jnp.bfloat16):
    loudness = shard_levels(rng, shape, cuts, -0.22, 0.18) if cuts else 1.0
    values = jax.random.normal(rng, shape, jnp.float32) * deviation * loudness
    return jnp.minimum(jnp.maximum(values, -most), most).astype(dtype)


def setup_inputs(seed: int = 0) -> dict:
    seeds = jax.random.split(jax.random.key(seed), 16)
    return {
        "states": gaussian(seeds[0], (2, PAGES, L, D), 1.0, 6.0, ((0, 2), (1, 16))),
        "counts": draw_counts(jax.random.fold_in(seeds[15], 71), 0),
        "box_x": plant(jax.random.randint(seeds[2], (PAGES, L), 0, BOX), jax.random.fold_in(seeds[2], 1), 0, BOX - 1).astype(jnp.int32),
        "box_y": plant(jax.random.randint(seeds[3], (PAGES, L), 0, BOX), jax.random.fold_in(seeds[3], 1), 0, BOX - 1).astype(jnp.int32),
        "ln1_gain": jnp.clip(1.0 + 0.1 * jax.random.normal(seeds[4], (2, D), jnp.float32), 0.5, 1.5),
        "ln2_gain": jnp.clip(1.0 + 0.1 * jax.random.normal(seeds[5], (2, D), jnp.float32), 0.5, 1.5),
        "box_table": gaussian(seeds[6], (2, 2 * BOX, 2 * H), 0.7, 4.0, ((0, 2),), jnp.float32),
        "w_qkv": gaussian(seeds[7], (2, D, 3 * D), D ** -0.5, 0.21875, ((0, 2),)),
        "w_out": gaussian(seeds[8], (2, D, D), (D // 16) ** -0.5, 0.875, ((0, 2),)),
        "w_cq": gaussian(seeds[9], (2, D, D), D ** -0.5, 0.21875, ((0, 2),)),
        "w_ckv": gaussian(seeds[10], (2, D, 2 * D), D ** -0.5, 0.21875, ((0, 2),)),
        "w_cout": gaussian(seeds[11], (2, D, D), (D // 16) ** -0.5, 0.875, ((0, 2),)),
        "w_up": gaussian(seeds[12], (2, D, FF), D ** -0.5, 0.21875, ((0, 2),)),
        "w_down": gaussian(seeds[13], (2, FF, D), FF ** -0.5, 0.109375, ((0, 2),)),
        "cotangent": gaussian(seeds[14], (2, PAGES, L, D), 1.0, 6.0, ((0, 2), (1, 16))),
    }


@jax.custom_vjp
def low(v):
    return lax.optimization_barrier(v.astype(jnp.bfloat16)).astype(jnp.float32)

@jax.custom_vjp
def low_back(v):
    return v

def low_keep(v):
    return (low(v), None)

def low_pass(kept, grad):
    return (grad,)

def back_keep(v):
    return (v, None)

def back_low(kept, grad):
    return (low(grad),)
low.defvjp(low_keep, low_pass)
low_back.defvjp(back_keep, back_low)
EPSILON = 1e-05
PRECISE = lax.Precision.HIGHEST
MASKED = -1000000000.0

def norm_rows(inputs, gain_row):
    centre = inputs - lax.optimization_barrier(jnp.mean(inputs, axis=-1, keepdims=True))
    spread = lax.optimization_barrier(jnp.mean(centre * centre, axis=-1, keepdims=True))
    return centre * lax.rsqrt(spread + EPSILON) * gain_row

def box_bias(bias_table, box_left, box_top, head_count):
    offset = bias_table.shape[0] // 2
    rel_left = box_left[:, None] - box_left[None, :] + offset
    rel_top = box_top[:, None] - box_top[None, :] + offset
    rows_left = jnp.take(bias_table[:, :head_count], rel_left, axis=0)
    rows_top = jnp.take(bias_table[:, head_count:], rel_top, axis=0)
    return jnp.transpose(rows_left + rows_top, (2, 0, 1))

def key_mask(key_count, slot_count):
    return jnp.where(jnp.arange(slot_count) < key_count, 0.0, MASKED).astype(jnp.float32)

def project(inputs, weight):
    return jnp.einsum('spld,sde->sple', inputs, weight, precision=PRECISE)

def self_page(queries, key_rows, values, bias_table, box_left, box_top, key_count):
    head_size = queries.shape[-1]
    scores = low_back(jnp.einsum('qhd,khd->hqk', queries, key_rows, precision=PRECISE) * head_size ** (-0.5))
    scores = scores + box_bias(bias_table, box_left, box_top, queries.shape[1]) + key_mask(key_count, key_rows.shape[0])
    weights = low(jax.nn.softmax(scores, axis=-1))
    return jnp.einsum('hqk,khd->qhd', weights, values, precision=PRECISE)

def cross_page(queries, key_rows, values, key_count):
    head_size = queries.shape[-1]
    scores = low_back(jnp.einsum('qhd,khd->hqk', queries, key_rows, precision=PRECISE) * head_size ** (-0.5))
    scores = scores + key_mask(key_count, key_rows.shape[0])
    weights = low(jax.nn.softmax(scores, axis=-1))
    return jnp.einsum('hqk,khd->qhd', weights, values, precision=PRECISE)

def patch_grid(patch_counts):
    slots = jnp.arange(L).astype(jnp.int32)[None, :]
    side = jnp.where(patch_counts > GRID_SMALL * GRID_SMALL, GRID_LARGE, GRID_SMALL).astype(jnp.int32)[:, None]
    return ((slots % side).astype(jnp.int32), (slots // side).astype(jnp.int32))

def forward(states, ln1_gain, ln2_gain, box_table, w_qkv, w_out, w_cq, w_ckv, w_cout, w_up, w_down, counts, box_x, box_y):
    valid = (jnp.arange(L)[None, None, :] < counts[:, :, None]).astype(jnp.float32)[..., None]
    grid_left, grid_top = patch_grid(counts[1])
    lefts = jnp.stack((box_x, grid_left)).reshape(2 * PAGES, L).astype(jnp.int32)
    tops = jnp.stack((box_y, grid_top)).reshape(2 * PAGES, L).astype(jnp.int32)
    low_normed = low(norm_rows(states, ln1_gain[:, None, None, :]))
    joined = low(low_back(project(low_normed, w_qkv))).reshape(2 * PAGES, L, 3, H, HD)
    tables = jnp.repeat(box_table, PAGES, axis=0)
    attended = lax.map(lambda page_items: jax.checkpoint(self_page)(*page_items), (joined[:, :, 0], joined[:, :, 1], joined[:, :, 2], tables, lefts, tops, counts.reshape(2 * PAGES)))
    attended = low(low_back(attended)).reshape(2, PAGES, L, D)
    middle = states + low_back(project(attended, w_out))
    low_middle = low(middle)
    cross_query = low(low_back(project(low_middle, w_cq))).reshape(2 * PAGES, L, H, HD)
    cross_pairs = low(low_back(project(low_normed, w_ckv)))[::-1].reshape(2 * PAGES, L, 2, H, HD)
    crossed = lax.map(lambda page_items: jax.checkpoint(cross_page)(*page_items), (cross_query, cross_pairs[:, :, 0], cross_pairs[:, :, 1], counts[::-1].reshape(2 * PAGES)))
    crossed = low(low_back(crossed)).reshape(2, PAGES, L, D)
    after_cross = middle + low_back(project(crossed, w_cout))
    low_second = low(norm_rows(after_cross, ln2_gain[:, None, None, :]))
    hidden = low(jax.nn.gelu(low_back(project(low_second, w_up)), approximate=False))
    return (after_cross + project(hidden, w_down)) * valid

def reference(states, counts, box_x, box_y, ln1_gain, ln2_gain, box_table, w_qkv, w_out, w_cq, w_ckv, w_cout, w_up, w_down, cotangent):

    def run_block(states_in, gain_one, gain_two, table_in, qkv_in, out_in, cq_in, ckv_in, cout_in, up_in, down_in):
        return forward(states_in, gain_one, gain_two, table_in, qkv_in, out_in, cq_in, ckv_in, cout_in, up_in, down_in, counts, box_x, box_y)
    inputs = (states.astype(jnp.float32), ln1_gain.astype(jnp.float32), ln2_gain.astype(jnp.float32), box_table.astype(jnp.float32), w_qkv.astype(jnp.float32), w_out.astype(jnp.float32), w_cq.astype(jnp.float32), w_ckv.astype(jnp.float32), w_cout.astype(jnp.float32), w_up.astype(jnp.float32), w_down.astype(jnp.float32))
    outcome, pull_back = jax.vjp(run_block, *inputs)
    grads = pull_back(cotangent.astype(jnp.float32))
    return (outcome.astype(jnp.bfloat16), grads[0], grads[1], grads[2], grads[3], grads[4], grads[5], grads[6], grads[7], grads[8], grads[9], grads[10])
```

```python
import functools

import jax
import jax.numpy as jnp
from jax import lax
from jax.experimental import pallas as pl
from jax.experimental.pallas import tpu as pltpu
from jax.sharding import PartitionSpec as P

GRID_SMALL = 16
GRID_LARGE = 24
EPSILON = 1e-05
MASKED = -1000000000.0
BF = jnp.bfloat16
F32 = jnp.float32
WIDE = 128


def contract(left, right, left_dim, right_dim):
    return lax.dot_general(
        left, right, (((left_dim,), (right_dim,)), ((), ())), preferred_element_type=F32
    )


def params(mib=48):
    return pltpu.CompilerParams(vmem_limit_bytes=mib << 20)


def cost(us):
    return pl.CostEstimate(flops=int(us * 1.1e9), bytes_accessed=1 << 20, transcendentals=0)


def swapped(shard, axis, mask):
    return lax.ppermute(shard, axis, [(i, i ^ mask) for i in range(lax.axis_size(axis))])


def pieces(row):
    high = row.astype(BF).astype(F32)
    rest = row - high
    middle = rest.astype(BF).astype(F32)
    return high, middle, rest - middle


def extra_rows(rows, count):
    index = lax.broadcasted_iota(jnp.int32, (16, count), 0)
    block = jnp.zeros((16, count), F32)
    for place, row in enumerate(rows):
        block = jnp.where(index == place, row, block)
    return block.astype(BF)


def forward_kernel(has_bias, scale, *refs):
    if has_bias:
        q_ref, k_ref, v_ref, mask_ref, band_ref, onehot_ref, o_ref, lse_ref = refs
        onehot = onehot_ref[...]
    else:
        q_ref, k_ref, v_ref, mask_ref, o_ref, lse_ref = refs
    count = q_ref.shape[0]
    half = WIDE // 2
    queries = (q_ref[...] * scale).T
    key_rows = k_ref[...].T
    values = v_ref[...].T
    ones = jnp.ones((1, count), F32)
    query_extra = extra_rows([ones], count)
    key_extra = extra_rows([mask_ref[...]], count)
    outs = []
    for side in range(2):
        part = slice(half * side, half * side + half)
        if has_bias:
            band = contract(band_ref[side], onehot, 1, 0).astype(BF)
            left = jnp.concatenate([key_rows[part], onehot, key_extra], 0)
            right = jnp.concatenate([queries[part], band, query_extra], 0)
        else:
            left = jnp.concatenate([key_rows[part], key_extra], 0)
            right = jnp.concatenate([queries[part], query_extra], 0)
        scores = contract(left, right, 0, 0)
        top = jnp.max(scores, axis=0, keepdims=True)
        weights = jnp.exp(scores - top).astype(BF)
        output = contract(jnp.concatenate([values[part], query_extra], 0), weights, 1, 0)
        total = output[half : half + 1]
        outs.append(output[:half] * (1.0 / total))
        lse_ref[0, side : side + 1, :] = top + jnp.log(total)
    o_ref[...] = jnp.concatenate(outs, 0).astype(BF).T


def backward_kernel(has_bias, scale, *refs):
    if has_bias:
        (q_ref, k_ref, v_ref, do_ref, o_ref, lse_ref, mask_ref, band_ref, onehot_ref, flipped_ref) = refs[:10]
        dq_ref, dkv_ref, db_ref = refs[10:]
        onehot = onehot_ref[...]
        flipped = flipped_ref[...]
    else:
        q_ref, k_ref, v_ref, do_ref, o_ref, lse_ref, mask_ref = refs[:7]
        dq_ref, dkv_ref = refs[7:]
    count = q_ref.shape[0]
    half = WIDE // 2
    queries = (q_ref[...] * scale).T
    key_rows = k_ref[...].T
    values = v_ref[...].T
    grad_out = do_ref[...].T
    product = grad_out.astype(F32) * o_ref[...].T.astype(F32)
    ones = jnp.ones((1, count), F32)
    key_extra = extra_rows([ones, ones, ones, mask_ref[...]], count)
    value_extra = extra_rows([ones, ones, ones], count)
    d_queries, d_keys, d_values = [], [], []
    for side in range(2):
        part = slice(half * side, half * side + half)
        lse_rows = extra_rows([*pieces(-lse_ref[0, side : side + 1, :]), ones], count)
        delta = jnp.sum(product[part], axis=0, keepdims=True)
        delta_rows = extra_rows(list(pieces(-delta)), count)
        if has_bias:
            band = contract(band_ref[side], onehot, 1, 0).astype(BF)
            left = jnp.concatenate([queries[part], band, lse_rows], 0)
            right = jnp.concatenate([key_rows[part], onehot, key_extra], 0)
        else:
            left = jnp.concatenate([queries[part], lse_rows], 0)
            right = jnp.concatenate([key_rows[part], key_extra], 0)
        weights = jnp.exp(contract(left, right, 0, 0))
        d_weights = contract(
            jnp.concatenate([grad_out[part], delta_rows], 0),
            jnp.concatenate([values[part], value_extra], 0),
            0,
            0,
        )
        d_scores = (weights * d_weights).astype(BF)
        d_values.append(contract(grad_out[part], weights.astype(BF), 1, 0))
        d_keys.append(contract(queries[part], d_scores, 1, 0))
        scaled = key_rows[part] * scale
        if has_bias:
            both = contract(jnp.concatenate([scaled, onehot], 0), d_scores, 1, 1)
            d_queries.append(both[:half])
            db_ref[side] = contract(flipped, both[half:].astype(BF), 1, 1)
        else:
            d_queries.append(contract(scaled, d_scores, 1, 1))
    dq_ref[...] = jnp.concatenate(d_queries, 0).astype(BF).T
    dkv_ref[0] = jnp.concatenate(d_keys, 0).astype(BF).T
    dkv_ref[1] = jnp.concatenate(d_values, 0).astype(BF).T


def column(first):
    return lambda i: (0, first + i)


def attend_forward(query_rows, key_value_rows, first, mask, bias, scale, us):
    count = query_rows.shape[0]
    pairs = key_value_rows.shape[1] // WIDE // (3 if first else 2)
    block = lambda start: pl.BlockSpec((count, WIDE), column(start))
    row = pl.BlockSpec((1, count), lambda i: (0, 0))
    wide = pl.BlockSpec((WIDE, count), lambda i: (0, 0))
    specs = [block(0), block(first), block(first + pairs), row]
    operands = [query_rows, key_value_rows, key_value_rows, mask]
    if bias is not None:
        specs += [pl.BlockSpec((2, WIDE, WIDE), lambda i: (i, 0, 0)), wide]
        operands += [bias[0], bias[1]]
    return pl.pallas_call(
        functools.partial(forward_kernel, bias is not None, scale),
        grid=(pairs,),
        in_specs=specs,
        out_specs=[block(0), pl.BlockSpec((1, 2, count), lambda i: (i, 0, 0))],
        out_shape=[
            jax.ShapeDtypeStruct((count, pairs * WIDE), BF),
            jax.ShapeDtypeStruct((pairs, 2, count), F32),
        ],
        compiler_params=params(),
        cost_estimate=cost(us),
    )(*operands)


def attend_backward(query_rows, key_value_rows, first, grad_out, output, lse, mask, bias, scale, us):
    count = query_rows.shape[0]
    pairs = lse.shape[0]
    block = lambda start: pl.BlockSpec((count, WIDE), column(start))
    row = pl.BlockSpec((1, count), lambda i: (0, 0))
    wide = pl.BlockSpec((WIDE, count), lambda i: (0, 0))
    band = pl.BlockSpec((2, WIDE, WIDE), lambda i: (i, 0, 0))
    specs = [
        block(0),
        block(first),
        block(first + pairs),
        block(0),
        block(0),
        pl.BlockSpec((1, 2, count), lambda i: (i, 0, 0)),
        row,
    ]
    operands = [query_rows, key_value_rows, key_value_rows, grad_out, output, lse, mask]
    out_specs = [block(0), pl.BlockSpec((2, count, WIDE), lambda i: (0, 0, i))]
    out_shape = [
        jax.ShapeDtypeStruct((count, pairs * WIDE), BF),
        jax.ShapeDtypeStruct((2, count, pairs * WIDE), BF),
    ]
    if bias is not None:
        specs += [band, wide, wide]
        operands += list(bias)
        out_specs.append(band)
        out_shape.append(jax.ShapeDtypeStruct((2 * pairs, WIDE, WIDE), F32))
    return pl.pallas_call(
        functools.partial(backward_kernel, bias is not None, scale),
        grid=(pairs,),
        in_specs=specs,
        out_specs=out_specs,
        out_shape=out_shape,
        compiler_params=params(),
        cost_estimate=cost(us),
    )(*operands)


def same_block(shape):
    rows = lax.broadcasted_iota(jnp.int32, shape, 0) // (WIDE // 2)
    columns = lax.broadcasted_iota(jnp.int32, shape, 1) // (WIDE // 2)
    return rows == columns


def band_kernel(table_ref, band_ref):
    heads = band_ref.shape[0]
    shape = (WIDE, WIDE)
    keep = same_block(shape)
    lower = lax.broadcasted_iota(jnp.int32, shape, 0) >= WIDE // 2
    for head in range(heads):
        across = jnp.broadcast_to(table_ref[head : head + 1, :], shape)
        down = jnp.broadcast_to(table_ref[heads + head : heads + head + 1, :], shape)
        rolled = pltpu.roll(jnp.where(lower, down, across), WIDE // 2, 1, stride=1, stride_axis=0)
        band_ref[head] = jnp.where(keep, rolled, 0.0).astype(BF)


def make_bands(table):
    heads = table.shape[1] // 2
    return pl.pallas_call(
        band_kernel,
        out_shape=jax.ShapeDtypeStruct((heads, WIDE, WIDE), BF),
        compiler_params=params(),
        cost_estimate=cost(3),
    )(table.T)


def unband_kernel(grad_ref, table_ref):
    heads = grad_ref.shape[0]
    half = WIDE // 2
    shape = (WIDE, WIDE)
    keep = same_block(shape)
    for head in range(heads):
        rolled = pltpu.roll(jnp.where(keep, grad_ref[head], 0.0), 0, 1, stride=1, stride_axis=0)
        table_ref[head : head + 1, :] = jnp.sum(rolled[:half], axis=0, keepdims=True)
        table_ref[heads + head : heads + head + 1, :] = jnp.sum(rolled[half:], axis=0, keepdims=True)


def gather_bands(grads):
    heads = grads.shape[0]
    flipped = pl.pallas_call(
        unband_kernel,
        out_shape=jax.ShapeDtypeStruct((2 * heads, WIDE), F32),
        compiler_params=params(),
        cost_estimate=cost(3),
    )(grads)
    return flipped[:, ::-1].T


def gelu_pair(value):
    distance = jnp.abs(value) * 0.7071067811865476
    bell = jnp.exp(-0.5 * value * value)
    t = 1.0 / (1.0 + 0.3275911 * distance)
    poly = t * (0.254829592 + t * (-0.284496736 + t * (1.421413741 + t * (-1.453152027 + t * 1.061405429))))
    tail = 0.5 * poly * bell
    phi = jnp.where(value >= 0, 1.0 - tail, tail)
    return value * phi, phi + value * bell * 0.3989422804014327


def feed_kernel(me_ref, second_ref, grad_ref, up_ref, down_ref, hidden_ref, d_up_ref, send_ref, keep_ref, sums_ref):
    tile = pl.program_id(0)
    grad = grad_ref[...]
    value = contract(second_ref[...], up_ref[...], 1, 0)
    hidden, slope = gelu_pair(value)
    hidden = hidden.astype(BF)
    hidden_ref[...] = hidden
    back = contract(grad, down_ref[...], 1, 1)
    d_up_ref[...] = (slope * back).astype(BF)
    sums_ref[...] = contract(hidden, grad, 0, 0)
    rows = send_ref.shape[1]
    per_tile = sums_ref.shape[0] // rows
    place_rows(me_ref[0], tile * per_tile, per_tile, rows, sums_ref, send_ref, keep_ref, 0)


def place_rows(me, first, number, rows, sums_ref, send_ref, keep_ref, offset):
    halves = send_ref.shape[0]
    quarters = halves // 2
    for local in range(number):
        relative = (first + local) ^ me
        slot = ((relative >> 1) & 1) * quarters + (relative >> 2)
        block = sums_ref[local * rows : local * rows + rows, :].astype(BF)

        @pl.when(relative & 1 == 1)
        def _():
            send_ref[slot, offset : offset + rows, :] = block

        @pl.when(relative & 1 == 0)
        def _():
            keep_ref[slot, offset : offset + rows, :] = block


def feed_forward(me, second, grad, w_up, w_down, parts):
    count, width = second.shape
    hidden_width = w_up.shape[1]
    rows = hidden_width // parts
    tiles = hidden_width // width
    whole = pl.BlockSpec((count, width), lambda i, me: (0, 0))
    tile = pl.BlockSpec((count, width), lambda i, me: (0, i))
    slots = pl.BlockSpec((parts // 2, rows, width), lambda i, me: (0, 0, 0))
    return pl.pallas_call(
        feed_kernel,
        grid_spec=pltpu.PrefetchScalarGridSpec(
            num_scalar_prefetch=1,
            grid=(tiles,),
            in_specs=[
                whole,
                whole,
                pl.BlockSpec((width, width), lambda i, me: (0, i)),
                pl.BlockSpec((width, width), lambda i, me: (i, 0)),
            ],
            out_specs=[tile, tile, slots, slots],
            scratch_shapes=[pltpu.VMEM((width, width), F32)],
        ),
        out_shape=[
            jax.ShapeDtypeStruct((count, hidden_width), BF),
            jax.ShapeDtypeStruct((count, hidden_width), BF),
            jax.ShapeDtypeStruct((parts // 2, rows, width), BF),
            jax.ShapeDtypeStruct((parts // 2, rows, width), BF),
        ],
        compiler_params=params(56),
        cost_estimate=cost(22),
    )(me, second, grad, w_up, w_down)


def outer_kernel(plan, rows, me_ref, *refs):
    tile = pl.program_id(0)
    lefts, rights = refs[: len(plan)], refs[len(plan) : 2 * len(plan)]
    send_ref, keep_ref, sums_ref = refs[2 * len(plan) :]
    number = 2 * send_ref.shape[0]
    first = 0
    for (tiles,), left_ref, right_ref in zip(plan, lefts, rights):
        for step in range(tiles):

            @pl.when(tile == first + step)
            def _(left_ref=left_ref, right_ref=right_ref, offset=(first + step) * rows):
                sums_ref[...] = contract(left_ref[...], right_ref[...], 0, 0)
                place_rows(me_ref[0], 0, number, rows, sums_ref, send_ref, keep_ref, offset)

        first += tiles


def outer_products(me, pairs, parts, us, extra=None):
    count, width = pairs[0][0].shape
    rows = width // parts
    plan, specs_left, specs_right = [], [], []
    first = 0
    for left, right in pairs:
        tiles = right.shape[1] // width
        plan.append((tiles,))
        specs_left.append(pl.BlockSpec((count, width), lambda i, me: (0, 0)))
        specs_right.append(
            pl.BlockSpec(
                (count, width),
                lambda i, me, first=first, tiles=tiles: (0, jnp.clip(i - first, 0, tiles - 1)),
            )
        )
        first += tiles
    slots = pl.BlockSpec((parts // 2, first * rows, width), lambda i, me: (0, 0, 0))
    shape = jax.ShapeDtypeStruct((parts // 2, first * rows, width), BF)
    return pl.pallas_call(
        functools.partial(outer_kernel, plan, rows),
        grid_spec=pltpu.PrefetchScalarGridSpec(
            num_scalar_prefetch=1,
            grid=(first,),
            in_specs=specs_left + specs_right,
            out_specs=[slots, slots],
            scratch_shapes=[pltpu.VMEM((width, width), F32)],
        ),
        out_shape=[shape, shape],
        compiler_params=params(56),
        cost_estimate=cost(us),
    )(me, *[left for left, _ in pairs], *[right for _, right in pairs])


def reduce_parts(send, keep):
    half = send.shape[0] // 2
    arrived = swapped(send, "page", 1).astype(F32)
    away = (arrived[half:] + keep[half:].astype(F32)).astype(BF)
    mine = arrived[:half] + keep[:half].astype(F32)
    mine = mine + swapped(away, "page", 2).astype(F32)
    total = mine[0]
    for step in range(1, half):
        total = total + swapped(mine[step].astype(BF), "page", 4 * step).astype(F32)
    return total


def norm_rows(inputs, gain_row):
    centre = inputs - jnp.mean(inputs, axis=-1, keepdims=True)
    spread = jnp.mean(centre * centre, axis=-1, keepdims=True)
    return centre * lax.rsqrt(spread + EPSILON) * gain_row


def matmul(left, right):
    return contract(left, right, 1, 0)


def matmul_back(left, weight):
    return contract(left, weight, 1, 1)


def onehots(left, top, buckets):
    index = jnp.arange(buckets)[:, None]
    return jnp.concatenate([left[None, :] == index, top[None, :] == index], 0).astype(BF)


def body(
    states,
    counts,
    box_x,
    box_y,
    ln1_gain,
    ln2_gain,
    box_table,
    w_qkv,
    w_out,
    w_cq,
    w_ckv,
    w_cout,
    w_up,
    w_down,
    cotangent,
):
    slot_count, width = states.shape[2], states.shape[3]
    heads = box_table.shape[2] // 2
    buckets = box_table.shape[1] // 2
    scale = (width // heads) ** (-0.5)
    pairs = heads // 2
    parts = lax.axis_size("page")
    side = lax.axis_index("stream")
    me = lax.axis_index("page").astype(jnp.int32).reshape(1)
    own_count = jnp.take(counts[:, 0], side)
    other_count = jnp.take(counts[:, 0], 1 - side)
    slots = jnp.arange(slot_count)
    grid_side = jnp.where(own_count > GRID_SMALL * GRID_SMALL, GRID_LARGE, GRID_SMALL)
    left = jnp.where(side == 0, box_x[0], slots % grid_side)
    top = jnp.where(side == 0, box_y[0], slots // grid_side)
    onehot = onehots(left, top, buckets)
    flipped = onehots(buckets - 1 - left, buckets - 1 - top, buckets)
    mask_own = jnp.where(slots < own_count, 0.0, MASKED).astype(F32)[None]
    mask_other = jnp.where(slots < other_count, 0.0, MASKED).astype(F32)[None]
    valid = (slots < own_count).astype(F32)[:, None]
    bands = make_bands(box_table[0])
    weights = [w[0] for w in (w_qkv, w_out, w_cq, w_ckv, w_cout, w_up, w_down)]
    w_qkv, w_out, w_cq, w_ckv, w_cout, w_up, w_down = weights

    inputs = states[0, 0].astype(F32)
    normed, norm_pull = jax.vjp(norm_rows, inputs, ln1_gain[0])
    normed = normed.astype(BF)
    cross_kv = matmul(normed, w_ckv).astype(BF)
    partner = swapped(cross_kv, "stream", 1)
    joined = matmul(normed, w_qkv).astype(BF)
    attended, self_lse = attend_forward(joined, joined, pairs, mask_own, (bands, onehot), scale, 18)
    middle = inputs + matmul(attended, w_out)
    low_middle = middle.astype(BF)
    cross_query = matmul(low_middle, w_cq).astype(BF)
    crossed, cross_lse = attend_forward(cross_query, partner, 0, mask_other, None, scale, 16)
    after_cross = middle + matmul(crossed, w_cout)
    second, second_pull = jax.vjp(norm_rows, after_cross, ln2_gain[0])
    second = second.astype(BF)
    out_grad = cotangent[0, 0].astype(F32) * valid
    low_grad = out_grad.astype(BF)
    hidden, d_up, *down_parts = feed_forward(me, second, low_grad, w_up, w_down, parts)
    down_sum = reduce_parts(*down_parts)
    up_sum = reduce_parts(*outer_products(me, [(second, d_up)], parts, 6))
    d_after, ln2_grad = second_pull(matmul_back(d_up, w_up))
    d_after = d_after + out_grad
    low_after = d_after.astype(BF)
    d_crossed = matmul_back(low_after, w_cout).astype(BF)
    d_cross_query, d_partner = attend_backward(
        cross_query, partner, 0, d_crossed, crossed, cross_lse, mask_other, None, scale, 26
    )
    returned = swapped(d_partner, "stream", 1)
    d_middle = d_after + matmul_back(d_cross_query, w_cq)
    low_d_middle = d_middle.astype(BF)
    d_attended = matmul_back(low_d_middle, w_out).astype(BF)
    mid_sum = reduce_parts(
        *outer_products(
            me, [(crossed, low_after), (low_middle, d_cross_query), (attended, low_d_middle)], parts, 6
        )
    )
    d_query, d_pair, d_bands = attend_backward(
        joined, joined, pairs, d_attended, attended, self_lse, mask_own, (bands, onehot, flipped), scale, 29
    )
    table_grad = gather_bands(d_bands)
    d_normed = (
        matmul_back(d_query, w_qkv[:, :width])
        + matmul_back(d_pair[0], w_qkv[:, width : 2 * width])
        + matmul_back(d_pair[1], w_qkv[:, 2 * width :])
        + matmul_back(returned[0], w_ckv[:, :width])
        + matmul_back(returned[1], w_ckv[:, width:])
    )
    d_inputs, ln1_grad = norm_pull(d_normed)
    states_grad = d_inputs + d_middle
    last_send, last_keep = outer_products(
        me,
        [
            (normed, d_query),
            (normed, d_pair[0]),
            (normed, d_pair[1]),
            (normed, returned[0]),
            (normed, returned[1]),
        ],
        parts,
        10,
    )
    last_sum = reduce_parts(last_send, last_keep)
    small = jnp.concatenate(
        [ln1_grad.reshape(parts, -1), ln2_grad.reshape(parts, -1), table_grad.reshape(parts, -1)], 1
    )
    small_sum = reduce_small(me[0], small)
    result = ((after_cross + matmul(hidden, w_down)) * valid).astype(BF)

    rows = width // parts
    table_rows = 2 * buckets // parts

    def wide(block):
        return block.reshape(-1, rows, width).transpose(1, 0, 2).reshape(1, rows, -1)

    return (
        result[None, None],
        states_grad[None, None],
        small_sum[None, :rows],
        small_sum[None, rows : 2 * rows],
        small_sum[2 * rows :].reshape(1, table_rows, 2 * heads),
        wide(last_sum[: 3 * rows]),
        wide(mid_sum[2 * rows :]),
        wide(mid_sum[rows : 2 * rows]),
        wide(last_sum[3 * rows :]),
        wide(mid_sum[:rows]),
        wide(up_sum),
        down_sum[None],
    )


def reduce_small(me, small):
    parts = small.shape[0]
    order = jnp.arange(parts) ^ me
    small = jnp.take(small, order, axis=0).reshape(parts // 4, 2, 2, -1)
    small = small[:, :, 0] + swapped(small[:, :, 1], "page", 1)
    small = small[:, 0] + swapped(small[:, 1], "page", 2)
    total = small[0]
    for step in range(1, parts // 4):
        total = total + swapped(small[step], "page", 4 * step)
    return total


def solution(mesh):
    placed = (
        P("stream", "page", None, None),
        P(None, "page"),
        P("page", None),
        P("page", None),
        P("stream", None),
        P("stream", None),
        P("stream", None, None),
        P("stream", None, None),
        P("stream", None, None),
        P("stream", None, None),
        P("stream", None, None),
        P("stream", None, None),
        P("stream", None, None),
        P("stream", None, None),
        P("stream", "page", None, None),
    )
    return jax.shard_map(
        body,
        mesh=mesh,
        in_specs=placed,
        out_specs=(
            P("stream", "page", None, None),
            P("stream", "page", None, None),
            P("stream", "page"),
            P("stream", "page"),
            P("stream", "page", None),
            P("stream", "page", None),
            P("stream", "page", None),
            P("stream", "page", None),
            P("stream", "page", None),
            P("stream", "page", None),
            P("stream", "page", None),
            P("stream", "page", None),
        ),
        check_vma=False,
    )
```

```python
import functools

import jax
import jax.numpy as jnp
from jax import lax
from jax.experimental import pallas as pl
from jax.experimental.pallas import tpu as pltpu
from jax.sharding import PartitionSpec as P

GRID_SMALL = 16
GRID_LARGE = 24
EPSILON = 1e-05
MASKED = -1000000000.0
BF = jnp.bfloat16
F32 = jnp.float32
WIDE = 128


def contract(left, right, left_dim, right_dim):
    return lax.dot_general(
        left, right, (((left_dim,), (right_dim,)), ((), ())), preferred_element_type=F32
    )


def params(mib=48):
    return pltpu.CompilerParams(vmem_limit_bytes=mib << 20)


def cost(us):
    return pl.CostEstimate(flops=int(us * 1.1e9), bytes_accessed=1 << 20, transcendentals=0)


def swapped(shard, axis, mask):
    return lax.ppermute(shard, axis, [(i, i ^ mask) for i in range(lax.axis_size(axis))])


def pieces(row):
    high = row.astype(BF).astype(F32)
    rest = row - high
    middle = rest.astype(BF).astype(F32)
    return high, middle, rest - middle


def extra_rows(rows, count):
    index = lax.broadcasted_iota(jnp.int32, (16, count), 0)
    block = jnp.zeros((16, count), F32)
    for place, row in enumerate(rows):
        block = jnp.where(index == place, row, block)
    return block.astype(BF)


def forward_kernel(has_bias, scale, *refs):
    if has_bias:
        q_ref, k_ref, v_ref, mask_ref, band_ref, onehot_ref, o_ref, lse_ref = refs
        onehot = onehot_ref[...]
    else:
        q_ref, k_ref, v_ref, mask_ref, o_ref, lse_ref = refs
    count = q_ref.shape[0]
    half = WIDE // 2
    queries = (q_ref[...] * scale).T
    key_rows = k_ref[...].T
    values = v_ref[...].T
    ones = jnp.ones((1, count), F32)
    query_extra = extra_rows([ones], count)
    key_extra = extra_rows([mask_ref[...]], count)
    outs = []
    for side in range(2):
        part = slice(half * side, half * side + half)
        if has_bias:
            band = contract(band_ref[side], onehot, 1, 0).astype(BF)
            left = jnp.concatenate([key_rows[part], onehot, key_extra], 0)
            right = jnp.concatenate([queries[part], band, query_extra], 0)
        else:
            left = jnp.concatenate([key_rows[part], key_extra], 0)
            right = jnp.concatenate([queries[part], query_extra], 0)
        scores = contract(left, right, 0, 0)
        top = jnp.max(scores, axis=0, keepdims=True)
        weights = jnp.exp(scores - top).astype(BF)
        output = contract(jnp.concatenate([values[part], query_extra], 0), weights, 1, 0)
        total = output[half : half + 1]
        outs.append(output[:half] * (1.0 / total))
        lse_ref[0, side : side + 1, :] = top + jnp.log(total)
    o_ref[...] = jnp.concatenate(outs, 0).astype(BF).T


def backward_pair(scale, queries, key_rows, values, grad_out, output, lse, mask, bias):
    if bias is not None:
        bands, onehot, flipped = bias
    count = queries.shape[0]
    half = WIDE // 2
    queries = (queries * scale).T
    key_rows = key_rows.T
    values = values.T
    grad_out = grad_out.T
    product = grad_out.astype(F32) * output.T.astype(F32)
    ones = jnp.ones((1, count), F32)
    key_extra = extra_rows([ones, ones, ones, mask], count)
    value_extra = extra_rows([ones, ones, ones], count)
    d_queries, d_keys, d_values, d_bands = [], [], [], []
    for side in range(2):
        part = slice(half * side, half * side + half)
        lse_rows = extra_rows([*pieces(-lse[side : side + 1, :]), ones], count)
        delta = jnp.sum(product[part], axis=0, keepdims=True)
        delta_rows = extra_rows(list(pieces(-delta)), count)
        if bias is not None:
            band = contract(bands[side], onehot, 1, 0).astype(BF)
            left = jnp.concatenate([queries[part], band, lse_rows], 0)
            right = jnp.concatenate([key_rows[part], onehot, key_extra], 0)
        else:
            left = jnp.concatenate([queries[part], lse_rows], 0)
            right = jnp.concatenate([key_rows[part], key_extra], 0)
        weights = jnp.exp(contract(left, right, 0, 0))
        d_weights = contract(
            jnp.concatenate([grad_out[part], delta_rows], 0),
            jnp.concatenate([values[part], value_extra], 0),
            0,
            0,
        )
        d_scores = (weights * d_weights).astype(BF)
        d_values.append(contract(grad_out[part], weights.astype(BF), 1, 0))
        d_keys.append(contract(queries[part], d_scores, 1, 0))
        scaled = key_rows[part] * scale
        if bias is not None:
            both = contract(jnp.concatenate([scaled, onehot], 0), d_scores, 1, 1)
            d_queries.append(both[:half])
            d_bands.append(contract(flipped, both[half:].astype(BF), 1, 1))
        else:
            d_queries.append(contract(scaled, d_scores, 1, 1))
    out = tuple(jnp.concatenate(each, 0).astype(BF).T for each in (d_queries, d_keys, d_values))
    return out if bias is None else (*out, jnp.stack(d_bands))


def backward_kernel(has_bias, scale, *refs):
    q_ref, k_ref, v_ref, do_ref, o_ref, lse_ref, mask_ref = refs[:7]
    bias = tuple(ref[...] for ref in refs[7:10]) if has_bias else None
    outs = refs[10:] if has_bias else refs[7:]
    grads = backward_pair(
        scale, q_ref[...], k_ref[...], v_ref[...], do_ref[...], o_ref[...], lse_ref[0], mask_ref[...], bias
    )
    outs[0][...] = grads[0]
    outs[1][0] = grads[1]
    outs[1][1] = grads[2]
    if has_bias:
        outs[2][...] = grads[3]


def column(first):
    return lambda i: (0, first + i)


def attend_forward(query_rows, key_value_rows, first, mask, bias, scale, us):
    count = query_rows.shape[0]
    pairs = key_value_rows.shape[1] // WIDE // (3 if first else 2)
    block = lambda start: pl.BlockSpec((count, WIDE), column(start))
    row = pl.BlockSpec((1, count), lambda i: (0, 0))
    wide = pl.BlockSpec((WIDE, count), lambda i: (0, 0))
    specs = [block(0), block(first), block(first + pairs), row]
    operands = [query_rows, key_value_rows, key_value_rows, mask]
    if bias is not None:
        specs += [pl.BlockSpec((2, WIDE, WIDE), lambda i: (i, 0, 0)), wide]
        operands += [bias[0], bias[1]]
    return pl.pallas_call(
        functools.partial(forward_kernel, bias is not None, scale),
        grid=(pairs,),
        in_specs=specs,
        out_specs=[block(0), pl.BlockSpec((1, 2, count), lambda i: (i, 0, 0))],
        out_shape=[
            jax.ShapeDtypeStruct((count, pairs * WIDE), BF),
            jax.ShapeDtypeStruct((pairs, 2, count), F32),
        ],
        compiler_params=params(),
        cost_estimate=cost(us),
    )(*operands)


def attend_backward(query_rows, key_value_rows, first, grad_out, output, lse, mask, bias, scale, us):
    count = query_rows.shape[0]
    pairs = lse.shape[0]
    block = lambda start: pl.BlockSpec((count, WIDE), column(start))
    row = pl.BlockSpec((1, count), lambda i: (0, 0))
    wide = pl.BlockSpec((WIDE, count), lambda i: (0, 0))
    band = pl.BlockSpec((2, WIDE, WIDE), lambda i: (i, 0, 0))
    specs = [
        block(0),
        block(first),
        block(first + pairs),
        block(0),
        block(0),
        pl.BlockSpec((1, 2, count), lambda i: (i, 0, 0)),
        row,
    ]
    operands = [query_rows, key_value_rows, key_value_rows, grad_out, output, lse, mask]
    out_specs = [block(0), pl.BlockSpec((2, count, WIDE), lambda i: (0, 0, i))]
    out_shape = [
        jax.ShapeDtypeStruct((count, pairs * WIDE), BF),
        jax.ShapeDtypeStruct((2, count, pairs * WIDE), BF),
    ]
    if bias is not None:
        specs += [band, wide, wide]
        operands += list(bias)
        out_specs.append(band)
        out_shape.append(jax.ShapeDtypeStruct((2 * pairs, WIDE, WIDE), F32))
    return pl.pallas_call(
        functools.partial(backward_kernel, bias is not None, scale),
        grid=(pairs,),
        in_specs=specs,
        out_specs=out_specs,
        out_shape=out_shape,
        compiler_params=params(),
        cost_estimate=cost(us),
    )(*operands)


def same_block(shape):
    rows = lax.broadcasted_iota(jnp.int32, shape, 0) // (WIDE // 2)
    columns = lax.broadcasted_iota(jnp.int32, shape, 1) // (WIDE // 2)
    return rows == columns


def band_kernel(table_ref, band_ref):
    heads = band_ref.shape[0]
    shape = (WIDE, WIDE)
    keep = same_block(shape)
    lower = lax.broadcasted_iota(jnp.int32, shape, 0) >= WIDE // 2
    for head in range(heads):
        across = jnp.broadcast_to(table_ref[head : head + 1, :], shape)
        down = jnp.broadcast_to(table_ref[heads + head : heads + head + 1, :], shape)
        rolled = pltpu.roll(jnp.where(lower, down, across), WIDE // 2, 1, stride=1, stride_axis=0)
        band_ref[head] = jnp.where(keep, rolled, 0.0).astype(BF)


def make_bands(table):
    heads = table.shape[1] // 2
    return pl.pallas_call(
        band_kernel,
        out_shape=jax.ShapeDtypeStruct((heads, WIDE, WIDE), BF),
        compiler_params=params(),
        cost_estimate=cost(3),
    )(table.T)


def unband_kernel(grad_ref, table_ref):
    heads = grad_ref.shape[0]
    half = WIDE // 2
    shape = (WIDE, WIDE)
    keep = same_block(shape)
    for head in range(heads):
        rolled = pltpu.roll(jnp.where(keep, grad_ref[head], 0.0), 0, 1, stride=1, stride_axis=0)
        table_ref[head : head + 1, :] = jnp.sum(rolled[:half], axis=0, keepdims=True)
        table_ref[heads + head : heads + head + 1, :] = jnp.sum(rolled[half:], axis=0, keepdims=True)


def gather_bands(grads):
    heads = grads.shape[0]
    flipped = pl.pallas_call(
        unband_kernel,
        out_shape=jax.ShapeDtypeStruct((2 * heads, WIDE), F32),
        compiler_params=params(),
        cost_estimate=cost(3),
    )(grads)
    return flipped[:, ::-1].T


def gelu_pair(value):
    distance = jnp.abs(value) * 0.7071067811865476
    bell = jnp.exp(-0.5 * value * value)
    t = 1.0 / (1.0 + 0.3275911 * distance)
    poly = t * (0.254829592 + t * (-0.284496736 + t * (1.421413741 + t * (-1.453152027 + t * 1.061405429))))
    tail = 0.5 * poly * bell
    phi = jnp.where(value >= 0, 1.0 - tail, tail)
    return value * phi, phi + value * bell * 0.3989422804014327


def feed_kernel(me_ref, second_ref, grad_ref, up_ref, down_ref, hidden_ref, d_up_ref, send_ref, keep_ref, sums_ref):
    tile = pl.program_id(0)
    grad = grad_ref[...]
    value = contract(second_ref[...], up_ref[...], 1, 0)
    hidden, slope = gelu_pair(value)
    hidden = hidden.astype(BF)
    hidden_ref[...] = hidden
    back = contract(grad, down_ref[...], 1, 1)
    d_up_ref[...] = (slope * back).astype(BF)
    sums_ref[...] = contract(hidden, grad, 0, 0)
    rows = send_ref.shape[1]
    per_tile = sums_ref.shape[0] // rows
    place_rows(me_ref[0], tile * per_tile, per_tile, rows, sums_ref, send_ref, keep_ref, 0)


def place_rows(me, first, number, rows, sums_ref, send_ref, keep_ref, offset):
    halves = send_ref.shape[0]
    quarters = halves // 2
    for local in range(number):
        relative = (first + local) ^ me
        slot = ((relative >> 1) & 1) * quarters + (relative >> 2)
        block = sums_ref[local * rows : local * rows + rows, :].astype(BF)

        @pl.when(relative & 1 == 1)
        def _():
            send_ref[slot, offset : offset + rows, :] = block

        @pl.when(relative & 1 == 0)
        def _():
            keep_ref[slot, offset : offset + rows, :] = block


def feed_forward(me, second, grad, w_up, w_down, parts):
    count, width = second.shape
    hidden_width = w_up.shape[1]
    rows = hidden_width // parts
    tiles = hidden_width // width
    whole = pl.BlockSpec((count, width), lambda i, me: (0, 0))
    tile = pl.BlockSpec((count, width), lambda i, me: (0, i))
    slots = pl.BlockSpec((parts // 2, rows, width), lambda i, me: (0, 0, 0))
    return pl.pallas_call(
        feed_kernel,
        grid_spec=pltpu.PrefetchScalarGridSpec(
            num_scalar_prefetch=1,
            grid=(tiles,),
            in_specs=[
                whole,
                whole,
                pl.BlockSpec((width, width), lambda i, me: (0, i)),
                pl.BlockSpec((width, width), lambda i, me: (i, 0)),
            ],
            out_specs=[tile, tile, slots, slots],
            scratch_shapes=[pltpu.VMEM((width, width), F32)],
        ),
        out_shape=[
            jax.ShapeDtypeStruct((count, hidden_width), BF),
            jax.ShapeDtypeStruct((count, hidden_width), BF),
            jax.ShapeDtypeStruct((parts // 2, rows, width), BF),
            jax.ShapeDtypeStruct((parts // 2, rows, width), BF),
        ],
        compiler_params=params(56),
        cost_estimate=cost(22),
    )(me, second, grad, w_up, w_down)


def outer_kernel(plan, rows, me_ref, *refs):
    tile = pl.program_id(0)
    lefts, rights = refs[: len(plan)], refs[len(plan) : 2 * len(plan)]
    send_ref, keep_ref, sums_ref = refs[2 * len(plan) :]
    number = 2 * send_ref.shape[0]
    first = 0
    for (tiles,), left_ref, right_ref in zip(plan, lefts, rights):
        for step in range(tiles):

            @pl.when(tile == first + step)
            def _(left_ref=left_ref, right_ref=right_ref, offset=(first + step) * rows):
                sums_ref[...] = contract(left_ref[...], right_ref[...], 0, 0)
                place_rows(me_ref[0], 0, number, rows, sums_ref, send_ref, keep_ref, offset)

        first += tiles


def outer_products(me, pairs, parts, us, extra=None):
    count, width = pairs[0][0].shape
    rows = width // parts
    plan, specs_left, specs_right = [], [], []
    first = 0
    for left, right in pairs:
        tiles = right.shape[1] // width
        plan.append((tiles,))
        specs_left.append(pl.BlockSpec((count, width), lambda i, me: (0, 0)))
        specs_right.append(
            pl.BlockSpec(
                (count, width),
                lambda i, me, first=first, tiles=tiles: (0, jnp.clip(i - first, 0, tiles - 1)),
            )
        )
        first += tiles
    slots = pl.BlockSpec((parts // 2, first * rows, width), lambda i, me: (0, 0, 0))
    shape = jax.ShapeDtypeStruct((parts // 2, first * rows, width), BF)
    return pl.pallas_call(
        functools.partial(outer_kernel, plan, rows),
        grid_spec=pltpu.PrefetchScalarGridSpec(
            num_scalar_prefetch=1,
            grid=(first,),
            in_specs=specs_left + specs_right,
            out_specs=[slots, slots],
            scratch_shapes=[pltpu.VMEM((width, width), F32)],
        ),
        out_shape=[shape, shape],
        compiler_params=params(56),
        cost_estimate=cost(us),
    )(me, *[left for left, _ in pairs], *[right for _, right in pairs])


def reduce_parts(send, keep):
    half = send.shape[0] // 2
    arrived = swapped(send, "page", 1).astype(F32)
    away = (arrived[half:] + keep[half:].astype(F32)).astype(BF)
    mine = arrived[:half] + keep[:half].astype(F32)
    mine = mine + swapped(away, "page", 2).astype(F32)
    total = mine[0]
    for step in range(1, half):
        total = total + swapped(mine[step].astype(BF), "page", 4 * step).astype(F32)
    return total


def flip(position, mask):
    out = position
    bit = 1
    while bit <= mask:
        if mask & bit:
            out = out + bit * (1 - 2 * lax.rem(lax.div(position, bit), 2))
        bit *= 2
    return out


LINK_US = 6.7
CORE_US = 2.6


class Flow:
    def __init__(self, refs, me, side):
        self.r = refs
        self.me = me
        self.side = side
        self.now = 0.0
        self.y_free = 0.0
        self.z_free = 0.0
        self.pending = []
        self.started = 0

    def at(self, mask):
        return {"page": flip(self.me, mask)}

    def core_copy(self, unit):
        r = self.r
        return pltpu.make_async_remote_copy(
            src_ref=r.ring.at[unit % 3],
            dst_ref=r.core_in.at[unit % 4],
            send_sem=r.core_sent.at[unit],
            recv_sem=r.core_got.at[unit],
            device_id=self.at(1),
            device_id_type=pl.DeviceIdType.MESH,
        )

    def y_copy(self, unit):
        r = self.r
        return pltpu.make_async_remote_copy(
            src_ref=r.keep.at[unit, pl.ds(4, 4)],
            dst_ref=r.y_in.at[unit],
            send_sem=r.y_sent.at[unit],
            recv_sem=r.y_got.at[unit],
            device_id=self.at(2),
            device_id_type=pl.DeviceIdType.MESH,
        )

    def z_copies(self, unit, arriving=False):
        r = self.r
        copies = []
        if unit in DOWN_UNITS:
            step = DOWN_UNITS.index(unit)
            if step:
                copies.append(
                    pltpu.make_async_remote_copy(
                        src_ref=r.keep.at[unit, pl.ds(0, 4)],
                        dst_ref=r.z_down.at[step - 1],
                        send_sem=r.z_sent.at[unit, 0],
                        recv_sem=r.z_got.at[unit, 0],
                        device_id=self.at(4 * step),
                        device_id_type=pl.DeviceIdType.MESH,
                    )
                )
        else:
            for step in range(1, 4):
                target = unit
                if unit in UP_UNITS and not arriving:
                    target = UP_UNITS[UP_UNITS.index(unit) ^ step]
                copies.append(
                    pltpu.make_async_remote_copy(
                        src_ref=r.keep.at[unit, step],
                        dst_ref=r.z_in.at[PLAIN_UNITS.index(target), step - 1],
                        send_sem=r.z_sent.at[unit, step - 1],
                        recv_sem=r.z_got.at[target, step - 1],
                        device_id=self.at(4 * step),
                        device_id_type=pl.DeviceIdType.MESH,
                    )
                )
        return copies

    def produce(self, unit, left, right):
        r = self.r
        r.sums[...] = contract(left, right, 0, 0).astype(BF)
        self.tick(1.2)
        if unit >= 3:
            self.core_copy(unit - 3).wait_send()
        core = lax.rem(self.me, 2)
        y = lax.rem(lax.div(self.me, 2), 2)
        z = lax.div(self.me, 4)
        for rel_y in range(2):
            for rel_z in range(4):
                y_at = flip(y, rel_y)
                if unit in DOWN_UNITS:
                    first = y_at * 8 * ROWS
                    mine = first + core * 4 * ROWS + rel_z * ROWS
                    other = first + (1 - core) * 4 * ROWS + rel_z * ROWS
                else:
                    first = flip(z, rel_z) * 4 * ROWS + y_at * 2 * ROWS
                    mine = first + core * ROWS
                    other = first + (1 - core) * ROWS
                slot = rel_y * 4 + rel_z
                r.ring[unit % 3, slot] = r.sums[pl.ds(pl.multiple_of(other, 16), ROWS), :]
                r.keep[unit, slot] = r.sums[pl.ds(pl.multiple_of(mine, 16), ROWS), :]
        if unit >= 4:
            pl.semaphore_wait(r.credit.at[unit - 4], 1)
        self.core_copy(unit).start()
        self.now += 0.5
        self.pending.append([unit, 0, self.now + CORE_US])

    def advance(self, entry):
        self.plan(entry)()

    def plan(self, entry):
        unit, stage, _ = entry
        if stage == 0:
            self.y_free = max(self.now, self.y_free) + LINK_US
            entry[1:] = [1, self.y_free + 0.3]
        elif stage == 1:
            self.z_free = max(self.now, self.z_free) + LINK_US
            entry[1:] = [2, self.z_free + 0.5]
            if unit in UP_UNITS:
                entry[2] = float("inf")
                ups = [e for e in self.pending if e[0] in UP_UNITS and e[1] == 2]
                if len(ups) == len(UP_UNITS):
                    for other in ups:
                        other[2] = self.z_free + 0.5
        else:
            entry[1] = 3
        return functools.partial(self.run, unit, stage)

    def run(self, unit, stage):
        r = self.r
        if stage == 0:
            self.core_copy(unit).wait_recv()
            for slot in (4, 5, 6, 7, 0, 1, 2, 3):
                total = r.keep[unit, slot].astype(F32) + r.core_in[unit % 4, slot].astype(F32)
                r.keep[unit, slot] = total.astype(BF)
                if slot == 7:
                    self.y_copy(unit).start()
            if unit < UNITS - 4:
                pl.semaphore_signal(
                    r.credit.at[unit], 1, device_id=self.at(1), device_id_type=pl.DeviceIdType.MESH
                )
        elif stage == 1:
            self.y_copy(unit).wait_recv()
            for slot in (1, 2, 3, 0):
                total = r.keep[unit, slot].astype(F32) + r.y_in[unit, slot].astype(F32)
                r.keep[unit, slot] = total.astype(BF)
            for copy in self.z_copies(unit):
                copy.start()
        else:
            for copy in self.z_copies(unit, arriving=True):
                copy.wait_recv()
            self.finish(unit)

    def due(self):
        while True:
            ready = [e for e in self.pending if e[2] <= self.now]
            if not ready:
                return
            entry = min(ready, key=lambda e: e[2])
            yield entry
            self.pending = [e for e in self.pending if e[1] < 3]

    def tick(self, us):
        self.now += us
        for entry in self.due():
            self.advance(entry)

    def drain(self):
        while self.pending:
            self.now = max(self.now, min(e[2] for e in self.pending))
            for entry in self.due():
                self.advance(entry)
        for unit in range(UNITS - 3, UNITS):
            self.core_copy(unit).wait_send()
        for unit in range(UNITS):
            self.y_copy(unit).wait_send()
            for copy in self.z_copies(unit):
                copy.wait_send()

    def finish(self, unit):
        r = self.r
        if unit in DOWN_UNITS:
            step = DOWN_UNITS.index(unit)
            total = r.keep[unit, 0:4].astype(F32) if step == 0 else r.z_down[step - 1].astype(F32)
            total = total.reshape(4 * ROWS, -1)
            if step == 0:
                r.down_out[...] = total
            else:
                r.down_out[...] += total
            return
        total = r.keep[unit, 0].astype(F32)
        for step in range(3):
            total = total + r.z_in[PLAIN_UNITS.index(unit), step].astype(F32)
        if unit in UP_UNITS:
            tile = flip(lax.div(self.me, 4), UP_UNITS.index(unit))
            r.up_out[:, pl.ds(pl.multiple_of(tile * WIDTH, WIDE), WIDTH)] = total
            return
        name, first = PLACES[unit]
        getattr(r, name)[:, first : first + total.shape[1]] = total


WIDTH = 768
ROWS = 48
DOWN_UNITS = (0, 2, 4, 6)
UP_UNITS = (1, 3, 5, 7)
PLAIN_UNITS = (1, 3, 5, 7, 8, 9, 10, 11, 12, 13, 14, 15)
UNITS = 16
PLACES = {
    8: ("cout_out", 0),
    9: ("cq_out", 0),
    10: ("out_out", 0),
    11: ("qkv_out", 0),
    12: ("qkv_out", WIDTH),
    13: ("qkv_out", 2 * WIDTH),
    14: ("ckv_out", 0),
    15: ("ckv_out", WIDTH),
}


class Refs:
    pass


INPUTS = (
    "second", "low_grad", "after_cross", "w_up", "w_down", "w_cout", "crossed", "cross_query", "partner",
    "low_middle", "attended", "w_cq", "w_out", "joined", "normed", "states", "w_qkv", "w_ckv",
)
SMALL_INPUTS = (
    "valid", "gain1", "gain2", "cross_lse", "mask_other", "self_lse", "mask_own", "bands", "onehot", "flipped",
)
OUTPUTS = (
    "result_out", "states_out",
)
KEPT_OUTPUTS = (
    "down_out", "up_out", "cout_out", "cq_out", "out_out", "qkv_out", "ckv_out", "small_out",
)
SCRATCH = (
    "s", "f", "w", "fetched", "stored", "sums", "keep", "ring", "core_in", "y_in", "z_in", "z_down",
    "core_sent", "core_got", "y_sent", "y_got", "z_sent", "z_got", "credit", "back_sent", "back_got",
    "small_in", "small_sent", "small_got", "d_bands",
)


def back_kernel(scale, *refs):
    r = Refs()
    for name, ref in zip(INPUTS + SMALL_INPUTS + OUTPUTS + KEPT_OUTPUTS + SCRATCH, refs, strict=True):
        setattr(r, name, ref)
    me = lax.axis_index("page")
    side = lax.axis_index("stream")
    flow = Flow(r, me, side)
    count, width = r.second.shape
    pairs = width // WIDE
    half_rows = count // 2
    z = lax.div(me, 4)

    copies = []

    def fetch(source, target):
        copy = pltpu.make_async_copy(source, target, r.fetched.at[len(copies)])
        copies.append(copy)
        copy.start()
        return copy

    def tile_of(step):
        return pl.ds(pl.multiple_of(flip(z, step) * width, WIDE), width)

    got_second = fetch(r.second, r.s.at[0])
    got_up = [fetch(r.w_up.at[:, tile_of(0)], r.w.at[0])]
    got_grad = fetch(r.low_grad, r.s.at[1])
    got_down = [fetch(r.w_down.at[tile_of(0)], r.w.at[1])]
    got_after = fetch(r.after_cross, r.f.at[2])
    got_up.append(fetch(r.w_up.at[:, tile_of(1)], r.w.at[2]))
    got_down.append(fetch(r.w_down.at[tile_of(1)], r.w.at[3]))
    got_cout = fetch(r.w_cout, r.w.at[4])
    got_crossed = fetch(r.crossed, r.s.at[2])
    got_query = fetch(r.cross_query, r.s.at[8])
    got_keys = fetch(r.partner.at[:, 0:width], r.s.at[9])
    got_values = fetch(r.partner.at[:, width : 2 * width], r.s.at[10])
    got_middle = fetch(r.low_middle, r.s.at[11])
    got_attended = fetch(r.attended, r.s.at[12])

    barrier = pltpu.get_barrier_semaphore()
    others = [{"page": flip(me, mask)} for mask in (1, 2, 4, 8, 12)] + [{"stream": 1 - side}]
    for other in others:
        pl.semaphore_signal(barrier, 1, device_id=other, device_id_type=pl.DeviceIdType.MESH)
    pl.semaphore_wait(barrier, len(others))

    hidden_at, d_up_at = 5, 6
    for step in range(4):
        up_at, down_at = (0, 1) if step % 2 == 0 else (2, 3)
        if step == 0:
            got_second.wait()
        got_up[step].wait()
        if step == 0:
            got_grad.wait()
        got_down[step].wait()
        if step == 0:
            got_after.wait()

        @pl.loop(0, 2)
        def _(part, step=step, up_at=up_at, down_at=down_at):
            rows = pl.ds(pl.multiple_of(part * half_rows, 16), half_rows)
            value = contract(r.s[0, rows, :], r.w[up_at], 1, 0)
            hidden, slope = gelu_pair(value)
            hidden = hidden.astype(BF)
            r.s[hidden_at, rows, :] = hidden
            back = contract(r.s[1, rows, :], r.w[down_at], 1, 1)
            d_up = (slope * back).astype(BF)
            r.s[d_up_at, rows, :] = d_up

        flow.tick(2.4)
        flow.produce(DOWN_UNITS[step], r.s[hidden_at], r.s[1])
        flow.tick(0.1)
        flow.produce(UP_UNITS[step], r.s[0], r.s[d_up_at])

        @pl.loop(0, 2)
        def _(part, step=step, up_at=up_at, down_at=down_at):
            rows = pl.ds(pl.multiple_of(part * half_rows, 16), half_rows)
            forward = contract(r.s[hidden_at, rows, :], r.w[down_at], 1, 0)
            back = contract(r.s[d_up_at, rows, :], r.w[up_at], 1, 1)
            if step == 0:
                r.f[1, rows, :] = r.f[2, rows, :] + forward
                r.f[0, rows, :] = back
            else:
                r.f[1, rows, :] += forward
                r.f[0, rows, :] += back

        if step < 2:
            got_up.append(fetch(r.w_up.at[:, tile_of(step + 2)], r.w.at[up_at]))
            got_down.append(fetch(r.w_down.at[tile_of(step + 2)], r.w.at[down_at]))
        flow.tick(2.2)
    got_w_cq = fetch(r.w_cq, r.w.at[0])
    got_w_out = fetch(r.w_out, r.w.at[1])

    r.s[7] = (r.f[1] * r.valid[...]).astype(BF)
    sent_result = pltpu.make_async_copy(r.s.at[7], r.result_out, r.stored.at[0])
    sent_result.start()
    gain2_grad = norm_back(r.f, 2, 0, 0, r.gain2, r.s, 1, r.s, 3)
    r.small_out[6:12, :] = fold(gain2_grad)
    flow.tick(1.5)
    got_cout.wait()
    r.s[4] = contract(r.s[3], r.w[4], 1, 1).astype(BF)
    flow.tick(1.2)
    got_crossed.wait()
    got_qkv = [fetch(r.joined.at[:, width * i : width * (i + 1)], r.s.at[at]) for i, at in enumerate((0, 1, 13))]
    got_w_q = [fetch(r.w_qkv.at[:, width * i : width * (i + 1)], r.w.at[at]) for i, at in enumerate((2, 3, 4))]
    flow.produce(8, r.s[2], r.s[3])
    flow.tick(0.1)

    got_query.wait()
    got_keys.wait()
    got_values.wait()
    sent_result.wait()

    def back_copy(pair):
        lanes = pl.ds(pl.multiple_of(pair * WIDE, WIDE), WIDE)
        return pltpu.make_async_remote_copy(
            src_ref=r.s.at[pl.ds(6, 2), :, lanes],
            dst_ref=r.s.at[pl.ds(15, 2), :, lanes],
            send_sem=r.back_sent.at[pair],
            recv_sem=r.back_got.at[pair],
            device_id={"stream": 1 - side},
            device_id_type=pl.DeviceIdType.MESH,
        )

    def pair_loop(us, step):
        events = []
        for pair in range(pairs):
            flow.now += us
            events.append([])
            for entry in flow.due():
                events[-1].append(flow.plan(entry))

        @pl.loop(0, pairs)
        def _(pair):
            step(pair)
            for place, steps in enumerate(events):
                if steps:

                    @pl.when(pair == place)
                    def _(steps=steps):
                        for run in steps:
                            run()

    def cross_step(pair):
        lanes = pl.ds(pl.multiple_of(pair * WIDE, WIDE), WIDE)
        d_query, d_key, d_value = backward_pair(
            scale,
            r.s[8, :, lanes],
            r.s[9, :, lanes],
            r.s[10, :, lanes],
            r.s[4, :, lanes],
            r.s[2, :, lanes],
            r.cross_lse[pair],
            r.mask_other[...],
            None,
        )
        r.s[5, :, lanes] = d_query
        r.s[6, :, lanes] = d_key
        r.s[7, :, lanes] = d_value
        back_copy(pair).start()

    pair_loop(2.6, cross_step)

    got_middle.wait()
    flow.produce(9, r.s[11], r.s[5])
    got_w_cq.wait()
    r.f[0] = r.f[0] + contract(r.s[5], r.w[0], 1, 1)
    r.s[3] = r.f[0].astype(BF)
    got_w_ck = fetch(r.w_ckv.at[:, 0:width], r.w.at[0])
    flow.tick(1.5)
    got_attended.wait()
    flow.produce(10, r.s[12], r.s[3])
    got_w_out.wait()
    r.s[4] = contract(r.s[3], r.w[1], 1, 1).astype(BF)
    got_w_cv = fetch(r.w_ckv.at[:, width : 2 * width], r.w.at[1])
    got_normed = fetch(r.normed, r.s.at[14])
    got_states = fetch(r.states, r.s.at[2])
    flow.tick(1.2)

    for copy in got_qkv:
        copy.wait()

    def self_step(pair):
        lanes = pl.ds(pl.multiple_of(pair * WIDE, WIDE), WIDE)
        d_query, d_key, d_value, d_bands = backward_pair(
            scale,
            r.s[0, :, lanes],
            r.s[1, :, lanes],
            r.s[13, :, lanes],
            r.s[4, :, lanes],
            r.s[12, :, lanes],
            r.self_lse[pair],
            r.mask_own[...],
            (r.bands[pair], r.onehot[...], r.flipped[...]),
        )
        r.s[8, :, lanes] = d_query
        r.s[9, :, lanes] = d_key
        r.s[10, :, lanes] = d_value
        r.d_bands[pair] = d_bands

    pair_loop(3.4, self_step)

    got_normed.wait()
    for unit, at in ((11, 8), (12, 9), (13, 10)):
        flow.produce(unit, r.s[14], r.s[at])
        flow.tick(0.1)
    for copy in got_w_q:
        copy.wait()
    r.f[1] = (
        contract(r.s[8], r.w[2], 1, 1) + contract(r.s[9], r.w[3], 1, 1) + contract(r.s[10], r.w[4], 1, 1)
    )
    flow.tick(3)
    for head in range(2 * pairs):
        across, down = unband(r.d_bands[head // 2, head % 2])
        r.small_out[16 + head : 17 + head, :] = across
        r.small_out[16 + 2 * pairs + head : 17 + 2 * pairs + head, :] = down
    flow.tick(1)

    @pl.loop(0, pairs)
    def _(pair):
        back_copy(pair).wait_send()
        back_copy(pair).wait_recv()

    for unit, at in ((14, 15), (15, 16)):
        flow.produce(unit, r.s[14], r.s[at])
        flow.tick(0.1)
    got_w_ck.wait()
    got_w_cv.wait()
    r.f[1] += contract(r.s[15], r.w[0], 1, 1) + contract(r.s[16], r.w[1], 1, 1)
    flow.tick(2)
    got_states.wait()

    @pl.loop(0, 2)
    def _(part):
        rows = pl.ds(pl.multiple_of(part * half_rows, 16), half_rows)
        r.f[2, rows, :] = r.s[2, rows, :].astype(F32)

    gain1_grad = norm_back(r.f, 2, 1, 0, r.gain1, None, None, None, None)
    sent_states = pltpu.make_async_copy(r.f.at[0], r.states_out, r.stored.at[1])
    sent_states.start()
    r.small_out[0:6, :] = fold(gain1_grad)
    r.small_out[12:16, :] = jnp.zeros((4, WIDE), F32)
    flow.tick(2)

    def small_copy(place, mask):
        return pltpu.make_async_remote_copy(
            src_ref=r.small_in.at[5 + SMALL_STAGE[place]],
            dst_ref=r.small_in.at[place],
            send_sem=r.small_sent.at[place],
            recv_sem=r.small_got.at[place],
            device_id={"page": flip(me, mask)},
            device_id_type=pl.DeviceIdType.MESH,
        )

    for stage, places in enumerate(((0,), (1,), (2, 3, 4))):
        r.small_in[5 + stage] = r.small_out[...]
        moves = [small_copy(place, (1, 2, 4, 8, 12)[place]) for place in places]
        for move in moves:
            move.start()
        flow.tick(1.5)
        for place, move in zip(places, moves):
            move.wait_recv()
            r.small_out[...] += r.small_in[place]
        for move in moves:
            move.wait_send()

    flow.drain()
    sent_states.wait()


SMALL_STAGE = (0, 1, 2, 2, 2)


def fold(row):
    return jnp.concatenate([row[:, WIDE * i : WIDE * (i + 1)] for i in range(row.shape[1] // WIDE)], 0)


def norm_back(f, inputs_at, grad_at, total_at, gain, s, s_grad_at, s_out, s_out_at):
    count = f.shape[1]
    chunk = count // 4
    gain_grad = jnp.zeros((1, f.shape[2]), F32)
    for part in range(4):
        rows = slice(part * chunk, (part + 1) * chunk)
        inputs = f[inputs_at, rows, :]
        grad = f[grad_at, rows, :]
        centre = inputs - jnp.mean(inputs, axis=-1, keepdims=True)
        spread = lax.rsqrt(jnp.mean(centre * centre, axis=-1, keepdims=True) + EPSILON)
        normed = centre * spread
        gain_grad = gain_grad + jnp.sum(grad * normed, axis=0, keepdims=True)
        scaled = grad * gain[...]
        back = spread * (
            scaled
            - jnp.mean(scaled, axis=-1, keepdims=True)
            - normed * jnp.mean(scaled * normed, axis=-1, keepdims=True)
        )
        if s is not None:
            total = s[s_grad_at, rows, :].astype(F32) + back
            s_out[s_out_at, rows, :] = total.astype(BF)
        else:
            total = f[total_at, rows, :] + back
        f[total_at, rows, :] = total
    return gain_grad


def unband(grad):
    half = WIDE // 2
    rolled = pltpu.roll(jnp.where(same_block((WIDE, WIDE)), grad, 0.0), 0, 1, stride=1, stride_axis=0)
    return jnp.sum(rolled[:half], axis=0, keepdims=True), jnp.sum(rolled[half:], axis=0, keepdims=True)


def backward_pass(operands, scale):
    count, width = operands["second"].shape
    hidden_width = operands["w_up"].shape[1]
    heads = operands["bands"].shape[0]
    pairs = heads // 2
    operands = dict(operands)
    operands["bands"] = operands["bands"].reshape(pairs, 2, WIDE, WIDE)
    rows = width // 16
    outs = [
        jax.ShapeDtypeStruct((count, width), BF),
        jax.ShapeDtypeStruct((count, width), F32),
        jax.ShapeDtypeStruct((hidden_width // 16, width), F32),
        jax.ShapeDtypeStruct((rows, hidden_width), F32),
        jax.ShapeDtypeStruct((rows, width), F32),
        jax.ShapeDtypeStruct((rows, width), F32),
        jax.ShapeDtypeStruct((rows, width), F32),
        jax.ShapeDtypeStruct((rows, 3 * width), F32),
        jax.ShapeDtypeStruct((rows, 2 * width), F32),
        jax.ShapeDtypeStruct((16 + 2 * heads, WIDE), F32),
    ]
    anywhere = pl.BlockSpec(memory_space=pl.ANY)
    inside = pl.BlockSpec(memory_space=pltpu.VMEM)
    dma = pltpu.SemaphoreType.DMA
    small = (16 + 2 * heads, WIDE)
    return pl.pallas_call(
        functools.partial(back_kernel, scale),
        in_specs=[anywhere] * len(INPUTS) + [inside] * len(SMALL_INPUTS),
        out_specs=[anywhere] * len(OUTPUTS) + [inside] * len(KEPT_OUTPUTS),
        out_shape=outs,
        scratch_shapes=[
            pltpu.VMEM((17, count, width), BF),
            pltpu.VMEM((3, count, width), F32),
            pltpu.VMEM((5, width, width), BF),
            dma((32,)),
            dma((2,)),
            pltpu.VMEM((width, width), BF),
            pltpu.VMEM((UNITS, 8, rows, width), BF),
            pltpu.VMEM((3, 8, rows, width), BF),
            pltpu.VMEM((4, 8, rows, width), BF),
            pltpu.VMEM((UNITS, 4, rows, width), BF),
            pltpu.VMEM((len(PLAIN_UNITS), 3, rows, width), BF),
            pltpu.VMEM((3, 4, rows, width), BF),
            dma((UNITS,)),
            dma((UNITS,)),
            dma((UNITS,)),
            dma((UNITS,)),
            dma((UNITS, 3)),
            dma((UNITS, 3)),
            pltpu.SemaphoreType.REGULAR((UNITS,)),
            dma((pairs,)),
            dma((pairs,)),
            pltpu.VMEM((8, *small), F32),
            dma((5,)),
            dma((5,)),
            pltpu.VMEM((pairs, 2, WIDE, WIDE), F32),
        ],
        compiler_params=pltpu.CompilerParams(
            collective_id=0, has_side_effects=True, vmem_limit_bytes=(64 << 20) - (256 << 10)
        ),
        cost_estimate=cost(150),
    )(*[operands[name] for name in INPUTS + SMALL_INPUTS])


def norm_rows(inputs, gain_row):
    centre = inputs - jnp.mean(inputs, axis=-1, keepdims=True)
    spread = jnp.mean(centre * centre, axis=-1, keepdims=True)
    return centre * lax.rsqrt(spread + EPSILON) * gain_row


def matmul(left, right):
    return contract(left, right, 1, 0)


def matmul_back(left, weight):
    return contract(left, weight, 1, 1)


def onehots(left, top, buckets):
    index = jnp.arange(buckets)[:, None]
    return jnp.concatenate([left[None, :] == index, top[None, :] == index], 0).astype(BF)


def body(
    states,
    counts,
    box_x,
    box_y,
    ln1_gain,
    ln2_gain,
    box_table,
    w_qkv,
    w_out,
    w_cq,
    w_ckv,
    w_cout,
    w_up,
    w_down,
    cotangent,
):
    slot_count, width = states.shape[2], states.shape[3]
    heads = box_table.shape[2] // 2
    buckets = box_table.shape[1] // 2
    scale = (width // heads) ** (-0.5)
    pairs = heads // 2
    parts = lax.axis_size("page")
    side = lax.axis_index("stream")
    me = lax.axis_index("page").astype(jnp.int32).reshape(1)
    own_count = jnp.take(counts[:, 0], side)
    other_count = jnp.take(counts[:, 0], 1 - side)
    slots = jnp.arange(slot_count)
    grid_side = jnp.where(own_count > GRID_SMALL * GRID_SMALL, GRID_LARGE, GRID_SMALL)
    left = jnp.where(side == 0, box_x[0], slots % grid_side)
    top = jnp.where(side == 0, box_y[0], slots // grid_side)
    onehot = onehots(left, top, buckets)
    flipped = onehots(buckets - 1 - left, buckets - 1 - top, buckets)
    mask_own = jnp.where(slots < own_count, 0.0, MASKED).astype(F32)[None]
    mask_other = jnp.where(slots < other_count, 0.0, MASKED).astype(F32)[None]
    valid = (slots < own_count).astype(F32)[:, None]
    bands = make_bands(box_table[0])
    weights = [w[0] for w in (w_qkv, w_out, w_cq, w_ckv, w_cout, w_up, w_down)]
    w_qkv, w_out, w_cq, w_ckv, w_cout, w_up, w_down = weights

    inputs = states[0, 0].astype(F32)
    normed, norm_pull = jax.vjp(norm_rows, inputs, ln1_gain[0])
    normed = normed.astype(BF)
    cross_kv = matmul(normed, w_ckv).astype(BF)
    partner = swapped(cross_kv, "stream", 1)
    joined = matmul(normed, w_qkv).astype(BF)
    attended, self_lse = attend_forward(joined, joined, pairs, mask_own, (bands, onehot), scale, 18)
    middle = inputs + matmul(attended, w_out)
    low_middle = middle.astype(BF)
    cross_query = matmul(low_middle, w_cq).astype(BF)
    crossed, cross_lse = attend_forward(cross_query, partner, 0, mask_other, None, scale, 16)
    after_cross = middle + matmul(crossed, w_cout)
    second, second_pull = jax.vjp(norm_rows, after_cross, ln2_gain[0])
    second = second.astype(BF)
    out_grad = cotangent[0, 0].astype(F32) * valid
    low_grad = out_grad.astype(BF)
    if parts == 16 and width == WIDTH and w_up.shape[1] == 4 * width:
        operands = dict(
            second=second,
            low_grad=low_grad,
            after_cross=after_cross,
            w_up=w_up,
            w_down=w_down,
            w_cout=w_cout,
            crossed=crossed,
            cross_query=cross_query,
            partner=partner,
            low_middle=low_middle,
            attended=attended,
            w_cq=w_cq,
            w_out=w_out,
            joined=joined,
            normed=normed,
            states=states[0, 0],
            w_qkv=w_qkv,
            w_ckv=w_ckv,
            valid=valid,
            gain1=ln1_gain,
            gain2=ln2_gain,
            cross_lse=cross_lse,
            mask_other=mask_other,
            self_lse=self_lse,
            mask_own=mask_own,
            bands=bands,
            onehot=onehot,
            flipped=flipped,
        )
        result, states_grad, down, up, cout, cq, out, qkv, ckv, small = backward_pass(operands, scale)
        rows = width // parts
        table_rows = 2 * buckets // parts
        gain_sums = small[:12].reshape(2, parts, rows)
        gain_sums = lax.dynamic_index_in_dim(gain_sums, me[0], 1, keepdims=True)
        table_sum = small[16:, ::-1].T.reshape(parts, table_rows, 2 * heads)
        table_sum = lax.dynamic_index_in_dim(table_sum, me[0], 0, keepdims=True)
        return (
            result[None, None],
            states_grad[None, None],
            gain_sums[0],
            gain_sums[1],
            table_sum,
            qkv[None],
            out[None],
            cq[None],
            ckv[None],
            cout[None],
            up[None],
            down[None],
        )
    hidden, d_up, *down_parts = feed_forward(me, second, low_grad, w_up, w_down, parts)
    down_sum = reduce_parts(*down_parts)
    up_sum = reduce_parts(*outer_products(me, [(second, d_up)], parts, 6))
    d_after, ln2_grad = second_pull(matmul_back(d_up, w_up))
    d_after = d_after + out_grad
    low_after = d_after.astype(BF)
    d_crossed = matmul_back(low_after, w_cout).astype(BF)
    d_cross_query, d_partner = attend_backward(
        cross_query, partner, 0, d_crossed, crossed, cross_lse, mask_other, None, scale, 26
    )
    returned = swapped(d_partner, "stream", 1)
    d_middle = d_after + matmul_back(d_cross_query, w_cq)
    low_d_middle = d_middle.astype(BF)
    d_attended = matmul_back(low_d_middle, w_out).astype(BF)
    mid_sum = reduce_parts(
        *outer_products(
            me, [(crossed, low_after), (low_middle, d_cross_query), (attended, low_d_middle)], parts, 6
        )
    )
    d_query, d_pair, d_bands = attend_backward(
        joined, joined, pairs, d_attended, attended, self_lse, mask_own, (bands, onehot, flipped), scale, 29
    )
    table_grad = gather_bands(d_bands)
    d_normed = (
        matmul_back(d_query, w_qkv[:, :width])
        + matmul_back(d_pair[0], w_qkv[:, width : 2 * width])
        + matmul_back(d_pair[1], w_qkv[:, 2 * width :])
        + matmul_back(returned[0], w_ckv[:, :width])
        + matmul_back(returned[1], w_ckv[:, width:])
    )
    d_inputs, ln1_grad = norm_pull(d_normed)
    states_grad = d_inputs + d_middle
    last_send, last_keep = outer_products(
        me,
        [
            (normed, d_query),
            (normed, d_pair[0]),
            (normed, d_pair[1]),
            (normed, returned[0]),
            (normed, returned[1]),
        ],
        parts,
        10,
    )
    last_sum = reduce_parts(last_send, last_keep)
    small = jnp.concatenate(
        [ln1_grad.reshape(parts, -1), ln2_grad.reshape(parts, -1), table_grad.reshape(parts, -1)], 1
    )
    small_sum = reduce_small(me[0], small)
    result = ((after_cross + matmul(hidden, w_down)) * valid).astype(BF)

    rows = width // parts
    table_rows = 2 * buckets // parts

    def wide(block):
        return block.reshape(-1, rows, width).transpose(1, 0, 2).reshape(1, rows, -1)

    return (
        result[None, None],
        states_grad[None, None],
        small_sum[None, :rows],
        small_sum[None, rows : 2 * rows],
        small_sum[2 * rows :].reshape(1, table_rows, 2 * heads),
        wide(last_sum[: 3 * rows]),
        wide(mid_sum[2 * rows :]),
        wide(mid_sum[rows : 2 * rows]),
        wide(last_sum[3 * rows :]),
        wide(mid_sum[:rows]),
        wide(up_sum),
        down_sum[None],
    )


def reduce_small(me, small):
    parts = small.shape[0]
    order = jnp.arange(parts) ^ me
    small = jnp.take(small, order, axis=0).reshape(parts // 4, 2, 2, -1)
    small = small[:, :, 0] + swapped(small[:, :, 1], "page", 1)
    small = small[:, 0] + swapped(small[:, 1], "page", 2)
    total = small[0]
    for step in range(1, parts // 4):
        total = total + swapped(small[step], "page", 4 * step)
    return total


def solution(mesh):
    placed = (
        P("stream", "page", None, None),
        P(None, "page"),
        P("page", None),
        P("page", None),
        P("stream", None),
        P("stream", None),
        P("stream", None, None),
        P("stream", None, None),
        P("stream", None, None),
        P("stream", None, None),
        P("stream", None, None),
        P("stream", None, None),
        P("stream", None, None),
        P("stream", None, None),
        P("stream", "page", None, None),
    )
    return jax.shard_map(
        body,
        mesh=mesh,
        in_specs=placed,
        out_specs=(
            P("stream", "page", None, None),
            P("stream", "page", None, None),
            P("stream", "page"),
            P("stream", "page"),
            P("stream", "page", None),
            P("stream", "page", None),
            P("stream", "page", None),
            P("stream", "page", None),
            P("stream", "page", None),
            P("stream", "page", None),
            P("stream", "page", None),
            P("stream", "page", None),
        ),
        check_vma=False,
    )
```

```python
import functools
from typing import Any, NamedTuple

import jax
import jax.numpy as jnp
from jax import lax
from jax.experimental import pallas as pl
from jax.experimental.pallas import tpu as pltpu
from jax.sharding import PartitionSpec as P

GRID_SMALL = 16
GRID_LARGE = 24
EPSILON = 1e-05
MASKED = -1000000000.0
PAGE = "page"
STREAM = "stream"
BF = jnp.bfloat16
F32 = jnp.float32
WIDE = 128


def contract(left, right, left_dim, right_dim):
    return lax.dot_general(
        left, right, (((left_dim,), (right_dim,)), ((), ())), preferred_element_type=F32
    )


def params(mib=48):
    return pltpu.CompilerParams(vmem_limit_bytes=mib << 20)


def cost(us):
    return pl.CostEstimate(flops=int(us * 1.1e9), bytes_accessed=1 << 20, transcendentals=0)


def swapped(shard, axis, mask):
    return lax.ppermute(shard, axis, [(i, i ^ mask) for i in range(lax.axis_size(axis))])


def pieces(row):
    high = row.astype(BF).astype(F32)
    rest = row - high
    middle = rest.astype(BF).astype(F32)
    return high, middle, rest - middle


def extra_rows(rows, count):
    index = lax.broadcasted_iota(jnp.int32, (16, count), 0)
    block = jnp.zeros((16, count), F32)
    for place, row in enumerate(rows):
        block = jnp.where(index == place, row, block)
    return block.astype(BF)


def forward_pair(scale, queries, key_rows, values, mask, bias):
    count = queries.shape[0]
    half = WIDE // 2
    queries = (queries * scale).T
    key_rows = key_rows.T
    values = values.T
    ones = jnp.ones((1, count), F32)
    query_extra = extra_rows([ones], count)
    key_extra = extra_rows([mask], count)
    outs, logs = [], []
    for side in range(2):
        part = slice(half * side, half * side + half)
        if bias is not None:
            bands, onehot = bias
            band = contract(bands[side], onehot, 1, 0).astype(BF)
            left = jnp.concatenate([key_rows[part], onehot, key_extra], 0)
            right = jnp.concatenate([queries[part], band, query_extra], 0)
        else:
            left = jnp.concatenate([key_rows[part], key_extra], 0)
            right = jnp.concatenate([queries[part], query_extra], 0)
        scores = contract(left, right, 0, 0)
        top = jnp.max(scores, axis=0, keepdims=True)
        weights = jnp.exp(scores - top).astype(BF)
        output = contract(jnp.concatenate([values[part], query_extra], 0), weights, 1, 0)
        total = output[half : half + 1]
        outs.append(output[:half] * (1.0 / total))
        logs.append(top + jnp.log(total))
    return jnp.concatenate(outs, 0).astype(BF).T, jnp.concatenate(logs, 0)


def forward_kernel(has_bias, scale, *refs):
    q_ref, k_ref, v_ref, mask_ref = refs[:4]
    bias = (refs[4][...], refs[5][...]) if has_bias else None
    o_ref, lse_ref = refs[-2:]
    o_ref[...], lse_ref[0] = forward_pair(scale, q_ref[...], k_ref[...], v_ref[...], mask_ref[...], bias)


def backward_pair(scale, queries, key_rows, values, grad_out, output, lse, mask, bias):
    if bias is not None:
        bands, onehot, flipped = bias
    count = queries.shape[0]
    half = WIDE // 2
    queries = (queries * scale).T
    key_rows = key_rows.T
    values = values.T
    grad_out = grad_out.T
    product = grad_out.astype(F32) * output.T.astype(F32)
    ones = jnp.ones((1, count), F32)
    key_extra = extra_rows([ones, ones, ones, mask], count)
    value_extra = extra_rows([ones, ones, ones], count)
    d_queries, d_keys, d_values, d_bands = [], [], [], []
    for side in range(2):
        part = slice(half * side, half * side + half)
        lse_rows = extra_rows([*pieces(-lse[side : side + 1, :]), ones], count)
        delta = jnp.sum(product[part], axis=0, keepdims=True)
        delta_rows = extra_rows(list(pieces(-delta)), count)
        if bias is not None:
            band = contract(bands[side], onehot, 1, 0).astype(BF)
            left = jnp.concatenate([queries[part], band, lse_rows], 0)
            right = jnp.concatenate([key_rows[part], onehot, key_extra], 0)
        else:
            left = jnp.concatenate([queries[part], lse_rows], 0)
            right = jnp.concatenate([key_rows[part], key_extra], 0)
        weights = jnp.exp(contract(left, right, 0, 0))
        d_weights = contract(
            jnp.concatenate([grad_out[part], delta_rows], 0),
            jnp.concatenate([values[part], value_extra], 0),
            0,
            0,
        )
        d_scores = (weights * d_weights).astype(BF)
        d_values.append(contract(grad_out[part], weights.astype(BF), 1, 0))
        d_keys.append(contract(queries[part], d_scores, 1, 0))
        scaled = key_rows[part] * scale
        if bias is not None:
            both = contract(jnp.concatenate([scaled, flipped], 0), d_scores, 1, 1)
            d_queries.append(both[:half])
            d_bands.append(contract(onehot, both[half:].astype(BF), 1, 1))
        else:
            d_queries.append(contract(scaled, d_scores, 1, 1))
    out = tuple(jnp.concatenate(each, 0).astype(BF).T for each in (d_queries, d_keys, d_values))
    return out if bias is None else (*out, jnp.stack(d_bands))


def backward_kernel(has_bias, scale, *refs):
    q_ref, k_ref, v_ref, do_ref, o_ref, lse_ref, mask_ref = refs[:7]
    bias = tuple(ref[...] for ref in refs[7:10]) if has_bias else None
    outs = refs[10:] if has_bias else refs[7:]
    grads = backward_pair(
        scale, q_ref[...], k_ref[...], v_ref[...], do_ref[...], o_ref[...], lse_ref[0], mask_ref[...], bias
    )
    outs[0][...] = grads[0]
    outs[1][0] = grads[1]
    outs[1][1] = grads[2]
    if has_bias:
        outs[2][...] = grads[3]


def column(first):
    return lambda i: (0, first + i)


def attend_forward(query_rows, key_value_rows, first, mask, bias, scale, us):
    count = query_rows.shape[0]
    pairs = key_value_rows.shape[1] // WIDE // (3 if first else 2)
    block = lambda start: pl.BlockSpec((count, WIDE), column(start))
    row = pl.BlockSpec((1, count), lambda i: (0, 0))
    wide = pl.BlockSpec((WIDE, count), lambda i: (0, 0))
    specs = [block(0), block(first), block(first + pairs), row]
    operands = [query_rows, key_value_rows, key_value_rows, mask]
    if bias is not None:
        specs += [pl.BlockSpec((2, WIDE, WIDE), lambda i: (i, 0, 0)), wide]
        operands += [bias[0], bias[1]]
    return pl.pallas_call(
        functools.partial(forward_kernel, bias is not None, scale),
        grid=(pairs,),
        in_specs=specs,
        out_specs=[block(0), pl.BlockSpec((1, 2, count), lambda i: (i, 0, 0))],
        out_shape=[
            jax.ShapeDtypeStruct((count, pairs * WIDE), BF),
            jax.ShapeDtypeStruct((pairs, 2, count), F32),
        ],
        compiler_params=params(),
        cost_estimate=cost(us),
    )(*operands)


def attend_backward(query_rows, key_value_rows, first, grad_out, output, lse, mask, bias, scale, us):
    count = query_rows.shape[0]
    pairs = lse.shape[0]
    block = lambda start: pl.BlockSpec((count, WIDE), column(start))
    row = pl.BlockSpec((1, count), lambda i: (0, 0))
    wide = pl.BlockSpec((WIDE, count), lambda i: (0, 0))
    band = pl.BlockSpec((2, WIDE, WIDE), lambda i: (i, 0, 0))
    specs = [
        block(0),
        block(first),
        block(first + pairs),
        block(0),
        block(0),
        pl.BlockSpec((1, 2, count), lambda i: (i, 0, 0)),
        row,
    ]
    operands = [query_rows, key_value_rows, key_value_rows, grad_out, output, lse, mask]
    out_specs = [block(0), pl.BlockSpec((2, count, WIDE), lambda i: (0, 0, i))]
    out_shape = [
        jax.ShapeDtypeStruct((count, pairs * WIDE), BF),
        jax.ShapeDtypeStruct((2, count, pairs * WIDE), BF),
    ]
    if bias is not None:
        specs += [band, wide, wide]
        operands += list(bias)
        out_specs.append(band)
        out_shape.append(jax.ShapeDtypeStruct((2 * pairs, WIDE, WIDE), F32))
    return pl.pallas_call(
        functools.partial(backward_kernel, bias is not None, scale),
        grid=(pairs,),
        in_specs=specs,
        out_specs=out_specs,
        out_shape=out_shape,
        compiler_params=params(),
        cost_estimate=cost(us),
    )(*operands)


def same_block(shape):
    rows = lax.broadcasted_iota(jnp.int32, shape, 0) // (WIDE // 2)
    columns = lax.broadcasted_iota(jnp.int32, shape, 1) // (WIDE // 2)
    return rows == columns


def band_kernel(table_ref, band_ref):
    heads = band_ref.shape[0]
    shape = (WIDE, WIDE)
    keep = same_block(shape)
    lower = lax.broadcasted_iota(jnp.int32, shape, 0) >= WIDE // 2
    for head in range(heads):
        across = jnp.broadcast_to(table_ref[head : head + 1, :], shape)
        down = jnp.broadcast_to(table_ref[heads + head : heads + head + 1, :], shape)
        rolled = pltpu.roll(jnp.where(lower, down, across), WIDE // 2, 1, stride=1, stride_axis=0)
        band_ref[head] = jnp.where(keep, rolled, 0.0).astype(BF)


def make_bands(table):
    heads = table.shape[1] // 2
    return pl.pallas_call(
        band_kernel,
        out_shape=jax.ShapeDtypeStruct((heads, WIDE, WIDE), BF),
        compiler_params=params(),
        cost_estimate=cost(3),
    )(table.T)


def unband_kernel(grad_ref, table_ref):
    heads = grad_ref.shape[0]
    half = WIDE // 2
    shape = (WIDE, WIDE)
    keep = same_block(shape)
    for head in range(heads):
        rolled = pltpu.roll(jnp.where(keep, grad_ref[head], 0.0), 1, 1, stride=1, stride_axis=0)
        table_ref[head : head + 1, :] = jnp.sum(rolled[:half], axis=0, keepdims=True)
        table_ref[heads + head : heads + head + 1, :] = jnp.sum(rolled[half:], axis=0, keepdims=True)


def gather_bands(grads):
    heads = grads.shape[0]
    table = pl.pallas_call(
        unband_kernel,
        out_shape=jax.ShapeDtypeStruct((2 * heads, WIDE), F32),
        compiler_params=params(),
        cost_estimate=cost(3),
    )(grads)
    return table.T


def gelu_pair(value):
    distance = jnp.abs(value) * 0.7071067811865476
    bell = jnp.exp(-0.5 * value * value)
    t = 1.0 / (1.0 + 0.3275911 * distance)
    poly = t * (0.254829592 + t * (-0.284496736 + t * (1.421413741 + t * (-1.453152027 + t * 1.061405429))))
    tail = 0.5 * poly * bell
    phi = jnp.where(value >= 0, 1.0 - tail, tail)
    return value * phi, phi + value * bell * 0.3989422804014327


def feed_kernel(me_ref, second_ref, grad_ref, up_ref, down_ref, hidden_ref, d_up_ref, send_ref, keep_ref, sums_ref):
    tile = pl.program_id(0)
    grad = grad_ref[...]
    value = contract(second_ref[...], up_ref[...], 1, 0)
    hidden, slope = gelu_pair(value)
    hidden = hidden.astype(BF)
    hidden_ref[...] = hidden
    back = contract(grad, down_ref[...], 1, 1)
    d_up_ref[...] = (slope * back).astype(BF)
    sums_ref[...] = contract(hidden, grad, 0, 0)
    rows = send_ref.shape[1]
    per_tile = sums_ref.shape[0] // rows
    place_rows(me_ref[0], tile * per_tile, per_tile, rows, sums_ref, send_ref, keep_ref, 0)


def place_rows(me, first, number, rows, sums_ref, send_ref, keep_ref, offset):
    halves = send_ref.shape[0]
    quarters = halves // 2
    for local in range(number):
        relative = (first + local) ^ me
        slot = ((relative >> 1) & 1) * quarters + (relative >> 2)
        block = sums_ref[local * rows : local * rows + rows, :].astype(BF)

        @pl.when(relative & 1 == 1)
        def _():
            send_ref[slot, offset : offset + rows, :] = block

        @pl.when(relative & 1 == 0)
        def _():
            keep_ref[slot, offset : offset + rows, :] = block


def feed_forward(me, second, grad, w_up, w_down, parts):
    count, width = second.shape
    hidden_width = w_up.shape[1]
    rows = hidden_width // parts
    tiles = hidden_width // width
    whole = pl.BlockSpec((count, width), lambda i, me: (0, 0))
    tile = pl.BlockSpec((count, width), lambda i, me: (0, i))
    slots = pl.BlockSpec((parts // 2, rows, width), lambda i, me: (0, 0, 0))
    return pl.pallas_call(
        feed_kernel,
        grid_spec=pltpu.PrefetchScalarGridSpec(
            num_scalar_prefetch=1,
            grid=(tiles,),
            in_specs=[
                whole,
                whole,
                pl.BlockSpec((width, width), lambda i, me: (0, i)),
                pl.BlockSpec((width, width), lambda i, me: (i, 0)),
            ],
            out_specs=[tile, tile, slots, slots],
            scratch_shapes=[pltpu.VMEM((width, width), F32)],
        ),
        out_shape=[
            jax.ShapeDtypeStruct((count, hidden_width), BF),
            jax.ShapeDtypeStruct((count, hidden_width), BF),
            jax.ShapeDtypeStruct((parts // 2, rows, width), BF),
            jax.ShapeDtypeStruct((parts // 2, rows, width), BF),
        ],
        compiler_params=params(56),
        cost_estimate=cost(22),
    )(me, second, grad, w_up, w_down)


def outer_kernel(plan, rows, me_ref, *refs):
    tile = pl.program_id(0)
    lefts, rights = refs[: len(plan)], refs[len(plan) : 2 * len(plan)]
    send_ref, keep_ref, sums_ref = refs[2 * len(plan) :]
    number = 2 * send_ref.shape[0]
    first = 0
    for (tiles,), left_ref, right_ref in zip(plan, lefts, rights):
        for step in range(tiles):

            @pl.when(tile == first + step)
            def _(left_ref=left_ref, right_ref=right_ref, offset=(first + step) * rows):
                sums_ref[...] = contract(left_ref[...], right_ref[...], 0, 0)
                place_rows(me_ref[0], 0, number, rows, sums_ref, send_ref, keep_ref, offset)

        first += tiles


def outer_products(me, pairs, parts, us, extra=None):
    count, width = pairs[0][0].shape
    rows = width // parts
    plan, specs_left, specs_right = [], [], []
    first = 0
    for left, right in pairs:
        tiles = right.shape[1] // width
        plan.append((tiles,))
        specs_left.append(pl.BlockSpec((count, width), lambda i, me: (0, 0)))
        specs_right.append(
            pl.BlockSpec(
                (count, width),
                lambda i, me, first=first, tiles=tiles: (0, jnp.clip(i - first, 0, tiles - 1)),
            )
        )
        first += tiles
    slots = pl.BlockSpec((parts // 2, first * rows, width), lambda i, me: (0, 0, 0))
    shape = jax.ShapeDtypeStruct((parts // 2, first * rows, width), BF)
    return pl.pallas_call(
        functools.partial(outer_kernel, plan, rows),
        grid_spec=pltpu.PrefetchScalarGridSpec(
            num_scalar_prefetch=1,
            grid=(first,),
            in_specs=specs_left + specs_right,
            out_specs=[slots, slots],
            scratch_shapes=[pltpu.VMEM((width, width), F32)],
        ),
        out_shape=[shape, shape],
        compiler_params=params(56),
        cost_estimate=cost(us),
    )(me, *[left for left, _ in pairs], *[right for _, right in pairs])


def reduce_parts(send, keep):
    half = send.shape[0] // 2
    arrived = swapped(send, PAGE, 1).astype(F32)
    away = (arrived[half:] + keep[half:].astype(F32)).astype(BF)
    mine = arrived[:half] + keep[:half].astype(F32)
    mine = mine + swapped(away, PAGE, 2).astype(F32)
    total = mine[0]
    for step in range(1, half):
        total = total + swapped(mine[step].astype(BF), PAGE, 4 * step).astype(F32)
    return total


def flip(position, mask):
    out = position
    bit = 1
    while bit <= mask:
        if mask & bit:
            out = out + bit * (1 - 2 * lax.rem(lax.div(position, bit), 2))
        bit *= 2
    return out


RING = 2
STORES = 8
FETCHES = 14
LANDINGS = 3
LINK_US = 6.7
CORE_US = 2.6
LATE_US = 30.0
LATENCY_US = 2.0


CORE, NEAR, FAR, JOIN, LAST, DONE, Y, Z = range(8)
KV = 98
WEIGHTS = (96, 97)


class Flow:
    def __init__(self, refs, me, side):
        self.r = refs
        self.me = me
        self.side = side
        self.now = 0.0
        self.y_free = 0.0
        self.z_free = 0.0
        self.pending = []
        self.near_done = {}
        self.stores = []

    def at(self, mask):
        return {PAGE: flip(self.me, mask)}

    def core_copy(self, unit):
        r = self.r
        return pltpu.make_async_remote_copy(
            src_ref=r.ring.at[unit % RING],
            dst_ref=r.core_in.at[unit % LANDINGS],
            send_sem=r.core_sent.at[unit % RING],
            recv_sem=r.core_got.at[unit % LANDINGS],
            device_id=self.at(1),
            device_id_type=pl.DeviceIdType.MESH,
        )

    def y_copy(self, unit):
        r = self.r
        source, landing = r.keep.at[unit, 1], r.y_in.at[Y_PLACES[unit]]
        if unit in TURNED_UNITS:
            source, landing = r.keep.at[unit, 1, 0], r.z_in.at[PLAIN_UNITS.index(unit), 2]
        return pltpu.make_async_remote_copy(
            src_ref=source,
            dst_ref=landing,
            send_sem=r.y_sent.at[0],
            recv_sem=r.y_got.at[Y_PLACES[unit]],
            device_id=self.at(2),
            device_id_type=pl.DeviceIdType.MESH,
        )

    def z_place(self, unit):
        if unit in PLAIN_UNITS:
            return PLAIN_UNITS.index(unit)
        return len(PLAIN_UNITS) + DOWN_STEPS[DOWN_UNITS.index(unit)] // 2

    def near_copy(self, unit, arriving=False):
        r = self.r
        if unit in DOWN_UNITS:
            step = DOWN_STEPS[DOWN_UNITS.index(unit)]
            if (step & 1 == 1) == arriving:
                return None
            target = unit if arriving else DOWN_UNITS[DOWN_STEPS.index(step ^ 1)]
            source, landing = r.keep.at[unit], r.near_down.at[step // 2]
        elif unit in TURNED_UNITS:
            target = unit
            source = r.keep.at[unit, :, pl.ds(2, 2)]
            landing = r.turned_in.at[TURNED_UNITS.index(unit)]
        else:
            target = unit
            if unit in UP_UNITS and not arriving:
                target = UP_UNITS[DOWN_STEPS.index(DOWN_STEPS[UP_UNITS.index(unit)] ^ 1)]
            source = r.keep.at[unit, 0, pl.ds(2, 2)]
            landing = r.z_in.at[PLAIN_UNITS.index(target), pl.ds(0, 2)]
        return pltpu.make_async_remote_copy(
            src_ref=source,
            dst_ref=landing,
            send_sem=r.near_sent.at[0],
            recv_sem=r.near_got.at[self.z_place(target)],
            device_id=self.at(4),
            device_id_type=pl.DeviceIdType.MESH,
        )

    def far_copy(self, unit, arriving=False):
        r = self.r
        if unit in DOWN_UNITS:
            step = DOWN_STEPS[DOWN_UNITS.index(unit)]
            if step != (0 if arriving else 2):
                return None
            target = DOWN_UNITS[DOWN_STEPS.index(0)]
            source, landing = r.keep.at[unit, 0], r.far_down
        elif unit in TURNED_UNITS:
            target = unit
            source, landing = r.keep.at[unit, :, 1], r.z_in.at[PLAIN_UNITS.index(unit), pl.ds(0, 2)]
        else:
            target = unit
            if unit in UP_UNITS and not arriving:
                target = UP_UNITS[DOWN_STEPS.index(DOWN_STEPS[UP_UNITS.index(unit)] ^ 2)]
            source, landing = r.keep.at[unit, 0, 1], r.z_in.at[PLAIN_UNITS.index(target), 2]
        return pltpu.make_async_remote_copy(
            src_ref=source,
            dst_ref=landing,
            send_sem=r.far_sent.at[0],
            recv_sem=r.far_got.at[self.z_place(target)],
            device_id=self.at(8),
            device_id_type=pl.DeviceIdType.MESH,
        )

    def produce(self, unit, left, *rights):
        r = self.r
        first = 0
        for right in rights:
            last = first + right.shape[1]
            r.sums[:, first:last] = contract(left, right, 0, 0).astype(BF)
            first = last
        self.tick(1.2)
        if unit >= RING:
            self.core_copy(unit - RING).wait_send()
        core = lax.rem(self.me, 2)
        y = lax.rem(lax.div(self.me, 2), 2)
        z = lax.div(self.me, 4)
        for rel_y in range(2):
            for rel_z in range(4):
                y_at = flip(y, rel_y)
                if unit in DOWN_UNITS:
                    first = y_at * 8 * ROWS
                    mine = first + core * 4 * ROWS + rel_z * ROWS
                    other = first + (1 - core) * 4 * ROWS + rel_z * ROWS
                else:
                    first = flip(z, rel_z) * 4 * ROWS + y_at * 2 * ROWS
                    mine = first + core * ROWS
                    other = first + (1 - core) * ROWS
                slot = rel_y * 4 + (rel_z if unit in DOWN_UNITS else SLOT_OF[rel_z])
                r.ring[unit % RING, rel_y, slot - 4 * rel_y] = r.sums[pl.ds(pl.multiple_of(other, 16), ROWS), :]
                r.keep[unit, rel_y, slot - 4 * rel_y] = r.sums[pl.ds(pl.multiple_of(mine, 16), ROWS), :]
        if unit >= LANDINGS:
            pl.semaphore_wait(r.credit.at[unit - LANDINGS], 1)
        self.core_copy(unit).start()
        self.now += 0.5
        self.pending.append([unit, CORE, self.now + CORE_US])

    def advance(self, entry):
        self.plan(entry)()

    def z_busy(self, us):
        self.z_free = max(self.now, self.z_free) + us
        return self.z_free + LATENCY_US

    def y_busy(self, us):
        self.y_free = max(self.now, self.y_free) + us
        return self.y_free + 0.3

    def plan(self, entry):
        unit, stage, _ = entry
        step = None
        if unit in WEIGHTS:
            if stage < 3:
                entry[1:] = [stage + 1, self.now + (3.8, 8.0, 2.5)[stage]]
            else:
                entry[1] = DONE
            return functools.partial(self.run, unit, stage)
        if unit in DOWN_UNITS:
            step = DOWN_STEPS[DOWN_UNITS.index(unit)]
        if unit == KV:
            entry[1] = DONE
        elif unit == SMALL:
            free = max(self.now, self.y_free if stage == CORE else self.z_free)
            following = {CORE: Y, Y: Z, Z: DONE}[stage]
            entry[1:] = [following, free + (2.0 if stage == CORE else 6.0)]
        elif unit in TURNED_UNITS and stage != DONE:
            if stage == CORE:
                entry[1:] = [NEAR, self.z_busy(LINK_US)]
            elif stage == NEAR:
                entry[1:] = [FAR, self.z_busy(LINK_US)]
            elif stage == FAR:
                entry[1:] = [LAST, self.y_busy(LINK_US / 4) + LATE_US]
            else:
                entry[1] = DONE
        elif stage == CORE:
            if step is not None and step & 1:
                self.near_done[step ^ 1] = self.z_busy(2 * LINK_US)
                entry[1] = DONE
            elif step is not None:
                entry[1:] = [JOIN, self.near_done[step]]
            else:
                entry[1:] = [Y, self.y_busy(LINK_US)]
        elif stage == JOIN:
            entry[1:] = [Y, self.y_busy(LINK_US)]
        elif stage == Y:
            if step is not None:
                done = self.z_busy(2 * LINK_US) if step == 2 else self.z_free + LATE_US
                entry[1:] = [DONE, 0.0] if step == 2 else [FAR, done + LATE_US]
            else:
                entry[1:] = [NEAR, self.z_busy(LINK_US / 2)]
                if unit in UP_UNITS:
                    self.meet(entry, [unit, UP_UNITS[DOWN_STEPS.index(DOWN_STEPS[UP_UNITS.index(unit)] ^ 1)]])
        elif stage == NEAR:
            entry[1:] = [FAR, self.z_busy(LINK_US / 2) + (8.0 if unit in KV_UNITS else LATE_US)]
            if unit in UP_UNITS:
                self.meet(entry, UP_UNITS)
        else:
            entry[1] = DONE
            if unit == KV_UNITS[1]:
                self.pending.append([KV, CORE, self.now + LATE_US])
        return functools.partial(self.run, unit, stage)

    def meet(self, entry, units):
        due, entry[2] = entry[2], float("inf")
        waiting = [e for e in self.pending if e[0] in units and e[1] == entry[1]]
        if len(waiting) == len(units):
            for other in waiting:
                other[2] = due

    def join(self, unit, half, places, arrived):
        r = self.r
        for place in places:
            total = r.keep[unit, half, place].astype(F32) + arrived[place].astype(F32)
            r.keep[unit, half, place] = total.astype(BF)

    def run(self, unit, stage):
        r = self.r
        if unit in WEIGHTS:
            self.weight_arrival(WEIGHTS.index(unit), stage).wait_recv()
            if stage < 3:
                self.weight_copy(WEIGHTS.index(unit), stage + 1).start()
            return
        if unit == KV:
            self.kv_copy().wait_recv()
            self.store(KV)
            return
        if unit == SMALL:
            self.run_small((CORE, Y, Z).index(stage))
            return
        step = None
        if unit in DOWN_UNITS:
            step = DOWN_STEPS[DOWN_UNITS.index(unit)]
        turned = unit in TURNED_UNITS
        if stage == CORE:
            self.core_copy(unit).wait_recv()
            arrived = r.core_in.at[unit % LANDINGS]
            self.join(unit, 1, (0, 1, 2, 3), arrived.at[1])
            if step is None and not turned:
                self.y_copy(unit).start()
            self.join(unit, 0, (0, 1, 2, 3), arrived.at[0])
            if turned or (step is not None and step & 1):
                self.near_copy(unit).start()
            if unit < UNITS - LANDINGS:
                pl.semaphore_signal(
                    r.credit.at[unit], 1, device_id=self.at(1), device_id_type=pl.DeviceIdType.MESH
                )
        elif stage == JOIN:
            self.near_copy(unit, arriving=True).wait_recv()
            arrived = r.near_down.at[step // 2]
            self.join(unit, 1, (0, 1, 2, 3), arrived.at[1])
            self.y_copy(unit).start()
            self.join(unit, 0, (0, 1, 2, 3), arrived.at[0])
        elif stage == Y:
            self.y_copy(unit).wait_recv()
            self.join(unit, 0, (2, 3, 0, 1), r.y_in.at[Y_PLACES[unit]])
            if step is None:
                self.near_copy(unit).start()
            elif step == 2:
                self.far_copy(unit).start()
        elif stage == NEAR:
            self.near_copy(unit, arriving=True).wait_recv()
            if turned:
                arrived = r.turned_in.at[TURNED_UNITS.index(unit)]
                for half in (0, 1):
                    self.join(unit, half, (1, 0), arrived.at[half])
            else:
                self.join(unit, 0, (1, 0), r.z_in.at[PLAIN_UNITS.index(unit)])
            self.far_copy(unit).start()
        elif turned and stage == FAR:
            self.far_copy(unit, arriving=True).wait_recv()
            arrived = r.z_in.at[PLAIN_UNITS.index(unit)]
            for half in (1, 0):
                total = r.keep[unit, half, 0].astype(F32) + arrived[half].astype(F32)
                r.keep[unit, half, 0] = total.astype(BF)
                if half:
                    self.y_copy(unit).start()
        elif turned:
            self.y_copy(unit).wait_recv()
            self.finish(unit)
        else:
            self.far_copy(unit, arriving=True).wait_recv()
            self.finish(unit)

    def small_copies(self, stage):
        r = self.r
        return [
            pltpu.make_async_remote_copy(
                src_ref=r.small_in.at[5 + stage],
                dst_ref=r.small_in.at[place],
                send_sem=r.small_sent.at[0],
                recv_sem=r.small_got.at[place],
                device_id=self.at(mask),
                device_id_type=pl.DeviceIdType.MESH,
            )
            for place, mask in SMALL_STEPS[stage]
        ]

    def kv_copy(self):
        r = self.r
        return pltpu.make_async_remote_copy(
            src_ref=r.kv_out,
            dst_ref=r.kv_in,
            send_sem=r.kv_sent.at[0],
            recv_sem=r.kv_got.at[0],
            device_id={STREAM: 1 - self.side},
            device_id_type=pl.DeviceIdType.MESH,
        )

    def weight_copy(self, half, stage):
        r = self.r
        core, y, z = lax.rem(self.me, 2), lax.rem(lax.div(self.me, 2), 2), lax.rem(lax.div(self.me, 4), 2)
        share = r.other_w.shape[-2]
        target, device = r.other_w.at[half, z, y, core], {STREAM: 1 - self.side}
        source = target
        if stage == 0:
            first = pl.multiple_of((z * 4 + y * 2 + core) * share, 16)
            source = r.w_ckv.at[pl.ds(first, share), half * WIDTH : (half + 1) * WIDTH]
        elif stage == 1:
            device = self.at(4)
        elif stage == 2:
            source = target = r.other_w.at[half, :, y, core]
            device = self.at(2)
        else:
            source = target = r.other_w.at[half, :, :, core]
            device = self.at(1)
        return pltpu.make_async_remote_copy(
            src_ref=source,
            dst_ref=target,
            send_sem=r.weight_sent.at[0],
            recv_sem=r.weight_got.at[half, stage],
            device_id=device,
            device_id_type=pl.DeviceIdType.MESH,
        )

    def weight_arrival(self, half, stage):
        r = self.r
        core, y, z = lax.rem(self.me, 2), lax.rem(lax.div(self.me, 2), 2), lax.rem(lax.div(self.me, 4), 2)
        target = (
            r.other_w.at[half, z, y, core],
            r.other_w.at[half, 1 - z, y, core],
            r.other_w.at[half, :, 1 - y, core],
            r.other_w.at[half, :, :, 1 - core],
        )[stage]
        return pltpu.make_async_remote_copy(
            src_ref=target,
            dst_ref=target,
            send_sem=r.weight_sent.at[0],
            recv_sem=r.weight_got.at[half, stage],
            device_id=self.at(1),
            device_id_type=pl.DeviceIdType.MESH,
        )

    def start_weights(self):
        for half in range(2):
            self.weight_copy(half, 0).start()
            self.pending.append([WEIGHTS[half], 0, self.now + 4.0 + 3.0 * half])

    def finish_weights(self):
        while True:
            left = [e for e in self.pending if e[0] in WEIGHTS]
            if not left:
                return
            entry = min(left, key=lambda e: e[2])
            self.now = max(self.now, entry[2])
            self.advance(entry)
            self.pending = [e for e in self.pending if e[1] != DONE]

    def start_small(self):
        r = self.r
        r.small_in[5] = r.small_sum[...]
        for copy in self.small_copies(0):
            copy.start()
        self.pending.append([SMALL, CORE, self.now + CORE_US + 1.0])

    def run_small(self, stage):
        r = self.r
        for copy in self.small_copies(stage):
            copy.wait_recv()
        for place, _ in SMALL_STEPS[stage]:
            r.small_sum[...] += r.small_in[place]
        if stage < 2:
            r.small_in[6 + stage] = r.small_sum[...]
            for copy in self.small_copies(stage + 1):
                copy.start()

    def due(self):
        while True:
            ready = [e for e in self.pending if e[2] <= self.now]
            if not ready:
                return
            entry = min(ready, key=lambda e: e[2])
            yield entry
            self.pending = [e for e in self.pending if e[1] != DONE]

    def tick(self, us):
        self.now += us
        for entry in self.due():
            self.advance(entry)

    def drain(self):
        while self.pending:
            self.now = max(self.now, min(e[2] for e in self.pending))
            for entry in self.due():
                self.advance(entry)
        for unit in range(UNITS - RING, UNITS):
            self.core_copy(unit).wait_send()
        r = self.r
        for whole, sent in (
            (r.y_in, r.y_sent),
            (r.keep.at[pl.ds(0, 5)], r.near_sent),
            (r.keep.at[pl.ds(0, 2)], r.far_sent),
            (r.small_in.at[pl.ds(0, 5)], r.small_sent),
            (r.other_w, r.weight_sent),
            (r.s.at[Slot.normed], r.normed_sent),
        ):
            pltpu.make_async_copy(whole, whole, sent.at[0]).wait()
        self.kv_copy().wait_send()
        for place in range(max(0, len(self.stores) - STORES), len(self.stores)):
            self.store_copy(place).wait()

    def store_copy(self, place):
        r = self.r
        unit, part = self.stores[place]
        if unit == KV:
            pairs = [(r.kv_in, r.ckv_out)]
        elif unit in DOWN_UNITS:
            pairs = [(r.done.at[pl.ds(0, 4)], r.down_out)]
        elif unit in UP_UNITS:
            tile = flip(lax.div(self.me, 4), DOWN_STEPS[UP_UNITS.index(unit)])
            columns = pl.ds(pl.multiple_of(tile * WIDTH, WIDE), WIDTH)
            pairs = [(r.done.at[self.done_at(unit)], r.up_out.at[:, columns])]
        elif unit in THIRD_UNITS:
            third = WIDTH // 3
            first = third * THIRD_UNITS.index(unit)
            source = r.done.at[self.done_at(unit)]
            pairs = [
                (source.at[:, pl.ds(i * third, third)], r.qkv_out.at[:, pl.ds(i * WIDTH + first, third)])
                for i in range(3)
            ]
        else:
            pairs = [(r.done.at[self.done_at(unit)], {8: r.cout_out, 11: r.cq_out, 12: r.out_out}[unit])]
        return pltpu.make_async_copy(*pairs[part], r.stored_sums.at[place % STORES])

    def done_at(self, unit):
        return 4 + PLAIN_UNITS.index(unit)

    def store(self, unit):
        for part in range(3 if unit in THIRD_UNITS else 1):
            place = len(self.stores)
            if place >= STORES:
                self.store_copy(place - STORES).wait()
            self.stores.append((unit, part))
            self.store_copy(place).start()

    def finish(self, unit):
        r = self.r
        if unit in DOWN_UNITS:
            r.done[0:4] = r.keep[unit, 0].astype(F32) + r.far_down[...].astype(F32)
            self.store(unit)
            return
        total = r.keep[unit, 0, 0].astype(F32) + r.z_in[PLAIN_UNITS.index(unit), 2].astype(F32)
        if unit in KV_UNITS:
            half = KV_UNITS.index(unit)
            r.kv_out[:, half * WIDTH : (half + 1) * WIDTH] = total
            if half:
                self.kv_copy().start()
            return
        r.done[self.done_at(unit)] = total
        self.store(unit)


WIDTH = 768
ROWS = 48
DOWN_UNITS = (1, 3, 5, 7)
TURNED_UNITS = ()
UP_UNITS = (0, 2, 4, 6)
DOWN_STEPS = (1, 3, 2, 0)
SLOT_OF = (0, 2, 1, 3)
PLAIN_UNITS = (0, 2, 4, 6, 8, 9, 10, 11, 12, 13, 14, 15)
UNITS = 16
Y_PLACES = {unit: at for at, unit in enumerate((0, 2, 4, 5, 6, 7, 8, 9, 10, 11, 12, 13, 14, 15))}
KV_UNITS = (9, 10)
THIRD_UNITS = (13, 14, 15)


class Fetch:
    def __init__(self, source, target, semaphores, free):
        self.free = free
        self.place = free.pop(0)
        self.copy = pltpu.make_async_copy(source, target, semaphores.at[self.place])
        self.copy.start()

    def wait(self):
        self.copy.wait()
        self.free.append(self.place)


class Refs(NamedTuple):
    states: Any
    cotangent: Any
    w_qkv: Any
    w_out: Any
    w_cq: Any
    w_ckv: Any
    w_cout: Any
    w_up: Any
    w_down: Any
    counts: Any
    box_x: Any
    box_y: Any
    gain1: Any
    gain2: Any
    table_in: Any
    result_out: Any
    states_out: Any
    held_out: Any
    down_out: Any
    up_out: Any
    cout_out: Any
    cq_out: Any
    out_out: Any
    qkv_out: Any
    ckv_out: Any
    gain1_out: Any
    gain2_out: Any
    table_out: Any
    s: Any
    f: Any
    w: Any
    fetched: Any
    stored: Any
    sums: Any
    keep: Any
    ring: Any
    core_in: Any
    y_in: Any
    z_in: Any
    near_down: Any
    far_down: Any
    turned_in: Any
    core_sent: Any
    core_got: Any
    y_sent: Any
    y_got: Any
    near_sent: Any
    near_got: Any
    far_sent: Any
    far_got: Any
    credit: Any
    normed_sent: Any
    normed_got: Any
    back_sent: Any
    back_got: Any
    weight_sent: Any
    weight_got: Any
    other_w: Any
    done: Any
    stored_sums: Any
    kv_out: Any
    kv_in: Any
    kv_sent: Any
    kv_got: Any
    self_lse: Any
    cross_lse: Any
    bands: Any
    onehot: Any
    flipped: Any
    small_sum: Any
    table: Any
    gain_sums: Any
    table_sum: Any
    small_in: Any
    small_sent: Any
    small_got: Any
    d_bands: Any


INPUTS, SMALL_INPUTS, OUTPUTS, KEPT_OUTPUTS = 9, 6, 13, 0


def layer_kernel(scale, *refs):
    r = Refs(*refs)
    me = lax.axis_index(PAGE)
    side = lax.axis_index(STREAM)
    flow = Flow(r, me, side)
    count, width = r.states.shape
    pairs = width // WIDE
    half_rows = count // 2
    core, y, z = lax.rem(me, 2), lax.rem(lax.div(me, 2), 2), lax.div(me, 4)
    partner = {STREAM: 1 - side}

    free = list(range(FETCHES))

    def fetch(source, target):
        return Fetch(source, target, r.fetched, free)

    def slot(name):
        return r.s.at[name]

    def tile_of(step):
        return pl.ds(pl.multiple_of(flip(z, DOWN_STEPS[step]) * width, WIDE), width)

    def columns(ref, first):
        return ref.at[:, width * first : width * (first + 1)]

    got_states = fetch(r.states, slot(Slot.second))
    got_q, got_k, got_v = [fetch(columns(r.w_qkv, i), r.w.at[i]) for i in range(3)]
    got_out = fetch(r.w_out, r.w.at[3])
    got_cq = fetch(r.w_cq, r.w.at[4])
    got_grad = fetch(r.cotangent, slot(Slot.low_grad))

    barrier = pltpu.get_barrier_semaphore()
    others = [{PAGE: flip(me, mask)} for mask in (1, 2, 4, 8, 12)] + [partner]
    for other in others:
        pl.semaphore_signal(barrier, 1, device_id=other, device_id_type=pl.DeviceIdType.MESH)

    own_count, other_count = r.counts[side], r.counts[1 - side]
    slots_row = lax.broadcasted_iota(jnp.int32, (1, count), 1)
    mask_own = jnp.where(slots_row < own_count, 0.0, MASKED).astype(F32)
    mask_other = jnp.where(slots_row < other_count, 0.0, MASKED).astype(F32)
    slots_column = lax.broadcasted_iota(jnp.int32, (count, 1), 0)
    valid = jnp.where(slots_column < own_count, 1.0, 0.0).astype(F32)
    buckets = WIDE // 2
    small = own_count <= GRID_SMALL * GRID_SMALL
    tall = [jnp.floor((slots_row.astype(F32) + 0.5) * (1.0 / grid)).astype(jnp.int32) for grid in (GRID_SMALL, GRID_LARGE)]
    grid_top = jnp.where(small, tall[0], tall[1])
    grid_left = slots_row - jnp.where(small, tall[0] * GRID_SMALL, tall[1] * GRID_LARGE)
    left = jnp.where(side == 0, r.box_x[...], grid_left)
    top = jnp.where(side == 0, r.box_y[...], grid_top)
    index = lax.broadcasted_iota(jnp.int32, (buckets, count), 0)

    def marks(first, second):
        both = [jnp.where(index == first, 1.0, 0.0), jnp.where(index == second, 1.0, 0.0)]
        return jnp.concatenate(both, 0).astype(BF)

    r.onehot[...] = marks(left, top)
    r.flipped[...] = marks(buckets - 1 - left, buckets - 1 - top)
    keep = same_block((WIDE, WIDE))
    lower = lax.broadcasted_iota(jnp.int32, (WIDE, WIDE), 0) >= buckets
    heads = 2 * pairs
    for head in range(heads):
        across = jnp.broadcast_to(r.table_in[head : head + 1, :], (WIDE, WIDE))
        down = jnp.broadcast_to(r.table_in[heads + head : heads + head + 1, :], (WIDE, WIDE))
        rolled = pltpu.roll(jnp.where(lower, down, across), buckets, 1, stride=1, stride_axis=0)
        r.bands[head // 2, head % 2] = jnp.where(keep, rolled, 0.0).astype(BF)

    def normed_copy(part):
        rows = pl.ds(part * half_rows, half_rows)
        return pltpu.make_async_remote_copy(
            src_ref=slot(Slot.normed).at[rows],
            dst_ref=slot(Slot.other).at[rows],
            send_sem=r.normed_sent.at[0],
            recv_sem=r.normed_got.at[part],
            device_id=partner,
            device_id_type=pl.DeviceIdType.MESH,
        )

    got_states.wait()
    for part in range(2):
        rows = slice(part * half_rows, (part + 1) * half_rows)
        inputs = r.s[Slot.second, rows, :].astype(F32)
        r.f[2, rows, :] = inputs
        r.s[Slot.normed, rows, :] = norm_rows(inputs, r.gain1[...]).astype(BF)
    pl.semaphore_wait(barrier, len(others))

    flow.start_weights()
    for part in range(2):
        normed_copy(part).start()
    flow.tick(0.1)
    for name, copy, at in ((Slot.query, got_q, 0), (Slot.key, got_k, 1), (Slot.value, got_v, 2)):
        copy.wait()
        slot(name)[...] = contract(slot(Slot.normed)[...], r.w[at], 1, 0).astype(BF)
        flow.tick(1.0)
    held = [pltpu.make_async_copy(slot(name), r.held_out.at[i], r.stored.at[2 + i]) for i, name in enumerate((Slot.query, Slot.key, Slot.value))]
    for copy in held:
        copy.start()
    got_cout = fetch(r.w_cout, r.w.at[0])
    got_down = [fetch(r.w_down.at[tile_of(step)], r.w.at[1 + step]) for step in range(2)]

    def pair_loop(us, step, first=0, last=pairs):
        events = []
        for pair in range(first, last):
            flow.now += us
            events.append([])
            for entry in flow.due():
                events[-1].append(flow.plan(entry))

        @pl.loop(first, last)
        def _(pair):
            step(pair)
            for place, steps in enumerate(events, first):
                if steps:

                    @pl.when(pair == place)
                    def _(steps=steps):
                        for run in steps:
                            run()

    def lanes_of(pair):
        return pl.ds(pl.multiple_of(pair * WIDE, WIDE), WIDE)

    def self_forward(pair):
        lanes = lanes_of(pair)
        output, lse = forward_pair(
            scale,
            r.s[Slot.query, :, lanes],
            r.s[Slot.key, :, lanes],
            r.s[Slot.value, :, lanes],
            mask_own,
            (r.bands[pair], r.onehot[...]),
        )
        r.s[Slot.attended, :, lanes] = output
        r.self_lse[pair] = lse

    pair_loop(1.95, self_forward)

    got_out.wait()
    r.f[2] = r.f[2] + contract(slot(Slot.attended)[...], r.w[3], 1, 0)
    slot(Slot.low_middle)[...] = r.f[2].astype(BF)
    got_down.append(fetch(r.w_down.at[tile_of(2)], r.w.at[3]))
    got_cq.wait()
    slot(Slot.cross_query)[...] = contract(slot(Slot.low_middle)[...], r.w[4], 1, 0).astype(BF)
    got_down.append(fetch(r.w_down.at[tile_of(3)], r.w.at[4]))
    flow.tick(2.2)
    got_grad.wait()
    slot(Slot.low_grad)[...] = (slot(Slot.low_grad)[...].astype(F32) * valid).astype(BF)
    flow.tick(0.5)

    back_slots = (Slot.back0, Slot.back1, Slot.back2, Slot.back3)
    hidden_slots = (Slot.query, Slot.key, Slot.value, Slot.hidden3)
    got_up = []
    for step in range(4):
        got_down[step].wait()
        r.s[back_slots[step]] = contract(slot(Slot.low_grad)[...], r.w[1 + step], 1, 1).astype(BF)
        got_up.append(fetch(r.w_up.at[:, tile_of(step)], r.w.at[1 + step]))
        flow.tick(1.05)
    flow.finish_weights()
    for copy in held:
        copy.wait()
    for part in range(2):
        normed_copy(part).wait_recv()
    flow.now = max(flow.now, 30.0)
    for at, name in enumerate((Slot.cross_key, Slot.cross_value)):
        slot(name)[...] = contract(slot(Slot.other)[...], r.other_w[at].reshape(width, width), 1, 0).astype(BF)
    flow.tick(2.0)

    def cross_forward(pair):
        lanes = lanes_of(pair)
        output, lse = forward_pair(
            scale,
            r.s[Slot.cross_query, :, lanes],
            r.s[Slot.cross_key, :, lanes],
            r.s[Slot.cross_value, :, lanes],
            mask_other,
            None,
        )
        r.s[Slot.crossed, :, lanes] = output
        r.cross_lse[pair] = lse

    pair_loop(1.8, cross_forward)
    got_cout.wait()
    r.f[2] = r.f[2] + contract(slot(Slot.crossed)[...], r.w[0], 1, 0)
    for part in range(2):
        rows = slice(part * half_rows, (part + 1) * half_rows)
        r.s[Slot.second, rows, :] = norm_rows(r.f[2, rows, :], r.gain2[...]).astype(BF)
    flow.tick(2.0)

    second_at, grad_at = Slot.second, Slot.low_grad
    for step in range(4):
        hidden_at, d_up_at, up_at = hidden_slots[step], back_slots[step], 1 + step
        got_up[step].wait()

        @pl.loop(0, 2)
        def _(part, hidden_at=hidden_at, d_up_at=d_up_at, up_at=up_at):
            rows = pl.ds(pl.multiple_of(part * half_rows, 16), half_rows)
            hidden, slope = gelu_pair(contract(r.s[second_at, rows, :], r.w[up_at], 1, 0))
            r.s[hidden_at, rows, :] = hidden.astype(BF)
            r.s[d_up_at, rows, :] = (slope * r.s[d_up_at, rows, :].astype(F32)).astype(BF)

        flow.tick(2.0)
        flow.produce(UP_UNITS[step], r.s[second_at], r.s[d_up_at])
        flow.tick(0.1)
        flow.produce(DOWN_UNITS[step], r.s[hidden_at], r.s[grad_at])
        flow.tick(0.1)
        back = contract(r.s[d_up_at], r.w[up_at], 1, 1)
        r.f[0] = back if step == 0 else r.f[0] + back
        flow.tick(1.2)
    got_cq, got_out = fetch(r.w_cq, r.w.at[1]), fetch(r.w_out, r.w.at[2])
    got_q, got_k = [fetch(columns(r.w_qkv, i), r.w.at[3 + i]) for i in range(2)]

    low_after_at, d_crossed_at = Slot.back0, Slot.second
    r.small_sum[6:12, :] = fold(norm_back(r.f.at[2], r.f, 0, r.gain2, r.s, grad_at, low_after_at))
    flow.tick(1.7)
    r.s[d_crossed_at] = contract(r.s[low_after_at], r.w[0], 1, 1).astype(BF)
    got_v = fetch(columns(r.w_qkv, 2), r.w.at[0])
    flow.tick(1.1)
    flow.produce(8, slot(Slot.crossed)[...], r.s[low_after_at])
    flow.tick(0.1)

    d_query_at, d_key_at, d_value_at = Slot.back1, Slot.low_grad, Slot.d_value

    def cross_backward(pair):
        lanes = lanes_of(pair)
        d_query, d_key, d_value = backward_pair(
            scale,
            r.s[Slot.cross_query, :, lanes],
            r.s[Slot.cross_key, :, lanes],
            r.s[Slot.cross_value, :, lanes],
            r.s[d_crossed_at, :, lanes],
            r.s[Slot.crossed, :, lanes],
            r.cross_lse[pair],
            mask_other,
            None,
        )
        r.s[d_query_at, :, lanes] = d_query
        r.s[d_key_at, :, lanes] = d_key
        r.s[d_value_at, :, lanes] = d_value

    pair_loop(2.45, cross_backward)

    flow.produce(9, slot(Slot.other)[...], r.s[d_key_at])
    flow.tick(0.1)
    flow.produce(10, slot(Slot.other)[...], r.s[d_value_at])
    back_at = Slot.crossed
    r.s[back_at] = (
        contract(r.s[d_key_at], r.other_w[0].reshape(width, width), 1, 1)
        + contract(r.s[d_value_at], r.other_w[1].reshape(width, width), 1, 1)
    ).astype(BF)
    back_copy = pltpu.make_async_remote_copy(
        src_ref=r.s.at[back_at],
        dst_ref=slot(Slot.returned),
        send_sem=r.back_sent.at[0],
        recv_sem=r.back_got.at[0],
        device_id=partner,
        device_id_type=pl.DeviceIdType.MESH,
    )
    back_copy.start()
    flow.tick(2.0)
    got_states = fetch(r.states, r.s.at[d_key_at])

    query_at, key_at, value_at = Slot.back3, Slot.back0, Slot.d_value
    got_held = [fetch(r.held_out.at[i], r.s.at[at]) for i, at in enumerate((query_at, key_at, value_at))]

    flow.produce(11, slot(Slot.low_middle)[...], r.s[d_query_at])
    got_cq.wait()
    r.f[0] = r.f[0] + contract(r.s[d_query_at], r.w[1], 1, 1)
    d_middle_at, d_attended_at = Slot.cross_key, Slot.cross_value
    r.s[d_middle_at] = r.f[0].astype(BF)
    flow.tick(1.5)
    flow.produce(12, slot(Slot.attended)[...], r.s[d_middle_at])
    got_out.wait()
    r.s[d_attended_at] = contract(r.s[d_middle_at], r.w[2], 1, 1).astype(BF)
    got_down = [fetch(r.w_down.at[tile_of(step)], r.w.at[1 + step]) for step in range(2)]
    flow.tick(1.2)

    dq_at, dk_at, dv_at = Slot.cross_query, Slot.back2, Slot.second
    for copy in got_held:
        copy.wait()

    def self_backward(pair):
        lanes = lanes_of(pair)
        d_query, d_key, d_value, d_bands = backward_pair(
            scale,
            r.s[query_at, :, lanes],
            r.s[key_at, :, lanes],
            r.s[value_at, :, lanes],
            r.s[d_attended_at, :, lanes],
            r.s[Slot.attended, :, lanes],
            r.self_lse[pair],
            mask_own,
            (r.bands[pair], r.onehot[...], r.flipped[...]),
        )
        r.s[dq_at, :, lanes] = d_query
        r.s[dk_at, :, lanes] = d_key
        r.s[dv_at, :, lanes] = d_value
        r.d_bands[pair] = d_bands

    third = width // 3
    normed_at = Slot.normed
    for part in range(3):
        pair_loop(3.2, self_backward, part * pairs // 3, (part + 1) * pairs // 3)
        wanted = slice(part * third, (part + 1) * third)
        flow.produce(13 + part, r.s[normed_at], r.s[dq_at, :, wanted], r.s[dk_at, :, wanted], r.s[dv_at, :, wanted])
    for copy in (got_q, got_k, got_v):
        copy.wait()
    r.f[1] = (
        contract(r.s[dq_at], r.w[3], 1, 1)
        + contract(r.s[dk_at], r.w[4], 1, 1)
        + contract(r.s[dv_at], r.w[0], 1, 1)
    )
    got_down += [fetch(r.w_down.at[tile_of(step)], r.w.at[1 + step]) for step in range(2, 4)]
    flow.tick(3.2)
    for head in range(heads):
        across, down = unband(r.d_bands[head // 2, head % 2])
        r.small_sum[16 + head : 17 + head, :] = across
        r.small_sum[16 + heads + head : 17 + heads + head, :] = down
    flow.tick(1.0)
    got_states.wait()
    back_copy.wait_recv()
    for part in range(2):
        rows = slice(part * half_rows, (part + 1) * half_rows)
        r.f[1, rows, :] += r.s[Slot.returned, rows, :].astype(F32)
    gain1_grad = norm_back(r.s.at[d_key_at], r.f, 1, r.gain1, None, None, None)
    sent_states = pltpu.make_async_copy(r.f.at[0], r.states_out, r.stored.at[1])
    sent_states.start()
    r.small_sum[0:6, :] = fold(gain1_grad)
    r.small_sum[12:16, :] = jnp.zeros((4, WIDE), F32)
    flow.tick(2.0)

    flow.start_small()
    flow.tick(0.2)

    result_at = Slot.back3
    for step in range(4):
        got_down[step].wait()
        r.f[2] = r.f[2] + contract(r.s[hidden_slots[step]], r.w[1 + step], 1, 0)
        flow.tick(1.3)
    r.s[result_at] = (r.f[2] * valid).astype(BF)
    sent_result = pltpu.make_async_copy(r.s.at[result_at], r.result_out, r.stored.at[0])
    sent_result.start()
    flow.tick(0.4)
    flow.drain()
    gains = r.small_sum[...]
    shift = width - me * ROWS
    for place in range(2):
        row = jnp.concatenate([gains[6 * place + i : 6 * place + i + 1] for i in range(width // WIDE)], 1)
        r.gain_sums[place] = pltpu.roll(row, lax.rem(shift, width), 1)[:, :ROWS]
    flat = jnp.concatenate([gains[16:], jnp.zeros((WIDE - 2 * heads, WIDE), F32)], 0)
    r.table[...] = flat.T
    table_rows = r.table_out.shape[0]
    r.table_sum[...] = r.table[pl.ds(pl.multiple_of(me * table_rows, 8), table_rows), 0 : 2 * heads]
    last = [
        pltpu.make_async_copy(source, target, r.stored.at[5 + i])
        for i, (source, target) in enumerate(
            ((r.gain_sums.at[0], r.gain1_out), (r.gain_sums.at[1], r.gain2_out), (r.table_sum, r.table_out))
        )
    ]
    for copy in last:
        copy.start()
    for copy in last:
        copy.wait()
    back_copy.wait_send()
    sent_result.wait()
    sent_states.wait()


class Slot:
    (
        normed,
        other,
        query,
        key,
        value,
        attended,
        low_middle,
        cross_query,
        cross_key,
        cross_value,
        crossed,
        second,
        low_grad,
        hidden3,
        back0,
        back1,
        back2,
        back3,
        d_value,
        returned,
    ) = range(20)


SMALL = 99
SMALL_STEPS = (((0, 1),), ((1, 2),), ((2, 4), (3, 8), (4, 12)))


def fold(row):
    return jnp.concatenate([row[:, WIDE * i : WIDE * (i + 1)] for i in range(row.shape[1] // WIDE)], 0)


def norm_back(source, f, grad_at, gain, s, s_grad_at, s_out_at):
    count = f.shape[1]
    chunk = count // 4
    gain_grad = jnp.zeros((1, f.shape[2]), F32)
    for part in range(4):
        rows = slice(part * chunk, (part + 1) * chunk)
        inputs = source[rows, :].astype(F32)
        grad = f[grad_at, rows, :]
        centre = inputs - jnp.mean(inputs, axis=-1, keepdims=True)
        spread = lax.rsqrt(jnp.mean(centre * centre, axis=-1, keepdims=True) + EPSILON)
        normed = centre * spread
        gain_grad = gain_grad + jnp.sum(grad * normed, axis=0, keepdims=True)
        scaled = grad * gain[...]
        back = spread * (
            scaled
            - jnp.mean(scaled, axis=-1, keepdims=True)
            - normed * jnp.mean(scaled * normed, axis=-1, keepdims=True)
        )
        if s is not None:
            total = s[s_grad_at, rows, :].astype(F32) + back
            s[s_out_at, rows, :] = total.astype(BF)
        else:
            total = f[0, rows, :] + back
        f[0, rows, :] = total
    return gain_grad


def unband(grad):
    half = WIDE // 2
    rolled = pltpu.roll(jnp.where(same_block((WIDE, WIDE)), grad, 0.0), 1, 1, stride=1, stride_axis=0)
    return jnp.sum(rolled[:half], axis=0, keepdims=True), jnp.sum(rolled[half:], axis=0, keepdims=True)


def deliver_kernel(*refs):
    number = (len(refs) - 2) // 3
    sources, targets, held = refs[:number], refs[number : 2 * number], refs[2 * number : 3 * number]
    came, went = refs[-2:]
    arrivals = [pltpu.make_async_copy(sources[i], held[i], came.at[i]) for i in range(number)]
    departures = [pltpu.make_async_copy(held[i], targets[i], went.at[i]) for i in range(number)]
    for copy in arrivals:
        copy.start()
    for arrival, departure in zip(arrivals, departures):
        arrival.wait()
        departure.start()
    for copy in departures:
        copy.wait()


def deliver(arrays):
    anywhere = pl.BlockSpec(memory_space=pl.ANY)
    return pl.pallas_call(
        deliver_kernel,
        in_specs=[anywhere] * len(arrays),
        out_specs=[anywhere] * len(arrays),
        out_shape=[jax.ShapeDtypeStruct(array.shape, array.dtype) for array in arrays],
        scratch_shapes=[pltpu.VMEM(array.shape, array.dtype) for array in arrays]
        + [pltpu.SemaphoreType.DMA((len(arrays),))] * 2,
        compiler_params=params(63),
        cost_estimate=cost(3),
    )(*arrays)


def whole_layer(operands, scale):
    count, width = operands[0].shape
    hidden_width = operands[7].shape[1]
    heads = operands[-1].shape[0] // 2
    pairs = heads // 2
    rows = width // 16
    outs = [
        jax.ShapeDtypeStruct((count, width), BF),
        jax.ShapeDtypeStruct((count, width), F32),
        jax.ShapeDtypeStruct((3, count, width), BF),
        jax.ShapeDtypeStruct((4, rows, width), F32),
        jax.ShapeDtypeStruct((rows, hidden_width), F32),
        jax.ShapeDtypeStruct((rows, width), F32),
        jax.ShapeDtypeStruct((rows, width), F32),
        jax.ShapeDtypeStruct((rows, width), F32),
        jax.ShapeDtypeStruct((rows, 3 * width), F32),
        jax.ShapeDtypeStruct((rows, 2 * width), F32),
        jax.ShapeDtypeStruct((1, rows), F32),
        jax.ShapeDtypeStruct((1, rows), F32),
        jax.ShapeDtypeStruct((WIDE // 16, 2 * heads), F32),
    ]
    anywhere = pl.BlockSpec(memory_space=pl.ANY)
    inside = pl.BlockSpec(memory_space=pltpu.VMEM)
    scalars = pl.BlockSpec(memory_space=pltpu.SMEM)
    dma = pltpu.SemaphoreType.DMA
    small = (16 + 2 * heads, WIDE)
    scratch = [
        pltpu.VMEM((20, count, width), BF),
        pltpu.VMEM((3, count, width), F32),
        pltpu.VMEM((5, width, width), BF),
        dma((FETCHES,)),
        dma((8,)),
        pltpu.VMEM((width, width), BF),
        pltpu.VMEM((UNITS, 2, 4, rows, width), BF),
        pltpu.VMEM((RING, 2, 4, rows, width), BF),
        pltpu.VMEM((LANDINGS, 2, 4, rows, width), BF),
        pltpu.VMEM((len(Y_PLACES), 4, rows, width), BF),
        pltpu.VMEM((len(PLAIN_UNITS), 3, rows, width), BF),
        pltpu.VMEM((2, 2, 4, rows, width), BF),
        pltpu.VMEM((4, rows, width), BF),
        pltpu.VMEM((max(1, len(TURNED_UNITS)), 2, 2, 16 if not TURNED_UNITS else rows, width), BF),
        dma((RING,)),
        dma((LANDINGS,)),
        dma((1,)),
        dma((len(Y_PLACES),)),
        dma((1,)),
        dma((len(PLAIN_UNITS) + 2,)),
        dma((1,)),
        dma((len(PLAIN_UNITS) + 1,)),
        pltpu.SemaphoreType.REGULAR((UNITS - LANDINGS,)),
        dma((1,)),
        dma((2,)),
        dma((1,)),
        dma((1,)),
        dma((1,)),
        dma((2, 4)),
        pltpu.VMEM((2, 2, 2, 2, width // 8, width), BF),
        pltpu.VMEM((4 + len(PLAIN_UNITS), rows, width), F32),
        dma((STORES,)),
        pltpu.VMEM((rows, 2 * width), F32),
        pltpu.VMEM((rows, 2 * width), F32),
        dma((1,)),
        dma((1,)),
        pltpu.VMEM((pairs, 2, count), F32),
        pltpu.VMEM((pairs, 2, count), F32),
        pltpu.VMEM((pairs, 2, WIDE, WIDE), BF),
        pltpu.VMEM((WIDE, count), BF),
        pltpu.VMEM((WIDE, count), BF),
        pltpu.VMEM(small, F32),
        pltpu.VMEM((WIDE, WIDE), F32),
        pltpu.VMEM((2, 1, rows), F32),
        pltpu.VMEM((WIDE // 16, 2 * heads), F32),
        pltpu.VMEM((8, *small), F32),
        dma((1,)),
        dma((5,)),
        pltpu.VMEM((pairs, 2, WIDE, WIDE), F32),
    ]
    outputs = pl.pallas_call(
        functools.partial(layer_kernel, scale),
        in_specs=[anywhere] * INPUTS + [scalars] + [inside] * (SMALL_INPUTS - 1),
        out_specs=[anywhere] * OUTPUTS + [inside] * KEPT_OUTPUTS,
        out_shape=outs,
        scratch_shapes=scratch,
        compiler_params=pltpu.CompilerParams(
            collective_id=0, has_side_effects=True, vmem_limit_bytes=(64 << 20) - (256 << 10)
        ),
        cost_estimate=cost(150),
    )(*operands)
    down = outputs[3].reshape(4 * rows, width)
    return [*outputs[:2], down, *outputs[4:]]


def norm_rows(inputs, gain_row):
    centre = inputs - jnp.mean(inputs, axis=-1, keepdims=True)
    spread = jnp.mean(centre * centre, axis=-1, keepdims=True)
    return centre * lax.rsqrt(spread + EPSILON) * gain_row


def matmul(left, right):
    return contract(left, right, 1, 0)


def matmul_back(left, weight):
    return contract(left, weight, 1, 1)


def onehots(left, top, buckets):
    index = jnp.arange(buckets)[:, None]
    return jnp.concatenate([left[None, :] == index, top[None, :] == index], 0).astype(BF)


def body(
    states,
    counts,
    box_x,
    box_y,
    ln1_gain,
    ln2_gain,
    box_table,
    w_qkv,
    w_out,
    w_cq,
    w_ckv,
    w_cout,
    w_up,
    w_down,
    cotangent,
):
    slot_count, width = states.shape[2], states.shape[3]
    heads = box_table.shape[2] // 2
    buckets = box_table.shape[1] // 2
    scale = (width // heads) ** (-0.5)
    pairs = heads // 2
    parts = lax.axis_size(PAGE)
    side = lax.axis_index(STREAM)
    me = lax.axis_index(PAGE).astype(jnp.int32).reshape(1)
    own_count = jnp.take(counts[:, 0], side)
    other_count = jnp.take(counts[:, 0], 1 - side)
    slots = jnp.arange(slot_count)
    grid_side = jnp.where(own_count > GRID_SMALL * GRID_SMALL, GRID_LARGE, GRID_SMALL)
    left = jnp.where(side == 0, box_x[0], slots % grid_side)
    top = jnp.where(side == 0, box_y[0], slots // grid_side)
    onehot = onehots(left, top, buckets)
    flipped = onehots(buckets - 1 - left, buckets - 1 - top, buckets)
    mask_own = jnp.where(slots < own_count, 0.0, MASKED).astype(F32)[None]
    mask_other = jnp.where(slots < other_count, 0.0, MASKED).astype(F32)[None]
    valid = (slots < own_count).astype(F32)[:, None]
    bands = make_bands(box_table[0])
    weights = [w[0] for w in (w_qkv, w_out, w_cq, w_ckv, w_cout, w_up, w_down)]
    w_qkv, w_out, w_cq, w_ckv, w_cout, w_up, w_down = weights

    if parts == 16 and width == WIDTH and w_up.shape[1] == 4 * width:
        operands = [
            states[0, 0],
            cotangent[0, 0],
            w_qkv,
            w_out,
            w_cq,
            w_ckv,
            w_cout,
            w_up,
            w_down,
            counts[:, 0],
            box_x,
            box_y,
            ln1_gain,
            ln2_gain,
            box_table[0].T,
        ]
        result, states_grad, down, up, cout, cq, out, qkv, ckv, gain1, gain2, table = deliver(
            whole_layer(operands, scale)
        )
        return (
            result[None, None],
            states_grad[None, None],
            gain1,
            gain2,
            table[None],
            qkv[None],
            out[None],
            cq[None],
            ckv[None],
            cout[None],
            up[None],
            down[None],
        )

    inputs = states[0, 0].astype(F32)
    normed, norm_pull = jax.vjp(norm_rows, inputs, ln1_gain[0])
    normed = normed.astype(BF)
    cross_kv = matmul(normed, w_ckv).astype(BF)
    partner = swapped(cross_kv, STREAM, 1)
    joined = matmul(normed, w_qkv).astype(BF)
    attended, self_lse = attend_forward(joined, joined, pairs, mask_own, (bands, onehot), scale, 18)
    middle = inputs + matmul(attended, w_out)
    low_middle = middle.astype(BF)
    cross_query = matmul(low_middle, w_cq).astype(BF)
    crossed, cross_lse = attend_forward(cross_query, partner, 0, mask_other, None, scale, 16)
    after_cross = middle + matmul(crossed, w_cout)
    second, second_pull = jax.vjp(norm_rows, after_cross, ln2_gain[0])
    second = second.astype(BF)
    out_grad = cotangent[0, 0].astype(F32) * valid
    low_grad = out_grad.astype(BF)
    hidden, d_up, *down_parts = feed_forward(me, second, low_grad, w_up, w_down, parts)
    down_sum = reduce_parts(*down_parts)
    up_sum = reduce_parts(*outer_products(me, [(second, d_up)], parts, 6))
    d_after, ln2_grad = second_pull(matmul_back(d_up, w_up))
    d_after = d_after + out_grad
    low_after = d_after.astype(BF)
    d_crossed = matmul_back(low_after, w_cout).astype(BF)
    d_cross_query, d_partner = attend_backward(
        cross_query, partner, 0, d_crossed, crossed, cross_lse, mask_other, None, scale, 26
    )
    returned = swapped(d_partner, STREAM, 1)
    d_middle = d_after + matmul_back(d_cross_query, w_cq)
    low_d_middle = d_middle.astype(BF)
    d_attended = matmul_back(low_d_middle, w_out).astype(BF)
    mid_sum = reduce_parts(
        *outer_products(
            me, [(crossed, low_after), (low_middle, d_cross_query), (attended, low_d_middle)], parts, 6
        )
    )
    d_query, d_pair, d_bands = attend_backward(
        joined, joined, pairs, d_attended, attended, self_lse, mask_own, (bands, onehot, flipped), scale, 29
    )
    table_grad = gather_bands(d_bands)
    d_normed = (
        matmul_back(d_query, w_qkv[:, :width])
        + matmul_back(d_pair[0], w_qkv[:, width : 2 * width])
        + matmul_back(d_pair[1], w_qkv[:, 2 * width :])
        + matmul_back(returned[0], w_ckv[:, :width])
        + matmul_back(returned[1], w_ckv[:, width:])
    )
    d_inputs, ln1_grad = norm_pull(d_normed)
    states_grad = d_inputs + d_middle
    last_send, last_keep = outer_products(
        me,
        [
            (normed, d_query),
            (normed, d_pair[0]),
            (normed, d_pair[1]),
            (normed, returned[0]),
            (normed, returned[1]),
        ],
        parts,
        10,
    )
    last_sum = reduce_parts(last_send, last_keep)
    small = jnp.concatenate(
        [ln1_grad.reshape(parts, -1), ln2_grad.reshape(parts, -1), table_grad.reshape(parts, -1)], 1
    )
    small_sum = reduce_small(me[0], small)
    result = ((after_cross + matmul(hidden, w_down)) * valid).astype(BF)

    rows = width // parts
    table_rows = 2 * buckets // parts

    def wide(block):
        return block.reshape(-1, rows, width).transpose(1, 0, 2).reshape(1, rows, -1)

    return (
        result[None, None],
        states_grad[None, None],
        small_sum[None, :rows],
        small_sum[None, rows : 2 * rows],
        small_sum[2 * rows :].reshape(1, table_rows, 2 * heads),
        wide(last_sum[: 3 * rows]),
        wide(mid_sum[2 * rows :]),
        wide(mid_sum[rows : 2 * rows]),
        wide(last_sum[3 * rows :]),
        wide(mid_sum[:rows]),
        wide(up_sum),
        down_sum[None],
    )


def reduce_small(me, small):
    parts = small.shape[0]
    order = jnp.arange(parts) ^ me
    small = jnp.take(small, order, axis=0).reshape(parts // 4, 2, 2, -1)
    small = small[:, :, 0] + swapped(small[:, :, 1], PAGE, 1)
    small = small[:, 0] + swapped(small[:, 1], PAGE, 2)
    total = small[0]
    for step in range(1, parts // 4):
        total = total + swapped(small[step], PAGE, 4 * step)
    return total


def solution(mesh):
    placed = (
        P(STREAM, PAGE, None, None),
        P(None, PAGE),
        P(PAGE, None),
        P(PAGE, None),
        P(STREAM, None),
        P(STREAM, None),
        P(STREAM, None, None),
        P(STREAM, None, None),
        P(STREAM, None, None),
        P(STREAM, None, None),
        P(STREAM, None, None),
        P(STREAM, None, None),
        P(STREAM, None, None),
        P(STREAM, None, None),
        P(STREAM, PAGE, None, None),
    )
    return jax.shard_map(
        body,
        mesh=mesh,
        in_specs=placed,
        out_specs=(
            P(STREAM, PAGE, None, None),
            P(STREAM, PAGE, None, None),
            P(STREAM, PAGE),
            P(STREAM, PAGE),
            P(STREAM, PAGE, None),
            P(STREAM, PAGE, None),
            P(STREAM, PAGE, None),
            P(STREAM, PAGE, None),
            P(STREAM, PAGE, None),
            P(STREAM, PAGE, None),
            P(STREAM, PAGE, None),
            P(STREAM, PAGE, None),
        ),
        check_vma=False,
    )
```

```python
import functools
from typing import Any, NamedTuple

import jax
import jax.numpy as jnp
from jax import lax
from jax.experimental import pallas as pl
from jax.experimental.pallas import tpu as pltpu
from jax.sharding import PartitionSpec as P

GRID_SMALL = 16
GRID_LARGE = 24
EPSILON = 1e-05
MASKED = -1000000000.0
PAGE = "page"
STREAM = "stream"
BF = jnp.bfloat16
F32 = jnp.float32
WIDE = 128


def contract(left, right, left_dim, right_dim):
    return lax.dot_general(
        left, right, (((left_dim,), (right_dim,)), ((), ())), preferred_element_type=F32
    )


def params(mib=48):
    return pltpu.CompilerParams(vmem_limit_bytes=mib << 20)


def cost(us):
    return pl.CostEstimate(flops=int(us * 1.1e9), bytes_accessed=1 << 20, transcendentals=0)


def swapped(shard, axis, mask):
    return lax.ppermute(shard, axis, [(i, i ^ mask) for i in range(lax.axis_size(axis))])


def pieces(row):
    high = row.astype(BF).astype(F32)
    rest = row - high
    middle = rest.astype(BF).astype(F32)
    return high, middle, rest - middle


def extra_rows(rows, count):
    index = lax.broadcasted_iota(jnp.int32, (16, count), 0)
    block = jnp.zeros((16, count), F32)
    for place, row in enumerate(rows):
        block = jnp.where(index == place, row, block)
    return block.astype(BF)


def forward_pair(scale, queries, key_rows, values, mask, bias):
    count = queries.shape[0]
    half = WIDE // 2
    queries = (queries * scale).T
    key_rows = key_rows.T
    values = values.T
    ones = jnp.ones((1, count), F32)
    query_extra = extra_rows([ones], count)
    key_extra = extra_rows([mask], count)
    outs, logs = [], []
    for side in range(2):
        part = slice(half * side, half * side + half)
        if bias is not None:
            bands, onehot = bias
            band = contract(bands[side], onehot, 1, 0).astype(BF)
            left = jnp.concatenate([key_rows[part], onehot, key_extra], 0)
            right = jnp.concatenate([queries[part], band, query_extra], 0)
        else:
            left = jnp.concatenate([key_rows[part], key_extra], 0)
            right = jnp.concatenate([queries[part], query_extra], 0)
        scores = contract(left, right, 0, 0)
        top = jnp.max(scores, axis=0, keepdims=True)
        weights = jnp.exp(scores - top).astype(BF)
        output = contract(jnp.concatenate([values[part], query_extra], 0), weights, 1, 0)
        total = output[half : half + 1]
        outs.append(output[:half] * (1.0 / total))
        logs.append(top + jnp.log(total))
    return jnp.concatenate(outs, 0).astype(BF).T, jnp.concatenate(logs, 0)


def forward_kernel(has_bias, scale, *refs):
    q_ref, k_ref, v_ref, mask_ref = refs[:4]
    bias = (refs[4][...], refs[5][...]) if has_bias else None
    o_ref, lse_ref = refs[-2:]
    o_ref[...], lse_ref[0] = forward_pair(scale, q_ref[...], k_ref[...], v_ref[...], mask_ref[...], bias)


def backward_pair(scale, queries, key_rows, values, grad_out, output, lse, mask, bias):
    if bias is not None:
        bands, onehot, flipped = bias
    count = queries.shape[0]
    half = WIDE // 2
    queries = (queries * scale).T
    key_rows = key_rows.T
    values = values.T
    grad_out = grad_out.T
    product = grad_out.astype(F32) * output.T.astype(F32)
    ones = jnp.ones((1, count), F32)
    key_extra = extra_rows([ones, ones, ones, mask], count)
    value_extra = extra_rows([ones, ones, ones], count)
    d_queries, d_keys, d_values, d_bands = [], [], [], []
    for side in range(2):
        part = slice(half * side, half * side + half)
        lse_rows = extra_rows([*pieces(-lse[side : side + 1, :]), ones], count)
        delta = jnp.sum(product[part], axis=0, keepdims=True)
        delta_rows = extra_rows(list(pieces(-delta)), count)
        if bias is not None:
            band = contract(bands[side], onehot, 1, 0).astype(BF)
            left = jnp.concatenate([queries[part], band, lse_rows], 0)
            right = jnp.concatenate([key_rows[part], onehot, key_extra], 0)
        else:
            left = jnp.concatenate([queries[part], lse_rows], 0)
            right = jnp.concatenate([key_rows[part], key_extra], 0)
        weights = jnp.exp(contract(left, right, 0, 0))
        d_weights = contract(
            jnp.concatenate([grad_out[part], delta_rows], 0),
            jnp.concatenate([values[part], value_extra], 0),
            0,
            0,
        )
        d_scores = (weights * d_weights).astype(BF)
        d_values.append(contract(grad_out[part], weights.astype(BF), 1, 0))
        d_keys.append(contract(queries[part], d_scores, 1, 0))
        scaled = key_rows[part] * scale
        if bias is not None:
            both = contract(jnp.concatenate([scaled, flipped], 0), d_scores, 1, 1)
            d_queries.append(both[:half])
            d_bands.append(contract(onehot, both[half:].astype(BF), 1, 1))
        else:
            d_queries.append(contract(scaled, d_scores, 1, 1))
    out = tuple(jnp.concatenate(each, 0).astype(BF).T for each in (d_queries, d_keys, d_values))
    return out if bias is None else (*out, jnp.stack(d_bands))


def backward_kernel(has_bias, scale, *refs):
    q_ref, k_ref, v_ref, do_ref, o_ref, lse_ref, mask_ref = refs[:7]
    bias = tuple(ref[...] for ref in refs[7:10]) if has_bias else None
    outs = refs[10:] if has_bias else refs[7:]
    grads = backward_pair(
        scale, q_ref[...], k_ref[...], v_ref[...], do_ref[...], o_ref[...], lse_ref[0], mask_ref[...], bias
    )
    outs[0][...] = grads[0]
    outs[1][0] = grads[1]
    outs[1][1] = grads[2]
    if has_bias:
        outs[2][...] = grads[3]


def column(first):
    return lambda i: (0, first + i)


def attend_forward(query_rows, key_value_rows, first, mask, bias, scale, us):
    count = query_rows.shape[0]
    pairs = key_value_rows.shape[1] // WIDE // (3 if first else 2)
    block = lambda start: pl.BlockSpec((count, WIDE), column(start))
    row = pl.BlockSpec((1, count), lambda i: (0, 0))
    wide = pl.BlockSpec((WIDE, count), lambda i: (0, 0))
    specs = [block(0), block(first), block(first + pairs), row]
    operands = [query_rows, key_value_rows, key_value_rows, mask]
    if bias is not None:
        specs += [pl.BlockSpec((2, WIDE, WIDE), lambda i: (i, 0, 0)), wide]
        operands += [bias[0], bias[1]]
    return pl.pallas_call(
        functools.partial(forward_kernel, bias is not None, scale),
        grid=(pairs,),
        in_specs=specs,
        out_specs=[block(0), pl.BlockSpec((1, 2, count), lambda i: (i, 0, 0))],
        out_shape=[
            jax.ShapeDtypeStruct((count, pairs * WIDE), BF),
            jax.ShapeDtypeStruct((pairs, 2, count), F32),
        ],
        compiler_params=params(),
        cost_estimate=cost(us),
    )(*operands)


def attend_backward(query_rows, key_value_rows, first, grad_out, output, lse, mask, bias, scale, us):
    count = query_rows.shape[0]
    pairs = lse.shape[0]
    block = lambda start: pl.BlockSpec((count, WIDE), column(start))
    row = pl.BlockSpec((1, count), lambda i: (0, 0))
    wide = pl.BlockSpec((WIDE, count), lambda i: (0, 0))
    band = pl.BlockSpec((2, WIDE, WIDE), lambda i: (i, 0, 0))
    specs = [
        block(0),
        block(first),
        block(first + pairs),
        block(0),
        block(0),
        pl.BlockSpec((1, 2, count), lambda i: (i, 0, 0)),
        row,
    ]
    operands = [query_rows, key_value_rows, key_value_rows, grad_out, output, lse, mask]
    out_specs = [block(0), pl.BlockSpec((2, count, WIDE), lambda i: (0, 0, i))]
    out_shape = [
        jax.ShapeDtypeStruct((count, pairs * WIDE), BF),
        jax.ShapeDtypeStruct((2, count, pairs * WIDE), BF),
    ]
    if bias is not None:
        specs += [band, wide, wide]
        operands += list(bias)
        out_specs.append(band)
        out_shape.append(jax.ShapeDtypeStruct((2 * pairs, WIDE, WIDE), F32))
    return pl.pallas_call(
        functools.partial(backward_kernel, bias is not None, scale),
        grid=(pairs,),
        in_specs=specs,
        out_specs=out_specs,
        out_shape=out_shape,
        compiler_params=params(),
        cost_estimate=cost(us),
    )(*operands)


def same_block(shape):
    rows = lax.broadcasted_iota(jnp.int32, shape, 0) // (WIDE // 2)
    columns = lax.broadcasted_iota(jnp.int32, shape, 1) // (WIDE // 2)
    return rows == columns


def band_kernel(table_ref, band_ref):
    heads = band_ref.shape[0]
    shape = (WIDE, WIDE)
    keep = same_block(shape)
    lower = lax.broadcasted_iota(jnp.int32, shape, 0) >= WIDE // 2
    for head in range(heads):
        across = jnp.broadcast_to(table_ref[head : head + 1, :], shape)
        down = jnp.broadcast_to(table_ref[heads + head : heads + head + 1, :], shape)
        rolled = pltpu.roll(jnp.where(lower, down, across), WIDE // 2, 1, stride=1, stride_axis=0)
        band_ref[head] = jnp.where(keep, rolled, 0.0).astype(BF)


def make_bands(table):
    heads = table.shape[1] // 2
    return pl.pallas_call(
        band_kernel,
        out_shape=jax.ShapeDtypeStruct((heads, WIDE, WIDE), BF),
        compiler_params=params(),
        cost_estimate=cost(3),
    )(table.T)


def unband_kernel(grad_ref, table_ref):
    heads = grad_ref.shape[0]
    half = WIDE // 2
    shape = (WIDE, WIDE)
    keep = same_block(shape)
    for head in range(heads):
        rolled = pltpu.roll(jnp.where(keep, grad_ref[head], 0.0), 1, 1, stride=1, stride_axis=0)
        table_ref[head : head + 1, :] = jnp.sum(rolled[:half], axis=0, keepdims=True)
        table_ref[heads + head : heads + head + 1, :] = jnp.sum(rolled[half:], axis=0, keepdims=True)


def gather_bands(grads):
    heads = grads.shape[0]
    table = pl.pallas_call(
        unband_kernel,
        out_shape=jax.ShapeDtypeStruct((2 * heads, WIDE), F32),
        compiler_params=params(),
        cost_estimate=cost(3),
    )(grads)
    return table.T


def gelu_pair(value):
    distance = jnp.abs(value) * 0.7071067811865476
    bell = jnp.exp(-0.5 * value * value)
    t = 1.0 / (1.0 + 0.3275911 * distance)
    poly = t * (0.254829592 + t * (-0.284496736 + t * (1.421413741 + t * (-1.453152027 + t * 1.061405429))))
    tail = 0.5 * poly * bell
    phi = jnp.where(value >= 0, 1.0 - tail, tail)
    return value * phi, phi + value * bell * 0.3989422804014327


def feed_kernel(me_ref, second_ref, grad_ref, up_ref, down_ref, hidden_ref, d_up_ref, send_ref, keep_ref, sums_ref):
    tile = pl.program_id(0)
    grad = grad_ref[...]
    value = contract(second_ref[...], up_ref[...], 1, 0)
    hidden, slope = gelu_pair(value)
    hidden = hidden.astype(BF)
    hidden_ref[...] = hidden
    back = contract(grad, down_ref[...], 1, 1)
    d_up_ref[...] = (slope * back).astype(BF)
    sums_ref[...] = contract(hidden, grad, 0, 0)
    rows = send_ref.shape[1]
    per_tile = sums_ref.shape[0] // rows
    place_rows(me_ref[0], tile * per_tile, per_tile, rows, sums_ref, send_ref, keep_ref, 0)


def place_rows(me, first, number, rows, sums_ref, send_ref, keep_ref, offset):
    halves = send_ref.shape[0]
    quarters = halves // 2
    for local in range(number):
        relative = (first + local) ^ me
        slot = ((relative >> 1) & 1) * quarters + (relative >> 2)
        block = sums_ref[local * rows : local * rows + rows, :].astype(BF)

        @pl.when(relative & 1 == 1)
        def _():
            send_ref[slot, offset : offset + rows, :] = block

        @pl.when(relative & 1 == 0)
        def _():
            keep_ref[slot, offset : offset + rows, :] = block


def feed_forward(me, second, grad, w_up, w_down, parts):
    count, width = second.shape
    hidden_width = w_up.shape[1]
    rows = hidden_width // parts
    tiles = hidden_width // width
    whole = pl.BlockSpec((count, width), lambda i, me: (0, 0))
    tile = pl.BlockSpec((count, width), lambda i, me: (0, i))
    slots = pl.BlockSpec((parts // 2, rows, width), lambda i, me: (0, 0, 0))
    return pl.pallas_call(
        feed_kernel,
        grid_spec=pltpu.PrefetchScalarGridSpec(
            num_scalar_prefetch=1,
            grid=(tiles,),
            in_specs=[
                whole,
                whole,
                pl.BlockSpec((width, width), lambda i, me: (0, i)),
                pl.BlockSpec((width, width), lambda i, me: (i, 0)),
            ],
            out_specs=[tile, tile, slots, slots],
            scratch_shapes=[pltpu.VMEM((width, width), F32)],
        ),
        out_shape=[
            jax.ShapeDtypeStruct((count, hidden_width), BF),
            jax.ShapeDtypeStruct((count, hidden_width), BF),
            jax.ShapeDtypeStruct((parts // 2, rows, width), BF),
            jax.ShapeDtypeStruct((parts // 2, rows, width), BF),
        ],
        compiler_params=params(56),
        cost_estimate=cost(22),
    )(me, second, grad, w_up, w_down)


def outer_kernel(plan, rows, me_ref, *refs):
    tile = pl.program_id(0)
    lefts, rights = refs[: len(plan)], refs[len(plan) : 2 * len(plan)]
    send_ref, keep_ref, sums_ref = refs[2 * len(plan) :]
    number = 2 * send_ref.shape[0]
    first = 0
    for (tiles,), left_ref, right_ref in zip(plan, lefts, rights):
        for step in range(tiles):

            @pl.when(tile == first + step)
            def _(left_ref=left_ref, right_ref=right_ref, offset=(first + step) * rows):
                sums_ref[...] = contract(left_ref[...], right_ref[...], 0, 0)
                place_rows(me_ref[0], 0, number, rows, sums_ref, send_ref, keep_ref, offset)

        first += tiles


def outer_products(me, pairs, parts, us, extra=None):
    count, width = pairs[0][0].shape
    rows = width // parts
    plan, specs_left, specs_right = [], [], []
    first = 0
    for left, right in pairs:
        tiles = right.shape[1] // width
        plan.append((tiles,))
        specs_left.append(pl.BlockSpec((count, width), lambda i, me: (0, 0)))
        specs_right.append(
            pl.BlockSpec(
                (count, width),
                lambda i, me, first=first, tiles=tiles: (0, jnp.clip(i - first, 0, tiles - 1)),
            )
        )
        first += tiles
    slots = pl.BlockSpec((parts // 2, first * rows, width), lambda i, me: (0, 0, 0))
    shape = jax.ShapeDtypeStruct((parts // 2, first * rows, width), BF)
    return pl.pallas_call(
        functools.partial(outer_kernel, plan, rows),
        grid_spec=pltpu.PrefetchScalarGridSpec(
            num_scalar_prefetch=1,
            grid=(first,),
            in_specs=specs_left + specs_right,
            out_specs=[slots, slots],
            scratch_shapes=[pltpu.VMEM((width, width), F32)],
        ),
        out_shape=[shape, shape],
        compiler_params=params(56),
        cost_estimate=cost(us),
    )(me, *[left for left, _ in pairs], *[right for _, right in pairs])


def reduce_parts(send, keep):
    half = send.shape[0] // 2
    arrived = swapped(send, PAGE, 1).astype(F32)
    away = (arrived[half:] + keep[half:].astype(F32)).astype(BF)
    mine = arrived[:half] + keep[:half].astype(F32)
    mine = mine + swapped(away, PAGE, 2).astype(F32)
    total = mine[0]
    for step in range(1, half):
        total = total + swapped(mine[step].astype(BF), PAGE, 4 * step).astype(F32)
    return total


def flip(position, mask):
    out = position
    bit = 1
    while bit <= mask:
        if mask & bit:
            out = out + bit * (1 - 2 * lax.rem(lax.div(position, bit), 2))
        bit *= 2
    return out


RING = 2
STORES = 8
FETCHES = 14
LANDINGS = 3
LINK_US = 6.6
CORE_US = 1.7
LATE_US = 30.0
LATENCY_US = 4.5


CORE, NEAR, FAR, JOIN, LAST, DONE, Y, Z = range(8)
KV = 98
WEIGHTS = (96, 97)


class Flow:
    def __init__(self, refs, me, side):
        self.r = refs
        self.me = me
        self.side = side
        self.now = 0.0
        self.y_free = 0.0
        self.z_free = 0.0
        self.middle_free = 0.0
        self.pending = []
        self.near_done = {}
        self.stores = []

    def at(self, mask):
        return {PAGE: flip(self.me, mask)}

    def core_copy(self, unit):
        r = self.r
        return pltpu.make_async_remote_copy(
            src_ref=r.ring.at[unit % RING],
            dst_ref=r.core_in.at[unit % LANDINGS],
            send_sem=r.core_sent.at[unit % RING],
            recv_sem=r.core_got.at[unit % LANDINGS],
            device_id=self.at(1),
            device_id_type=pl.DeviceIdType.MESH,
        )

    def y_copy(self, unit):
        r = self.r
        source, landing = r.keep.at[unit, 1], r.y_in.at[Y_PLACES[unit]]
        if unit in TURNED_UNITS:
            source, landing = r.keep.at[unit, 1, 0], r.z_in.at[PLAIN_UNITS.index(unit), 2]
        return pltpu.make_async_remote_copy(
            src_ref=source,
            dst_ref=landing,
            send_sem=r.y_sent.at[0],
            recv_sem=r.y_got.at[Y_PLACES[unit]],
            device_id=self.at(2),
            device_id_type=pl.DeviceIdType.MESH,
        )

    def z_place(self, unit):
        if unit in PLAIN_UNITS:
            return PLAIN_UNITS.index(unit)
        return len(PLAIN_UNITS) + DOWN_STEPS[DOWN_UNITS.index(unit)] // 2

    def near_copy(self, unit, arriving=False):
        r = self.r
        if unit in DOWN_UNITS:
            step = DOWN_STEPS[DOWN_UNITS.index(unit)]
            if (step in NEAR_STEPS) == arriving:
                return None
            target = unit if arriving else DOWN_UNITS[DOWN_STEPS.index(step ^ 1)]
            source, landing = r.keep.at[unit], r.near_down.at[step // 2]
        elif unit in TURNED_UNITS:
            target = unit
            source = r.keep.at[unit, :, pl.ds(2, 2)]
            landing = r.turned_in.at[TURNED_UNITS.index(unit)]
        else:
            target = unit
            if unit in UP_UNITS and not arriving:
                target = UP_UNITS[DOWN_STEPS.index(DOWN_STEPS[UP_UNITS.index(unit)] ^ 1)]
            source = r.keep.at[unit, 0, pl.ds(2, 2)]
            landing = r.z_in.at[PLAIN_UNITS.index(target), pl.ds(0, 2)]
        return pltpu.make_async_remote_copy(
            src_ref=source,
            dst_ref=landing,
            send_sem=r.near_sent.at[0],
            recv_sem=r.near_got.at[self.z_place(target)],
            device_id=self.at(4),
            device_id_type=pl.DeviceIdType.MESH,
        )

    def far_copy(self, unit, arriving=False):
        r = self.r
        if unit in DOWN_UNITS:
            step = DOWN_STEPS[DOWN_UNITS.index(unit)]
            if step != (0 if arriving else 3):
                return None
            target = DOWN_UNITS[DOWN_STEPS.index(0)]
            source, landing = r.keep.at[unit, 0], r.far_down
        elif unit in TURNED_UNITS:
            target = unit
            source, landing = r.keep.at[unit, :, 1], r.z_in.at[PLAIN_UNITS.index(unit), pl.ds(0, 2)]
        else:
            target = unit
            if unit in UP_UNITS and not arriving:
                target = UP_UNITS[DOWN_STEPS.index(DOWN_STEPS[UP_UNITS.index(unit)] ^ 3)]
            source, landing = r.keep.at[unit, 0, 1], r.z_in.at[PLAIN_UNITS.index(target), 2]
        return pltpu.make_async_remote_copy(
            src_ref=source,
            dst_ref=landing,
            send_sem=r.far_sent.at[0],
            recv_sem=r.far_got.at[self.z_place(target)],
            device_id=self.at(12),
            device_id_type=pl.DeviceIdType.MESH,
        )

    def produce(self, unit, left, *rights):
        r = self.r
        first = 0
        for right in rights:
            last = first + right.shape[1]
            r.sums[:, first:last] = contract(left, right, 0, 0).astype(BF)
            first = last
        self.tick(1.2)
        if unit >= RING:
            self.core_copy(unit - RING).wait_send()
        core = lax.rem(self.me, 2)
        y = lax.rem(lax.div(self.me, 2), 2)
        z = lax.div(self.me, 4)
        for rel_y in range(2):
            for rel_z in range(4):
                y_at = flip(y, rel_y)
                if unit in DOWN_UNITS:
                    first = y_at * 8 * ROWS
                    mine = first + core * 4 * ROWS + rel_z * ROWS
                    other = first + (1 - core) * 4 * ROWS + rel_z * ROWS
                else:
                    first = flip(z, rel_z) * 4 * ROWS + y_at * 2 * ROWS
                    mine = first + core * ROWS
                    other = first + (1 - core) * ROWS
                slot = rel_y * 4 + (rel_z if unit in DOWN_UNITS else SLOT_OF[rel_z])
                r.ring[unit % RING, rel_y, slot - 4 * rel_y] = r.sums[pl.ds(pl.multiple_of(other, 16), ROWS), :]
                r.keep[unit, rel_y, slot - 4 * rel_y] = r.sums[pl.ds(pl.multiple_of(mine, 16), ROWS), :]
        if unit >= LANDINGS:
            pl.semaphore_wait(r.credit.at[unit - LANDINGS], 1)
        self.core_copy(unit).start()
        self.now += 0.5
        self.pending.append([unit, CORE, self.now + CORE_US])

    def advance(self, entry):
        self.plan(entry)()

    def near_busy(self, blocks):
        self.z_free = max(self.now, self.z_free) + blocks * LINK_US / 4
        return self.z_free + LATENCY_US

    def far_busy(self, blocks):
        self.z_free = max(self.now, self.z_free) + blocks * LINK_US / 4
        self.middle_free = max(self.now, self.middle_free) + blocks * LINK_US / 2
        return max(self.z_free, self.middle_free) + LATENCY_US

    def y_busy(self, us):
        self.y_free = max(self.now, self.y_free) + us
        return self.y_free + 0.3

    def plan(self, entry):
        unit, stage, _ = entry
        step = None
        if unit in WEIGHTS:
            if stage < 3:
                entry[1:] = [stage + 1, self.now + (3.8, 8.0, 2.5)[stage]]
            else:
                entry[1] = DONE
            return functools.partial(self.run, unit, stage)
        if unit in DOWN_UNITS:
            step = DOWN_STEPS[DOWN_UNITS.index(unit)]
        if unit == KV:
            entry[1] = DONE
        elif unit == SMALL:
            free = max(self.now, self.y_free if stage == CORE else self.z_free)
            following = {CORE: Y, Y: Z, Z: DONE}[stage]
            entry[1:] = [following, free + (1.0 if stage == CORE else 7.0)]
        elif stage == CORE:
            if step in NEAR_STEPS:
                self.near_done[step ^ 1] = self.near_busy(8)
                entry[1] = DONE
            elif step is not None:
                entry[1:] = [JOIN, self.near_done[step]]
            else:
                entry[1:] = [Y, self.y_busy(LINK_US)]
        elif stage == JOIN:
            entry[1:] = [Y, self.y_busy(LINK_US)]
        elif stage == Y:
            if step is not None:
                done = self.far_busy(4) if step == 3 else self.z_free + LATE_US
                entry[1:] = [DONE, 0.0] if step == 3 else [FAR, done + LATE_US]
            else:
                entry[1:] = [NEAR, self.near_busy(2)]
                if unit in UP_UNITS:
                    self.meet(entry, [unit, UP_UNITS[DOWN_STEPS.index(DOWN_STEPS[UP_UNITS.index(unit)] ^ 1)]])
        elif stage == NEAR:
            entry[1:] = [FAR, self.far_busy(1) + (8.0 if unit in KV_UNITS else LATE_US)]
            if unit in UP_UNITS:
                self.meet(entry, UP_UNITS)
        else:
            entry[1] = DONE
            if unit == KV_UNITS[1]:
                self.pending.append([KV, CORE, self.now + LATE_US])
        return functools.partial(self.run, unit, stage)

    def meet(self, entry, units):
        due, entry[2] = entry[2], float("inf")
        waiting = [e for e in self.pending if e[0] in units and e[1] == entry[1]]
        if len(waiting) == len(units):
            for other in waiting:
                other[2] = due

    def join(self, unit, half, places, arrived):
        r = self.r
        for place in places:
            total = r.keep[unit, half, place].astype(F32) + arrived[place].astype(F32)
            r.keep[unit, half, place] = total.astype(BF)

    def run(self, unit, stage):
        r = self.r
        if unit in WEIGHTS:
            self.weight_arrival(WEIGHTS.index(unit), stage).wait_recv()
            if stage < 3:
                self.weight_copy(WEIGHTS.index(unit), stage + 1).start()
            return
        if unit == KV:
            self.kv_copy().wait_recv()
            self.store(KV)
            return
        if unit == SMALL:
            self.run_small((CORE, Y, Z).index(stage))
            return
        step = None
        if unit in DOWN_UNITS:
            step = DOWN_STEPS[DOWN_UNITS.index(unit)]
        turned = unit in TURNED_UNITS
        if stage == CORE:
            self.core_copy(unit).wait_recv()
            arrived = r.core_in.at[unit % LANDINGS]
            self.join(unit, 1, (0, 1, 2, 3), arrived.at[1])
            if step is None and not turned:
                self.y_copy(unit).start()
            self.join(unit, 0, (0, 1, 2, 3), arrived.at[0])
            if turned or step in NEAR_STEPS:
                self.near_copy(unit).start()
            if unit < UNITS - LANDINGS:
                pl.semaphore_signal(
                    r.credit.at[unit], 1, device_id=self.at(1), device_id_type=pl.DeviceIdType.MESH
                )
        elif stage == JOIN:
            self.near_copy(unit, arriving=True).wait_recv()
            arrived = r.near_down.at[step // 2]
            self.join(unit, 1, (0, 1, 2, 3), arrived.at[1])
            self.y_copy(unit).start()
            self.join(unit, 0, (0, 1, 2, 3), arrived.at[0])
        elif stage == Y:
            self.y_copy(unit).wait_recv()
            self.join(unit, 0, (2, 3, 0, 1), r.y_in.at[Y_PLACES[unit]])
            if step is None:
                self.near_copy(unit).start()
            elif step == 3:
                self.far_copy(unit).start()
        elif stage == NEAR:
            self.near_copy(unit, arriving=True).wait_recv()
            if turned:
                arrived = r.turned_in.at[TURNED_UNITS.index(unit)]
                for half in (0, 1):
                    self.join(unit, half, (1, 0), arrived.at[half])
            else:
                self.join(unit, 0, (1, 0), r.z_in.at[PLAIN_UNITS.index(unit)])
            self.far_copy(unit).start()
        elif turned and stage == FAR:
            self.far_copy(unit, arriving=True).wait_recv()
            arrived = r.z_in.at[PLAIN_UNITS.index(unit)]
            for half in (1, 0):
                total = r.keep[unit, half, 0].astype(F32) + arrived[half].astype(F32)
                r.keep[unit, half, 0] = total.astype(BF)
                if half:
                    self.y_copy(unit).start()
        elif turned:
            self.y_copy(unit).wait_recv()
            self.finish(unit)
        else:
            self.far_copy(unit, arriving=True).wait_recv()
            self.finish(unit)

    def small_copies(self, stage):
        r = self.r
        return [
            pltpu.make_async_remote_copy(
                src_ref=r.small_in.at[5 + stage],
                dst_ref=r.small_in.at[place],
                send_sem=r.small_sent.at[0],
                recv_sem=r.small_got.at[place],
                device_id=self.at(mask),
                device_id_type=pl.DeviceIdType.MESH,
            )
            for place, mask in SMALL_STEPS[stage]
        ]

    def kv_copy(self):
        r = self.r
        return pltpu.make_async_remote_copy(
            src_ref=r.kv_out,
            dst_ref=r.kv_in,
            send_sem=r.kv_sent.at[0],
            recv_sem=r.kv_got.at[0],
            device_id={STREAM: 1 - self.side},
            device_id_type=pl.DeviceIdType.MESH,
        )

    def weight_copy(self, half, stage):
        r = self.r
        core, y, z = lax.rem(self.me, 2), lax.rem(lax.div(self.me, 2), 2), lax.rem(lax.div(self.me, 4), 2)
        share = r.other_w.shape[-2]
        target, device = r.other_w.at[half, z, y, core], {STREAM: 1 - self.side}
        source = target
        if stage == 0:
            first = pl.multiple_of((z * 4 + y * 2 + core) * share, 16)
            source = r.w_ckv.at[pl.ds(first, share), half * WIDTH : (half + 1) * WIDTH]
        elif stage == 1:
            device = self.at(4)
        elif stage == 2:
            source = target = r.other_w.at[half, :, y, core]
            device = self.at(2)
        else:
            source = target = r.other_w.at[half, :, :, core]
            device = self.at(1)
        return pltpu.make_async_remote_copy(
            src_ref=source,
            dst_ref=target,
            send_sem=r.weight_sent.at[0],
            recv_sem=r.weight_got.at[half, stage],
            device_id=device,
            device_id_type=pl.DeviceIdType.MESH,
        )

    def weight_arrival(self, half, stage):
        r = self.r
        core, y, z = lax.rem(self.me, 2), lax.rem(lax.div(self.me, 2), 2), lax.rem(lax.div(self.me, 4), 2)
        target = (
            r.other_w.at[half, z, y, core],
            r.other_w.at[half, 1 - z, y, core],
            r.other_w.at[half, :, 1 - y, core],
            r.other_w.at[half, :, :, 1 - core],
        )[stage]
        return pltpu.make_async_remote_copy(
            src_ref=target,
            dst_ref=target,
            send_sem=r.weight_sent.at[0],
            recv_sem=r.weight_got.at[half, stage],
            device_id=self.at(1),
            device_id_type=pl.DeviceIdType.MESH,
        )

    def start_weights(self):
        for half in range(2):
            self.weight_copy(half, 0).start()
            self.pending.append([WEIGHTS[half], 0, self.now + 4.0 + 3.0 * half])

    def finish_weights(self):
        while True:
            left = [e for e in self.pending if e[0] in WEIGHTS]
            if not left:
                return
            entry = min(left, key=lambda e: e[2])
            self.now = max(self.now, entry[2])
            self.advance(entry)
            self.pending = [e for e in self.pending if e[1] != DONE]

    def start_small(self):
        r = self.r
        r.small_in[5] = r.small_sum[...]
        for copy in self.small_copies(0):
            copy.start()
        self.pending.append([SMALL, CORE, self.now + CORE_US + 1.0])

    def run_small(self, stage):
        r = self.r
        for copy in self.small_copies(stage):
            copy.wait_recv()
        for place, _ in SMALL_STEPS[stage]:
            r.small_sum[...] += r.small_in[place]
        if stage < 2:
            r.small_in[6 + stage] = r.small_sum[...]
            for copy in self.small_copies(stage + 1):
                copy.start()

    def due(self):
        while True:
            ready = [e for e in self.pending if e[2] <= self.now]
            if not ready:
                return
            entry = min(ready, key=lambda e: e[2])
            yield entry
            self.pending = [e for e in self.pending if e[1] != DONE]

    def tick(self, us):
        self.now += us
        for entry in self.due():
            self.advance(entry)

    def drain(self):
        while self.pending:
            self.now = max(self.now, min(e[2] for e in self.pending))
            for entry in self.due():
                self.advance(entry)
        for unit in range(UNITS - RING, UNITS):
            self.core_copy(unit).wait_send()
        r = self.r
        for whole, sent in (
            (r.y_in, r.y_sent),
            (r.keep.at[pl.ds(0, 5)], r.near_sent),
            (r.keep.at[pl.ds(0, 2)], r.far_sent),
            (r.small_in.at[pl.ds(0, 5)], r.small_sent),
            (r.other_w, r.weight_sent),
            (r.s.at[Slot.normed], r.normed_sent),
        ):
            pltpu.make_async_copy(whole, whole, sent.at[0]).wait()
        self.kv_copy().wait_send()
        for place in range(max(0, len(self.stores) - STORES), len(self.stores)):
            self.store_copy(place).wait()

    def store_copy(self, place):
        r = self.r
        unit, part = self.stores[place]
        if unit == KV:
            pairs = [(r.kv_in, r.ckv_out)]
        elif unit in DOWN_UNITS:
            pairs = [(r.done.at[pl.ds(0, 4)], r.down_out)]
        elif unit in UP_UNITS:
            tile = flip(lax.div(self.me, 4), DOWN_STEPS[UP_UNITS.index(unit)])
            columns = pl.ds(pl.multiple_of(tile * WIDTH, WIDE), WIDTH)
            pairs = [(r.done.at[self.done_at(unit)], r.up_out.at[:, columns])]
        elif unit in THIRD_UNITS:
            third = WIDTH // 3
            first = third * THIRD_UNITS.index(unit)
            source = r.done.at[self.done_at(unit)]
            pairs = [
                (source.at[:, pl.ds(i * third, third)], r.qkv_out.at[:, pl.ds(i * WIDTH + first, third)])
                for i in range(3)
            ]
        else:
            pairs = [(r.done.at[self.done_at(unit)], {8: r.cout_out, 11: r.cq_out, 12: r.out_out}[unit])]
        return pltpu.make_async_copy(*pairs[part], r.stored_sums.at[place % STORES])

    def done_at(self, unit):
        return 4 + PLAIN_UNITS.index(unit)

    def store(self, unit):
        for part in range(3 if unit in THIRD_UNITS else 1):
            place = len(self.stores)
            if place >= STORES:
                self.store_copy(place - STORES).wait()
            self.stores.append((unit, part))
            self.store_copy(place).start()

    def finish(self, unit):
        r = self.r
        if unit in DOWN_UNITS:
            r.done[0:4] = r.keep[unit, 0].astype(F32) + r.far_down[...].astype(F32)
            self.store(unit)
            return
        total = r.keep[unit, 0, 0].astype(F32) + r.z_in[PLAIN_UNITS.index(unit), 2].astype(F32)
        if unit in KV_UNITS:
            half = KV_UNITS.index(unit)
            r.kv_out[:, half * WIDTH : (half + 1) * WIDTH] = total
            if half:
                self.kv_copy().start()
            return
        r.done[self.done_at(unit)] = total
        self.store(unit)


WIDTH = 768
ROWS = 48
DOWN_UNITS = (1, 3, 5, 7)
TURNED_UNITS = ()
UP_UNITS = (0, 2, 4, 6)
DOWN_STEPS = (1, 2, 3, 0)
NEAR_STEPS = (1, 2)
SLOT_OF = (0, 2, 3, 1)
PLAIN_UNITS = (0, 2, 4, 6, 8, 9, 10, 11, 12, 13, 14, 15)
UNITS = 16
Y_PLACES = {unit: at for at, unit in enumerate((0, 2, 4, 5, 6, 7, 8, 9, 10, 11, 12, 13, 14, 15))}
KV_UNITS = (9, 10)
THIRD_UNITS = (13, 14, 15)


class Fetch:
    def __init__(self, source, target, semaphores, free):
        self.free = free
        self.place = free.pop(0)
        self.copy = pltpu.make_async_copy(source, target, semaphores.at[self.place])
        self.copy.start()

    def wait(self):
        self.copy.wait()
        self.free.append(self.place)


class Refs(NamedTuple):
    states: Any
    cotangent: Any
    w_qkv: Any
    w_out: Any
    w_cq: Any
    w_ckv: Any
    w_cout: Any
    w_up: Any
    w_down: Any
    counts: Any
    box_x: Any
    box_y: Any
    gain1: Any
    gain2: Any
    table_in: Any
    result_out: Any
    states_out: Any
    held_out: Any
    down_out: Any
    up_out: Any
    cout_out: Any
    cq_out: Any
    out_out: Any
    qkv_out: Any
    ckv_out: Any
    gain1_out: Any
    gain2_out: Any
    table_out: Any
    s: Any
    f: Any
    w: Any
    fetched: Any
    stored: Any
    sums: Any
    keep: Any
    ring: Any
    core_in: Any
    y_in: Any
    z_in: Any
    near_down: Any
    far_down: Any
    turned_in: Any
    core_sent: Any
    core_got: Any
    y_sent: Any
    y_got: Any
    near_sent: Any
    near_got: Any
    far_sent: Any
    far_got: Any
    credit: Any
    normed_sent: Any
    normed_got: Any
    back_sent: Any
    back_got: Any
    weight_sent: Any
    weight_got: Any
    other_w: Any
    done: Any
    stored_sums: Any
    kv_out: Any
    kv_in: Any
    kv_sent: Any
    kv_got: Any
    self_lse: Any
    cross_lse: Any
    bands: Any
    onehot: Any
    flipped: Any
    small_sum: Any
    table: Any
    gain_sums: Any
    table_sum: Any
    small_in: Any
    small_sent: Any
    small_got: Any
    d_bands: Any


INPUTS, SMALL_INPUTS, OUTPUTS, KEPT_OUTPUTS = 9, 6, 13, 0


def layer_kernel(scale, *refs):
    r = Refs(*refs)
    me = lax.axis_index(PAGE)
    side = lax.axis_index(STREAM)
    flow = Flow(r, me, side)
    count, width = r.states.shape
    pairs = width // WIDE
    half_rows = count // 2
    core, y, z = lax.rem(me, 2), lax.rem(lax.div(me, 2), 2), lax.div(me, 4)
    partner = {STREAM: 1 - side}

    free = list(range(FETCHES))

    def fetch(source, target):
        return Fetch(source, target, r.fetched, free)

    def slot(name):
        return r.s.at[name]

    def tile_of(step):
        return pl.ds(pl.multiple_of(flip(z, DOWN_STEPS[step]) * width, WIDE), width)

    def columns(ref, first):
        return ref.at[:, width * first : width * (first + 1)]

    got_states = fetch(r.states, slot(Slot.second))
    got_q, got_k, got_v = [fetch(columns(r.w_qkv, i), r.w.at[i]) for i in range(3)]
    got_out = fetch(r.w_out, r.w.at[3])
    got_cq = fetch(r.w_cq, r.w.at[4])
    got_grad = fetch(r.cotangent, slot(Slot.low_grad))

    barrier = pltpu.get_barrier_semaphore()
    others = [{PAGE: flip(me, mask)} for mask in (1, 2, 4, 8, 12)] + [partner]
    for other in others:
        pl.semaphore_signal(barrier, 1, device_id=other, device_id_type=pl.DeviceIdType.MESH)

    own_count, other_count = r.counts[side], r.counts[1 - side]
    slots_row = lax.broadcasted_iota(jnp.int32, (1, count), 1)
    mask_own = jnp.where(slots_row < own_count, 0.0, MASKED).astype(F32)
    mask_other = jnp.where(slots_row < other_count, 0.0, MASKED).astype(F32)
    slots_column = lax.broadcasted_iota(jnp.int32, (count, 1), 0)
    valid = jnp.where(slots_column < own_count, 1.0, 0.0).astype(F32)
    buckets = WIDE // 2
    small = own_count <= GRID_SMALL * GRID_SMALL
    tall = [jnp.floor((slots_row.astype(F32) + 0.5) * (1.0 / grid)).astype(jnp.int32) for grid in (GRID_SMALL, GRID_LARGE)]
    grid_top = jnp.where(small, tall[0], tall[1])
    grid_left = slots_row - jnp.where(small, tall[0] * GRID_SMALL, tall[1] * GRID_LARGE)
    left = jnp.where(side == 0, r.box_x[...], grid_left)
    top = jnp.where(side == 0, r.box_y[...], grid_top)
    index = lax.broadcasted_iota(jnp.int32, (buckets, count), 0)

    def marks(first, second):
        both = [jnp.where(index == first, 1.0, 0.0), jnp.where(index == second, 1.0, 0.0)]
        return jnp.concatenate(both, 0).astype(BF)

    r.onehot[...] = marks(left, top)
    r.flipped[...] = marks(buckets - 1 - left, buckets - 1 - top)
    keep = same_block((WIDE, WIDE))
    lower = lax.broadcasted_iota(jnp.int32, (WIDE, WIDE), 0) >= buckets
    heads = 2 * pairs
    for head in range(heads):
        across = jnp.broadcast_to(r.table_in[head : head + 1, :], (WIDE, WIDE))
        down = jnp.broadcast_to(r.table_in[heads + head : heads + head + 1, :], (WIDE, WIDE))
        rolled = pltpu.roll(jnp.where(lower, down, across), buckets, 1, stride=1, stride_axis=0)
        r.bands[head // 2, head % 2] = jnp.where(keep, rolled, 0.0).astype(BF)

    def normed_copy(part):
        rows = pl.ds(part * half_rows, half_rows)
        return pltpu.make_async_remote_copy(
            src_ref=slot(Slot.normed).at[rows],
            dst_ref=slot(Slot.other).at[rows],
            send_sem=r.normed_sent.at[0],
            recv_sem=r.normed_got.at[part],
            device_id=partner,
            device_id_type=pl.DeviceIdType.MESH,
        )

    got_states.wait()
    for part in range(2):
        rows = slice(part * half_rows, (part + 1) * half_rows)
        inputs = r.s[Slot.second, rows, :].astype(F32)
        r.f[2, rows, :] = inputs
        r.s[Slot.normed, rows, :] = norm_rows(inputs, r.gain1[...]).astype(BF)
    pl.semaphore_wait(barrier, len(others))

    flow.start_weights()
    for part in range(2):
        normed_copy(part).start()
    flow.tick(0.1)
    for name, copy, at in ((Slot.query, got_q, 0), (Slot.key, got_k, 1), (Slot.value, got_v, 2)):
        copy.wait()
        slot(name)[...] = contract(slot(Slot.normed)[...], r.w[at], 1, 0).astype(BF)
        flow.tick(1.0)
    held = [pltpu.make_async_copy(slot(name), r.held_out.at[i], r.stored.at[2 + i]) for i, name in enumerate((Slot.query, Slot.key, Slot.value))]
    for copy in held:
        copy.start()
    got_cout = fetch(r.w_cout, r.w.at[0])
    got_down = [fetch(r.w_down.at[tile_of(step)], r.w.at[1 + step]) for step in range(2)]

    def pair_loop(us, step, first=0, last=pairs):
        events = []
        for pair in range(first, last):
            flow.now += us
            events.append([])
            for entry in flow.due():
                events[-1].append(flow.plan(entry))

        @pl.loop(first, last)
        def _(pair):
            step(pair)
            for place, steps in enumerate(events, first):
                if steps:

                    @pl.when(pair == place)
                    def _(steps=steps):
                        for run in steps:
                            run()

    def lanes_of(pair):
        return pl.ds(pl.multiple_of(pair * WIDE, WIDE), WIDE)

    def self_forward(pair):
        lanes = lanes_of(pair)
        output, lse = forward_pair(
            scale,
            r.s[Slot.query, :, lanes],
            r.s[Slot.key, :, lanes],
            r.s[Slot.value, :, lanes],
            mask_own,
            (r.bands[pair], r.onehot[...]),
        )
        r.s[Slot.attended, :, lanes] = output
        r.self_lse[pair] = lse

    pair_loop(1.95, self_forward)

    got_out.wait()
    r.f[2] = r.f[2] + contract(slot(Slot.attended)[...], r.w[3], 1, 0)
    slot(Slot.low_middle)[...] = r.f[2].astype(BF)
    got_down.append(fetch(r.w_down.at[tile_of(2)], r.w.at[3]))
    got_cq.wait()
    slot(Slot.cross_query)[...] = contract(slot(Slot.low_middle)[...], r.w[4], 1, 0).astype(BF)
    got_down.append(fetch(r.w_down.at[tile_of(3)], r.w.at[4]))
    flow.tick(2.2)
    got_grad.wait()
    slot(Slot.low_grad)[...] = (slot(Slot.low_grad)[...].astype(F32) * valid).astype(BF)
    flow.tick(0.5)

    back_slots = (Slot.back0, Slot.back1, Slot.back2, Slot.back3)
    hidden_slots = (Slot.query, Slot.key, Slot.value, Slot.hidden3)
    got_up = []
    for step in range(4):
        got_down[step].wait()
        r.s[back_slots[step]] = contract(slot(Slot.low_grad)[...], r.w[1 + step], 1, 1).astype(BF)
        got_up.append(fetch(r.w_up.at[:, tile_of(step)], r.w.at[1 + step]))
        flow.tick(1.05)
    flow.finish_weights()
    for copy in held:
        copy.wait()
    for part in range(2):
        normed_copy(part).wait_recv()
    flow.now = max(flow.now, 30.0)
    for at, name in enumerate((Slot.cross_key, Slot.cross_value)):
        slot(name)[...] = contract(slot(Slot.other)[...], r.other_w[at].reshape(width, width), 1, 0).astype(BF)
    flow.tick(2.0)

    def cross_forward(pair):
        lanes = lanes_of(pair)
        output, lse = forward_pair(
            scale,
            r.s[Slot.cross_query, :, lanes],
            r.s[Slot.cross_key, :, lanes],
            r.s[Slot.cross_value, :, lanes],
            mask_other,
            None,
        )
        r.s[Slot.crossed, :, lanes] = output
        r.cross_lse[pair] = lse

    pair_loop(1.8, cross_forward)
    got_cout.wait()
    r.f[2] = r.f[2] + contract(slot(Slot.crossed)[...], r.w[0], 1, 0)
    for part in range(2):
        rows = slice(part * half_rows, (part + 1) * half_rows)
        r.s[Slot.second, rows, :] = norm_rows(r.f[2, rows, :], r.gain2[...]).astype(BF)
    flow.tick(2.0)

    second_at, grad_at = Slot.second, Slot.low_grad
    for step in range(4):
        hidden_at, d_up_at, up_at = hidden_slots[step], back_slots[step], 1 + step
        got_up[step].wait()

        @pl.loop(0, 2)
        def _(part, hidden_at=hidden_at, d_up_at=d_up_at, up_at=up_at):
            rows = pl.ds(pl.multiple_of(part * half_rows, 16), half_rows)
            hidden, slope = gelu_pair(contract(r.s[second_at, rows, :], r.w[up_at], 1, 0))
            r.s[hidden_at, rows, :] = hidden.astype(BF)
            r.s[d_up_at, rows, :] = (slope * r.s[d_up_at, rows, :].astype(F32)).astype(BF)

        flow.tick(2.0)
        flow.produce(UP_UNITS[step], r.s[second_at], r.s[d_up_at])
        flow.tick(0.1)
        flow.produce(DOWN_UNITS[step], r.s[hidden_at], r.s[grad_at])
        flow.tick(0.2)
    for step in range(4):
        for part in range(2):
            rows = slice(part * half_rows, (part + 1) * half_rows)
            back = contract(r.s[back_slots[step], rows, :], r.w[1 + step], 1, 1)
            r.f[0, rows, :] = back if step == 0 else r.f[0, rows, :] + back
        flow.tick(1.2)
    got_cq, got_out = fetch(r.w_cq, r.w.at[1]), fetch(r.w_out, r.w.at[2])
    got_q, got_k = [fetch(columns(r.w_qkv, i), r.w.at[3 + i]) for i in range(2)]

    low_after_at, d_crossed_at = Slot.back0, Slot.second
    r.small_sum[6:12, :] = fold(norm_back(r.f.at[2], r.f, 0, r.gain2, r.s, grad_at, low_after_at))
    flow.tick(1.7)
    r.s[d_crossed_at] = contract(r.s[low_after_at], r.w[0], 1, 1).astype(BF)
    got_v = fetch(columns(r.w_qkv, 2), r.w.at[0])
    flow.tick(1.1)
    flow.produce(8, slot(Slot.crossed)[...], r.s[low_after_at])
    flow.tick(0.1)

    d_query_at, d_key_at, d_value_at = Slot.back1, Slot.low_grad, Slot.d_value

    def cross_backward(pair):
        lanes = lanes_of(pair)
        d_query, d_key, d_value = backward_pair(
            scale,
            r.s[Slot.cross_query, :, lanes],
            r.s[Slot.cross_key, :, lanes],
            r.s[Slot.cross_value, :, lanes],
            r.s[d_crossed_at, :, lanes],
            r.s[Slot.crossed, :, lanes],
            r.cross_lse[pair],
            mask_other,
            None,
        )
        r.s[d_query_at, :, lanes] = d_query
        r.s[d_key_at, :, lanes] = d_key
        r.s[d_value_at, :, lanes] = d_value

    pair_loop(2.45, cross_backward)

    flow.produce(9, slot(Slot.other)[...], r.s[d_key_at])
    flow.tick(0.1)
    flow.produce(10, slot(Slot.other)[...], r.s[d_value_at])
    flow.tick(0.1)
    back_at = Slot.crossed
    r.s[back_at] = (
        contract(r.s[d_key_at], r.other_w[0].reshape(width, width), 1, 1)
        + contract(r.s[d_value_at], r.other_w[1].reshape(width, width), 1, 1)
    ).astype(BF)
    back_copy = pltpu.make_async_remote_copy(
        src_ref=r.s.at[back_at],
        dst_ref=slot(Slot.returned),
        send_sem=r.back_sent.at[0],
        recv_sem=r.back_got.at[0],
        device_id=partner,
        device_id_type=pl.DeviceIdType.MESH,
    )
    back_copy.start()
    flow.tick(2.0)
    got_states = fetch(r.states, r.s.at[d_key_at])

    query_at, key_at, value_at = Slot.back3, Slot.back0, Slot.d_value
    got_held = [fetch(r.held_out.at[i], r.s.at[at]) for i, at in enumerate((query_at, key_at, value_at))]

    flow.produce(11, slot(Slot.low_middle)[...], r.s[d_query_at])
    got_cq.wait()
    r.f[0] = r.f[0] + contract(r.s[d_query_at], r.w[1], 1, 1)
    d_middle_at, d_attended_at = Slot.cross_key, Slot.cross_value
    r.s[d_middle_at] = r.f[0].astype(BF)
    flow.tick(1.5)
    flow.produce(12, slot(Slot.attended)[...], r.s[d_middle_at])
    got_out.wait()
    r.s[d_attended_at] = contract(r.s[d_middle_at], r.w[2], 1, 1).astype(BF)
    got_down = [fetch(r.w_down.at[tile_of(step)], r.w.at[1 + step]) for step in range(2)]
    flow.tick(1.2)

    dq_at, dk_at, dv_at = Slot.cross_query, Slot.back2, Slot.second
    for copy in got_held:
        copy.wait()

    def self_backward(pair):
        lanes = lanes_of(pair)
        d_query, d_key, d_value, d_bands = backward_pair(
            scale,
            r.s[query_at, :, lanes],
            r.s[key_at, :, lanes],
            r.s[value_at, :, lanes],
            r.s[d_attended_at, :, lanes],
            r.s[Slot.attended, :, lanes],
            r.self_lse[pair],
            mask_own,
            (r.bands[pair], r.onehot[...], r.flipped[...]),
        )
        r.s[dq_at, :, lanes] = d_query
        r.s[dk_at, :, lanes] = d_key
        r.s[dv_at, :, lanes] = d_value
        r.d_bands[pair] = d_bands

    third = width // 3
    normed_at = Slot.normed
    for part in range(3):
        pair_loop(3.2, self_backward, part * pairs // 3, (part + 1) * pairs // 3)
        wanted = slice(part * third, (part + 1) * third)
        flow.produce(13 + part, r.s[normed_at], r.s[dq_at, :, wanted], r.s[dk_at, :, wanted], r.s[dv_at, :, wanted])
    for copy in (got_q, got_k, got_v):
        copy.wait()
    r.f[1] = (
        contract(r.s[dq_at], r.w[3], 1, 1)
        + contract(r.s[dk_at], r.w[4], 1, 1)
        + contract(r.s[dv_at], r.w[0], 1, 1)
    )
    got_down += [fetch(r.w_down.at[tile_of(step)], r.w.at[1 + step]) for step in range(2, 4)]
    flow.tick(3.2)
    for head in range(heads):
        across, down = unband(r.d_bands[head // 2, head % 2])
        r.small_sum[16 + head : 17 + head, :] = across
        r.small_sum[16 + heads + head : 17 + heads + head, :] = down
    flow.tick(1.0)
    got_states.wait()
    back_copy.wait_recv()
    for part in range(2):
        rows = slice(part * half_rows, (part + 1) * half_rows)
        r.f[1, rows, :] += r.s[Slot.returned, rows, :].astype(F32)
    gain1_grad = norm_back(r.s.at[d_key_at], r.f, 1, r.gain1, None, None, None)
    sent_states = pltpu.make_async_copy(r.f.at[0], r.states_out, r.stored.at[1])
    sent_states.start()
    r.small_sum[0:6, :] = fold(gain1_grad)
    r.small_sum[12:16, :] = jnp.zeros((4, WIDE), F32)
    flow.tick(2.0)

    flow.start_small()
    flow.tick(0.2)

    result_at = Slot.back3
    for step in range(4):
        got_down[step].wait()
        r.f[2] = r.f[2] + contract(r.s[hidden_slots[step]], r.w[1 + step], 1, 0)
        flow.tick(1.3)
    r.s[result_at] = (r.f[2] * valid).astype(BF)
    sent_result = pltpu.make_async_copy(r.s.at[result_at], r.result_out, r.stored.at[0])
    sent_result.start()
    flow.tick(0.4)
    flow.drain()
    gains = r.small_sum[...]
    shift = width - me * ROWS
    for place in range(2):
        row = jnp.concatenate([gains[6 * place + i : 6 * place + i + 1] for i in range(width // WIDE)], 1)
        r.gain_sums[place] = pltpu.roll(row, lax.rem(shift, width), 1)[:, :ROWS]
    flat = jnp.concatenate([gains[16:], jnp.zeros((WIDE - 2 * heads, WIDE), F32)], 0)
    r.table[...] = flat.T
    table_rows = r.table_out.shape[0]
    r.table_sum[...] = r.table[pl.ds(pl.multiple_of(me * table_rows, 8), table_rows), 0 : 2 * heads]
    last = [
        pltpu.make_async_copy(source, target, r.stored.at[5 + i])
        for i, (source, target) in enumerate(
            ((r.gain_sums.at[0], r.gain1_out), (r.gain_sums.at[1], r.gain2_out), (r.table_sum, r.table_out))
        )
    ]
    for copy in last:
        copy.start()
    for copy in last:
        copy.wait()
    back_copy.wait_send()
    sent_result.wait()
    sent_states.wait()


class Slot:
    (
        normed,
        other,
        query,
        key,
        value,
        attended,
        low_middle,
        cross_query,
        cross_key,
        cross_value,
        crossed,
        second,
        low_grad,
        hidden3,
        back0,
        back1,
        back2,
        back3,
        d_value,
        returned,
    ) = range(20)


SMALL = 99
SMALL_STEPS = (((0, 1),), ((1, 2),), ((2, 4), (3, 8), (4, 12)))


def fold(row):
    return jnp.concatenate([row[:, WIDE * i : WIDE * (i + 1)] for i in range(row.shape[1] // WIDE)], 0)


def norm_back(source, f, grad_at, gain, s, s_grad_at, s_out_at):
    count = f.shape[1]
    chunk = count // 4
    gain_grad = jnp.zeros((1, f.shape[2]), F32)
    for part in range(4):
        rows = slice(part * chunk, (part + 1) * chunk)
        inputs = source[rows, :].astype(F32)
        grad = f[grad_at, rows, :]
        centre = inputs - jnp.mean(inputs, axis=-1, keepdims=True)
        spread = lax.rsqrt(jnp.mean(centre * centre, axis=-1, keepdims=True) + EPSILON)
        normed = centre * spread
        gain_grad = gain_grad + jnp.sum(grad * normed, axis=0, keepdims=True)
        scaled = grad * gain[...]
        back = spread * (
            scaled
            - jnp.mean(scaled, axis=-1, keepdims=True)
            - normed * jnp.mean(scaled * normed, axis=-1, keepdims=True)
        )
        if s is not None:
            total = s[s_grad_at, rows, :].astype(F32) + back
            s[s_out_at, rows, :] = total.astype(BF)
        else:
            total = f[0, rows, :] + back
        f[0, rows, :] = total
    return gain_grad


def unband(grad):
    half = WIDE // 2
    rolled = pltpu.roll(jnp.where(same_block((WIDE, WIDE)), grad, 0.0), 1, 1, stride=1, stride_axis=0)
    return jnp.sum(rolled[:half], axis=0, keepdims=True), jnp.sum(rolled[half:], axis=0, keepdims=True)


def deliver_kernel(*refs):
    number = (len(refs) - 2) // 3
    sources, targets, held = refs[:number], refs[number : 2 * number], refs[2 * number : 3 * number]
    came, went = refs[-2:]
    arrivals = [pltpu.make_async_copy(sources[i], held[i], came.at[i]) for i in range(number)]
    departures = [pltpu.make_async_copy(held[i], targets[i], went.at[i]) for i in range(number)]
    for copy in arrivals:
        copy.start()
    for arrival, departure in zip(arrivals, departures):
        arrival.wait()
        departure.start()
    for copy in departures:
        copy.wait()


def deliver(arrays):
    anywhere = pl.BlockSpec(memory_space=pl.ANY)
    return pl.pallas_call(
        deliver_kernel,
        in_specs=[anywhere] * len(arrays),
        out_specs=[anywhere] * len(arrays),
        out_shape=[jax.ShapeDtypeStruct(array.shape, array.dtype) for array in arrays],
        scratch_shapes=[pltpu.VMEM(array.shape, array.dtype) for array in arrays]
        + [pltpu.SemaphoreType.DMA((len(arrays),))] * 2,
        compiler_params=params(63),
        cost_estimate=cost(3),
    )(*arrays)


def whole_layer(operands, scale):
    count, width = operands[0].shape
    hidden_width = operands[7].shape[1]
    heads = operands[-1].shape[0] // 2
    pairs = heads // 2
    rows = width // 16
    outs = [
        jax.ShapeDtypeStruct((count, width), BF),
        jax.ShapeDtypeStruct((count, width), F32),
        jax.ShapeDtypeStruct((3, count, width), BF),
        jax.ShapeDtypeStruct((4, rows, width), F32),
        jax.ShapeDtypeStruct((rows, hidden_width), F32),
        jax.ShapeDtypeStruct((rows, width), F32),
        jax.ShapeDtypeStruct((rows, width), F32),
        jax.ShapeDtypeStruct((rows, width), F32),
        jax.ShapeDtypeStruct((rows, 3 * width), F32),
        jax.ShapeDtypeStruct((rows, 2 * width), F32),
        jax.ShapeDtypeStruct((1, rows), F32),
        jax.ShapeDtypeStruct((1, rows), F32),
        jax.ShapeDtypeStruct((WIDE // 16, 2 * heads), F32),
    ]
    anywhere = pl.BlockSpec(memory_space=pl.ANY)
    inside = pl.BlockSpec(memory_space=pltpu.VMEM)
    scalars = pl.BlockSpec(memory_space=pltpu.SMEM)
    dma = pltpu.SemaphoreType.DMA
    small = (16 + 2 * heads, WIDE)
    scratch = [
        pltpu.VMEM((20, count, width), BF),
        pltpu.VMEM((3, count, width), F32),
        pltpu.VMEM((5, width, width), BF),
        dma((FETCHES,)),
        dma((8,)),
        pltpu.VMEM((width, width), BF),
        pltpu.VMEM((UNITS, 2, 4, rows, width), BF),
        pltpu.VMEM((RING, 2, 4, rows, width), BF),
        pltpu.VMEM((LANDINGS, 2, 4, rows, width), BF),
        pltpu.VMEM((len(Y_PLACES), 4, rows, width), BF),
        pltpu.VMEM((len(PLAIN_UNITS), 3, rows, width), BF),
        pltpu.VMEM((2, 2, 4, rows, width), BF),
        pltpu.VMEM((4, rows, width), BF),
        pltpu.VMEM((max(1, len(TURNED_UNITS)), 2, 2, 16 if not TURNED_UNITS else rows, width), BF),
        dma((RING,)),
        dma((LANDINGS,)),
        dma((1,)),
        dma((len(Y_PLACES),)),
        dma((1,)),
        dma((len(PLAIN_UNITS) + 2,)),
        dma((1,)),
        dma((len(PLAIN_UNITS) + 1,)),
        pltpu.SemaphoreType.REGULAR((UNITS - LANDINGS,)),
        dma((1,)),
        dma((2,)),
        dma((1,)),
        dma((1,)),
        dma((1,)),
        dma((2, 4)),
        pltpu.VMEM((2, 2, 2, 2, width // 8, width), BF),
        pltpu.VMEM((4 + len(PLAIN_UNITS), rows, width), F32),
        dma((STORES,)),
        pltpu.VMEM((rows, 2 * width), F32),
        pltpu.VMEM((rows, 2 * width), F32),
        dma((1,)),
        dma((1,)),
        pltpu.VMEM((pairs, 2, count), F32),
        pltpu.VMEM((pairs, 2, count), F32),
        pltpu.VMEM((pairs, 2, WIDE, WIDE), BF),
        pltpu.VMEM((WIDE, count), BF),
        pltpu.VMEM((WIDE, count), BF),
        pltpu.VMEM(small, F32),
        pltpu.VMEM((WIDE, WIDE), F32),
        pltpu.VMEM((2, 1, rows), F32),
        pltpu.VMEM((WIDE // 16, 2 * heads), F32),
        pltpu.VMEM((8, *small), F32),
        dma((1,)),
        dma((5,)),
        pltpu.VMEM((pairs, 2, WIDE, WIDE), F32),
    ]
    outputs = pl.pallas_call(
        functools.partial(layer_kernel, scale),
        in_specs=[anywhere] * INPUTS + [scalars] + [inside] * (SMALL_INPUTS - 1),
        out_specs=[anywhere] * OUTPUTS + [inside] * KEPT_OUTPUTS,
        out_shape=outs,
        scratch_shapes=scratch,
        compiler_params=pltpu.CompilerParams(
            collective_id=0, has_side_effects=True, vmem_limit_bytes=(64 << 20) - (256 << 10)
        ),
        cost_estimate=cost(150),
    )(*operands)
    down = outputs[3].reshape(4 * rows, width)
    return [*outputs[:2], down, *outputs[4:]]


def norm_rows(inputs, gain_row):
    centre = inputs - jnp.mean(inputs, axis=-1, keepdims=True)
    spread = jnp.mean(centre * centre, axis=-1, keepdims=True)
    return centre * lax.rsqrt(spread + EPSILON) * gain_row


def matmul(left, right):
    return contract(left, right, 1, 0)


def matmul_back(left, weight):
    return contract(left, weight, 1, 1)


def onehots(left, top, buckets):
    index = jnp.arange(buckets)[:, None]
    return jnp.concatenate([left[None, :] == index, top[None, :] == index], 0).astype(BF)


def body(
    states,
    counts,
    box_x,
    box_y,
    ln1_gain,
    ln2_gain,
    box_table,
    w_qkv,
    w_out,
    w_cq,
    w_ckv,
    w_cout,
    w_up,
    w_down,
    cotangent,
):
    slot_count, width = states.shape[2], states.shape[3]
    heads = box_table.shape[2] // 2
    buckets = box_table.shape[1] // 2
    scale = (width // heads) ** (-0.5)
    pairs = heads // 2
    parts = lax.axis_size(PAGE)
    side = lax.axis_index(STREAM)
    me = lax.axis_index(PAGE).astype(jnp.int32).reshape(1)
    own_count = jnp.take(counts[:, 0], side)
    other_count = jnp.take(counts[:, 0], 1 - side)
    slots = jnp.arange(slot_count)
    grid_side = jnp.where(own_count > GRID_SMALL * GRID_SMALL, GRID_LARGE, GRID_SMALL)
    left = jnp.where(side == 0, box_x[0], slots % grid_side)
    top = jnp.where(side == 0, box_y[0], slots // grid_side)
    onehot = onehots(left, top, buckets)
    flipped = onehots(buckets - 1 - left, buckets - 1 - top, buckets)
    mask_own = jnp.where(slots < own_count, 0.0, MASKED).astype(F32)[None]
    mask_other = jnp.where(slots < other_count, 0.0, MASKED).astype(F32)[None]
    valid = (slots < own_count).astype(F32)[:, None]
    bands = make_bands(box_table[0])
    weights = [w[0] for w in (w_qkv, w_out, w_cq, w_ckv, w_cout, w_up, w_down)]
    w_qkv, w_out, w_cq, w_ckv, w_cout, w_up, w_down = weights

    if parts == 16 and width == WIDTH and w_up.shape[1] == 4 * width:
        operands = [
            states[0, 0],
            cotangent[0, 0],
            w_qkv,
            w_out,
            w_cq,
            w_ckv,
            w_cout,
            w_up,
            w_down,
            counts[:, 0],
            box_x,
            box_y,
            ln1_gain,
            ln2_gain,
            box_table[0].T,
        ]
        result, states_grad, down, up, cout, cq, out, qkv, ckv, gain1, gain2, table = deliver(
            whole_layer(operands, scale)
        )
        return (
            result[None, None],
            states_grad[None, None],
            gain1,
            gain2,
            table[None],
            qkv[None],
            out[None],
            cq[None],
            ckv[None],
            cout[None],
            up[None],
            down[None],
        )

    inputs = states[0, 0].astype(F32)
    normed, norm_pull = jax.vjp(norm_rows, inputs, ln1_gain[0])
    normed = normed.astype(BF)
    cross_kv = matmul(normed, w_ckv).astype(BF)
    partner = swapped(cross_kv, STREAM, 1)
    joined = matmul(normed, w_qkv).astype(BF)
    attended, self_lse = attend_forward(joined, joined, pairs, mask_own, (bands, onehot), scale, 18)
    middle = inputs + matmul(attended, w_out)
    low_middle = middle.astype(BF)
    cross_query = matmul(low_middle, w_cq).astype(BF)
    crossed, cross_lse = attend_forward(cross_query, partner, 0, mask_other, None, scale, 16)
    after_cross = middle + matmul(crossed, w_cout)
    second, second_pull = jax.vjp(norm_rows, after_cross, ln2_gain[0])
    second = second.astype(BF)
    out_grad = cotangent[0, 0].astype(F32) * valid
    low_grad = out_grad.astype(BF)
    hidden, d_up, *down_parts = feed_forward(me, second, low_grad, w_up, w_down, parts)
    down_sum = reduce_parts(*down_parts)
    up_sum = reduce_parts(*outer_products(me, [(second, d_up)], parts, 6))
    d_after, ln2_grad = second_pull(matmul_back(d_up, w_up))
    d_after = d_after + out_grad
    low_after = d_after.astype(BF)
    d_crossed = matmul_back(low_after, w_cout).astype(BF)
    d_cross_query, d_partner = attend_backward(
        cross_query, partner, 0, d_crossed, crossed, cross_lse, mask_other, None, scale, 26
    )
    returned = swapped(d_partner, STREAM, 1)
    d_middle = d_after + matmul_back(d_cross_query, w_cq)
    low_d_middle = d_middle.astype(BF)
    d_attended = matmul_back(low_d_middle, w_out).astype(BF)
    mid_sum = reduce_parts(
        *outer_products(
            me, [(crossed, low_after), (low_middle, d_cross_query), (attended, low_d_middle)], parts, 6
        )
    )
    d_query, d_pair, d_bands = attend_backward(
        joined, joined, pairs, d_attended, attended, self_lse, mask_own, (bands, onehot, flipped), scale, 29
    )
    table_grad = gather_bands(d_bands)
    d_normed = (
        matmul_back(d_query, w_qkv[:, :width])
        + matmul_back(d_pair[0], w_qkv[:, width : 2 * width])
        + matmul_back(d_pair[1], w_qkv[:, 2 * width :])
        + matmul_back(returned[0], w_ckv[:, :width])
        + matmul_back(returned[1], w_ckv[:, width:])
    )
    d_inputs, ln1_grad = norm_pull(d_normed)
    states_grad = d_inputs + d_middle
    last_send, last_keep = outer_products(
        me,
        [
            (normed, d_query),
            (normed, d_pair[0]),
            (normed, d_pair[1]),
            (normed, returned[0]),
            (normed, returned[1]),
        ],
        parts,
        10,
    )
    last_sum = reduce_parts(last_send, last_keep)
    small = jnp.concatenate(
        [ln1_grad.reshape(parts, -1), ln2_grad.reshape(parts, -1), table_grad.reshape(parts, -1)], 1
    )
    small_sum = reduce_small(me[0], small)
    result = ((after_cross + matmul(hidden, w_down)) * valid).astype(BF)

    rows = width // parts
    table_rows = 2 * buckets // parts

    def wide(block):
        return block.reshape(-1, rows, width).transpose(1, 0, 2).reshape(1, rows, -1)

    return (
        result[None, None],
        states_grad[None, None],
        small_sum[None, :rows],
        small_sum[None, rows : 2 * rows],
        small_sum[2 * rows :].reshape(1, table_rows, 2 * heads),
        wide(last_sum[: 3 * rows]),
        wide(mid_sum[2 * rows :]),
        wide(mid_sum[rows : 2 * rows]),
        wide(last_sum[3 * rows :]),
        wide(mid_sum[:rows]),
        wide(up_sum),
        down_sum[None],
    )


def reduce_small(me, small):
    parts = small.shape[0]
    order = jnp.arange(parts) ^ me
    small = jnp.take(small, order, axis=0).reshape(parts // 4, 2, 2, -1)
    small = small[:, :, 0] + swapped(small[:, :, 1], PAGE, 1)
    small = small[:, 0] + swapped(small[:, 1], PAGE, 2)
    total = small[0]
    for step in range(1, parts // 4):
        total = total + swapped(small[step], PAGE, 4 * step)
    return total


def solution(mesh):
    placed = (
        P(STREAM, PAGE, None, None),
        P(None, PAGE),
        P(PAGE, None),
        P(PAGE, None),
        P(STREAM, None),
        P(STREAM, None),
        P(STREAM, None, None),
        P(STREAM, None, None),
        P(STREAM, None, None),
        P(STREAM, None, None),
        P(STREAM, None, None),
        P(STREAM, None, None),
        P(STREAM, None, None),
        P(STREAM, None, None),
        P(STREAM, PAGE, None, None),
    )
    return jax.shard_map(
        body,
        mesh=mesh,
        in_specs=placed,
        out_specs=(
            P(STREAM, PAGE, None, None),
            P(STREAM, PAGE, None, None),
            P(STREAM, PAGE),
            P(STREAM, PAGE),
            P(STREAM, PAGE, None),
            P(STREAM, PAGE, None),
            P(STREAM, PAGE, None),
            P(STREAM, PAGE, None),
            P(STREAM, PAGE, None),
            P(STREAM, PAGE, None),
            P(STREAM, PAGE, None),
            P(STREAM, PAGE, None),
        ),
        check_vma=False,
    )
```

```python
import functools
from typing import Any, NamedTuple

import jax
import jax.numpy as jnp
from jax import lax
from jax.experimental import pallas as pl
from jax.experimental.pallas import tpu as pltpu
from jax.sharding import PartitionSpec as P

GRID_SMALL = 16
GRID_LARGE = 24
EPSILON = 1e-05
MASKED = -1000000000.0
PAGE = "page"
STREAM = "stream"
BF = jnp.bfloat16
F32 = jnp.float32
WIDE = 128


def contract(left, right, left_dim, right_dim):
    return lax.dot_general(
        left, right, (((left_dim,), (right_dim,)), ((), ())), preferred_element_type=F32
    )


def params(mib=48):
    return pltpu.CompilerParams(vmem_limit_bytes=mib << 20)


def cost(us):
    return pl.CostEstimate(flops=int(us * 1.1e9), bytes_accessed=1 << 20, transcendentals=0)


def swapped(shard, axis, mask):
    return lax.ppermute(shard, axis, [(i, i ^ mask) for i in range(lax.axis_size(axis))])


def pieces(row):
    high = row.astype(BF).astype(F32)
    rest = row - high
    middle = rest.astype(BF).astype(F32)
    return high, middle, rest - middle


def extra_rows(rows, count):
    index = lax.broadcasted_iota(jnp.int32, (16, count), 0)
    block = jnp.zeros((16, count), F32)
    for place, row in enumerate(rows):
        block = jnp.where(index == place, row, block)
    return block.astype(BF)


def forward_pair(scale, queries, key_rows, values, mask, bias):
    count = queries.shape[0]
    half = WIDE // 2
    queries = (queries * scale).T
    key_rows = key_rows.T
    values = values.T
    ones = jnp.ones((1, count), F32)
    query_extra = extra_rows([ones], count)
    key_extra = extra_rows([mask], count)
    outs, logs = [], []
    for side in range(2):
        part = slice(half * side, half * side + half)
        if bias is not None:
            bands, onehot = bias
            band = contract(bands[side], onehot, 1, 0).astype(BF)
            left = jnp.concatenate([key_rows[part], onehot, key_extra], 0)
            right = jnp.concatenate([queries[part], band, query_extra], 0)
        else:
            left = jnp.concatenate([key_rows[part], key_extra], 0)
            right = jnp.concatenate([queries[part], query_extra], 0)
        scores = contract(left, right, 0, 0)
        top = jnp.max(scores, axis=0, keepdims=True)
        weights = jnp.exp(scores - top).astype(BF)
        output = contract(jnp.concatenate([values[part], query_extra], 0), weights, 1, 0)
        total = output[half : half + 1]
        outs.append(output[:half] * (1.0 / total))
        logs.append(top + jnp.log(total))
    return jnp.concatenate(outs, 0).astype(BF).T, jnp.concatenate(logs, 0)


def forward_kernel(has_bias, scale, *refs):
    q_ref, k_ref, v_ref, mask_ref = refs[:4]
    bias = (refs[4][...], refs[5][...]) if has_bias else None
    o_ref, lse_ref = refs[-2:]
    o_ref[...], lse_ref[0] = forward_pair(scale, q_ref[...], k_ref[...], v_ref[...], mask_ref[...], bias)


def backward_pair(scale, queries, key_rows, values, grad_out, output, lse, mask, bias):
    if bias is not None:
        bands, onehot, flipped = bias
    count = queries.shape[0]
    half = WIDE // 2
    queries = (queries * scale).T
    key_rows = key_rows.T
    values = values.T
    grad_out = grad_out.T
    product = grad_out.astype(F32) * output.T.astype(F32)
    ones = jnp.ones((1, count), F32)
    key_extra = extra_rows([ones, ones, ones, mask], count)
    value_extra = extra_rows([ones, ones, ones], count)
    d_queries, d_keys, d_values, d_bands = [], [], [], []
    for side in range(2):
        part = slice(half * side, half * side + half)
        lse_rows = extra_rows([*pieces(-lse[side : side + 1, :]), ones], count)
        delta = jnp.sum(product[part], axis=0, keepdims=True)
        delta_rows = extra_rows(list(pieces(-delta)), count)
        if bias is not None:
            band = contract(bands[side], onehot, 1, 0).astype(BF)
            left = jnp.concatenate([queries[part], band, lse_rows], 0)
            right = jnp.concatenate([key_rows[part], onehot, key_extra], 0)
        else:
            left = jnp.concatenate([queries[part], lse_rows], 0)
            right = jnp.concatenate([key_rows[part], key_extra], 0)
        weights = jnp.exp(contract(left, right, 0, 0))
        d_weights = contract(
            jnp.concatenate([grad_out[part], delta_rows], 0),
            jnp.concatenate([values[part], value_extra], 0),
            0,
            0,
        )
        d_scores = (weights * d_weights).astype(BF)
        d_values.append(contract(grad_out[part], weights.astype(BF), 1, 0))
        d_keys.append(contract(queries[part], d_scores, 1, 0))
        scaled = key_rows[part] * scale
        if bias is not None:
            both = contract(jnp.concatenate([scaled, flipped], 0), d_scores, 1, 1)
            d_queries.append(both[:half])
            d_bands.append(contract(onehot, both[half:].astype(BF), 1, 1))
        else:
            d_queries.append(contract(scaled, d_scores, 1, 1))
    out = tuple(jnp.concatenate(each, 0).astype(BF).T for each in (d_queries, d_keys, d_values))
    return out if bias is None else (*out, jnp.stack(d_bands))


def backward_kernel(has_bias, scale, *refs):
    q_ref, k_ref, v_ref, do_ref, o_ref, lse_ref, mask_ref = refs[:7]
    bias = tuple(ref[...] for ref in refs[7:10]) if has_bias else None
    outs = refs[10:] if has_bias else refs[7:]
    grads = backward_pair(
        scale, q_ref[...], k_ref[...], v_ref[...], do_ref[...], o_ref[...], lse_ref[0], mask_ref[...], bias
    )
    outs[0][...] = grads[0]
    outs[1][0] = grads[1]
    outs[1][1] = grads[2]
    if has_bias:
        outs[2][...] = grads[3]


def column(first):
    return lambda i: (0, first + i)


def attend_forward(query_rows, key_value_rows, first, mask, bias, scale, us):
    count = query_rows.shape[0]
    pairs = key_value_rows.shape[1] // WIDE // (3 if first else 2)
    block = lambda start: pl.BlockSpec((count, WIDE), column(start))
    row = pl.BlockSpec((1, count), lambda i: (0, 0))
    wide = pl.BlockSpec((WIDE, count), lambda i: (0, 0))
    specs = [block(0), block(first), block(first + pairs), row]
    operands = [query_rows, key_value_rows, key_value_rows, mask]
    if bias is not None:
        specs += [pl.BlockSpec((2, WIDE, WIDE), lambda i: (i, 0, 0)), wide]
        operands += [bias[0], bias[1]]
    return pl.pallas_call(
        functools.partial(forward_kernel, bias is not None, scale),
        grid=(pairs,),
        in_specs=specs,
        out_specs=[block(0), pl.BlockSpec((1, 2, count), lambda i: (i, 0, 0))],
        out_shape=[
            jax.ShapeDtypeStruct((count, pairs * WIDE), BF),
            jax.ShapeDtypeStruct((pairs, 2, count), F32),
        ],
        compiler_params=params(),
        cost_estimate=cost(us),
    )(*operands)


def attend_backward(query_rows, key_value_rows, first, grad_out, output, lse, mask, bias, scale, us):
    count = query_rows.shape[0]
    pairs = lse.shape[0]
    block = lambda start: pl.BlockSpec((count, WIDE), column(start))
    row = pl.BlockSpec((1, count), lambda i: (0, 0))
    wide = pl.BlockSpec((WIDE, count), lambda i: (0, 0))
    band = pl.BlockSpec((2, WIDE, WIDE), lambda i: (i, 0, 0))
    specs = [
        block(0),
        block(first),
        block(first + pairs),
        block(0),
        block(0),
        pl.BlockSpec((1, 2, count), lambda i: (i, 0, 0)),
        row,
    ]
    operands = [query_rows, key_value_rows, key_value_rows, grad_out, output, lse, mask]
    out_specs = [block(0), pl.BlockSpec((2, count, WIDE), lambda i: (0, 0, i))]
    out_shape = [
        jax.ShapeDtypeStruct((count, pairs * WIDE), BF),
        jax.ShapeDtypeStruct((2, count, pairs * WIDE), BF),
    ]
    if bias is not None:
        specs += [band, wide, wide]
        operands += list(bias)
        out_specs.append(band)
        out_shape.append(jax.ShapeDtypeStruct((2 * pairs, WIDE, WIDE), F32))
    return pl.pallas_call(
        functools.partial(backward_kernel, bias is not None, scale),
        grid=(pairs,),
        in_specs=specs,
        out_specs=out_specs,
        out_shape=out_shape,
        compiler_params=params(),
        cost_estimate=cost(us),
    )(*operands)


def same_block(shape):
    rows = lax.broadcasted_iota(jnp.int32, shape, 0) // (WIDE // 2)
    columns = lax.broadcasted_iota(jnp.int32, shape, 1) // (WIDE // 2)
    return rows == columns


def band_kernel(table_ref, band_ref):
    heads = band_ref.shape[0]
    shape = (WIDE, WIDE)
    keep = same_block(shape)
    lower = lax.broadcasted_iota(jnp.int32, shape, 0) >= WIDE // 2
    for head in range(heads):
        across = jnp.broadcast_to(table_ref[head : head + 1, :], shape)
        down = jnp.broadcast_to(table_ref[heads + head : heads + head + 1, :], shape)
        rolled = pltpu.roll(jnp.where(lower, down, across), WIDE // 2, 1, stride=1, stride_axis=0)
        band_ref[head] = jnp.where(keep, rolled, 0.0).astype(BF)


def make_bands(table):
    heads = table.shape[1] // 2
    return pl.pallas_call(
        band_kernel,
        out_shape=jax.ShapeDtypeStruct((heads, WIDE, WIDE), BF),
        compiler_params=params(),
        cost_estimate=cost(3),
    )(table.T)


def unband_kernel(grad_ref, table_ref):
    heads = grad_ref.shape[0]
    half = WIDE // 2
    shape = (WIDE, WIDE)
    keep = same_block(shape)
    for head in range(heads):
        rolled = pltpu.roll(jnp.where(keep, grad_ref[head], 0.0), 1, 1, stride=1, stride_axis=0)
        table_ref[head : head + 1, :] = jnp.sum(rolled[:half], axis=0, keepdims=True)
        table_ref[heads + head : heads + head + 1, :] = jnp.sum(rolled[half:], axis=0, keepdims=True)


def gather_bands(grads):
    heads = grads.shape[0]
    table = pl.pallas_call(
        unband_kernel,
        out_shape=jax.ShapeDtypeStruct((2 * heads, WIDE), F32),
        compiler_params=params(),
        cost_estimate=cost(3),
    )(grads)
    return table.T


def gelu_pair(value):
    density = jnp.exp(value * value * -0.5) * 0.3989422804014327
    t = 1.0 / (1.0 + 0.2316419 * jnp.abs(value))
    poly = t * (0.319381530 + t * (-0.356563782 + t * (1.781477937 + t * (-1.821255978 + t * 1.330274429))))
    tail = poly * density
    phi = jnp.where(value >= 0, 1.0 - tail, tail)
    return value * phi, phi + value * density


def feed_kernel(me_ref, second_ref, grad_ref, up_ref, down_ref, hidden_ref, d_up_ref, send_ref, keep_ref, sums_ref):
    tile = pl.program_id(0)
    grad = grad_ref[...]
    value = contract(second_ref[...], up_ref[...], 1, 0)
    hidden, slope = gelu_pair(value)
    hidden = hidden.astype(BF)
    hidden_ref[...] = hidden
    back = contract(grad, down_ref[...], 1, 1)
    d_up_ref[...] = (slope * back).astype(BF)
    sums_ref[...] = contract(hidden, grad, 0, 0)
    rows = send_ref.shape[1]
    per_tile = sums_ref.shape[0] // rows
    place_rows(me_ref[0], tile * per_tile, per_tile, rows, sums_ref, send_ref, keep_ref, 0)


def place_rows(me, first, number, rows, sums_ref, send_ref, keep_ref, offset):
    halves = send_ref.shape[0]
    quarters = halves // 2
    for local in range(number):
        relative = (first + local) ^ me
        slot = ((relative >> 1) & 1) * quarters + (relative >> 2)
        block = sums_ref[local * rows : local * rows + rows, :].astype(BF)

        @pl.when(relative & 1 == 1)
        def _():
            send_ref[slot, offset : offset + rows, :] = block

        @pl.when(relative & 1 == 0)
        def _():
            keep_ref[slot, offset : offset + rows, :] = block


def feed_forward(me, second, grad, w_up, w_down, parts):
    count, width = second.shape
    hidden_width = w_up.shape[1]
    rows = hidden_width // parts
    tiles = hidden_width // width
    whole = pl.BlockSpec((count, width), lambda i, me: (0, 0))
    tile = pl.BlockSpec((count, width), lambda i, me: (0, i))
    slots = pl.BlockSpec((parts // 2, rows, width), lambda i, me: (0, 0, 0))
    return pl.pallas_call(
        feed_kernel,
        grid_spec=pltpu.PrefetchScalarGridSpec(
            num_scalar_prefetch=1,
            grid=(tiles,),
            in_specs=[
                whole,
                whole,
                pl.BlockSpec((width, width), lambda i, me: (0, i)),
                pl.BlockSpec((width, width), lambda i, me: (i, 0)),
            ],
            out_specs=[tile, tile, slots, slots],
            scratch_shapes=[pltpu.VMEM((width, width), F32)],
        ),
        out_shape=[
            jax.ShapeDtypeStruct((count, hidden_width), BF),
            jax.ShapeDtypeStruct((count, hidden_width), BF),
            jax.ShapeDtypeStruct((parts // 2, rows, width), BF),
            jax.ShapeDtypeStruct((parts // 2, rows, width), BF),
        ],
        compiler_params=params(56),
        cost_estimate=cost(22),
    )(me, second, grad, w_up, w_down)


def outer_kernel(plan, rows, me_ref, *refs):
    tile = pl.program_id(0)
    lefts, rights = refs[: len(plan)], refs[len(plan) : 2 * len(plan)]
    send_ref, keep_ref, sums_ref = refs[2 * len(plan) :]
    number = 2 * send_ref.shape[0]
    first = 0
    for (tiles,), left_ref, right_ref in zip(plan, lefts, rights):
        for step in range(tiles):

            @pl.when(tile == first + step)
            def _(left_ref=left_ref, right_ref=right_ref, offset=(first + step) * rows):
                sums_ref[...] = contract(left_ref[...], right_ref[...], 0, 0)
                place_rows(me_ref[0], 0, number, rows, sums_ref, send_ref, keep_ref, offset)

        first += tiles


def outer_products(me, pairs, parts, us, extra=None):
    count, width = pairs[0][0].shape
    rows = width // parts
    plan, specs_left, specs_right = [], [], []
    first = 0
    for left, right in pairs:
        tiles = right.shape[1] // width
        plan.append((tiles,))
        specs_left.append(pl.BlockSpec((count, width), lambda i, me: (0, 0)))
        specs_right.append(
            pl.BlockSpec(
                (count, width),
                lambda i, me, first=first, tiles=tiles: (0, jnp.clip(i - first, 0, tiles - 1)),
            )
        )
        first += tiles
    slots = pl.BlockSpec((parts // 2, first * rows, width), lambda i, me: (0, 0, 0))
    shape = jax.ShapeDtypeStruct((parts // 2, first * rows, width), BF)
    return pl.pallas_call(
        functools.partial(outer_kernel, plan, rows),
        grid_spec=pltpu.PrefetchScalarGridSpec(
            num_scalar_prefetch=1,
            grid=(first,),
            in_specs=specs_left + specs_right,
            out_specs=[slots, slots],
            scratch_shapes=[pltpu.VMEM((width, width), F32)],
        ),
        out_shape=[shape, shape],
        compiler_params=params(56),
        cost_estimate=cost(us),
    )(me, *[left for left, _ in pairs], *[right for _, right in pairs])


def reduce_parts(send, keep):
    half = send.shape[0] // 2
    arrived = swapped(send, PAGE, 1).astype(F32)
    away = (arrived[half:] + keep[half:].astype(F32)).astype(BF)
    mine = arrived[:half] + keep[:half].astype(F32)
    mine = mine + swapped(away, PAGE, 2).astype(F32)
    total = mine[0]
    for step in range(1, half):
        total = total + swapped(mine[step].astype(BF), PAGE, 4 * step).astype(F32)
    return total


def flip(position, mask):
    out = position
    bit = 1
    while bit <= mask:
        if mask & bit:
            out = out + bit * (1 - 2 * lax.rem(lax.div(position, bit), 2))
        bit *= 2
    return out


RING = 2
STORES = 8
FETCHES = 14
LANDINGS = 3
LINK_US = 6.6
CORE_US = 1.7
LATE_US = 30.0
LATENCY_US = 4.5


CORE, NEAR, FAR, JOIN, LAST, DONE, Y, Z = range(8)
KV = 98
WEIGHTS = (96, 97)


class Flow:
    def __init__(self, refs, me, side):
        self.r = refs
        self.me = me
        self.side = side
        self.now = 0.0
        self.y_free = 0.0
        self.z_free = 0.0
        self.middle_free = 0.0
        self.pending = []
        self.near_done = {}
        self.stores = []

    def at(self, mask):
        return {PAGE: flip(self.me, mask)}

    def core_copy(self, unit):
        r = self.r
        return pltpu.make_async_remote_copy(
            src_ref=r.ring.at[unit % RING],
            dst_ref=r.core_in.at[unit % LANDINGS],
            send_sem=r.core_sent.at[unit % RING],
            recv_sem=r.core_got.at[unit % LANDINGS],
            device_id=self.at(1),
            device_id_type=pl.DeviceIdType.MESH,
        )

    def y_copy(self, unit):
        r = self.r
        if unit in TURNED_UNITS:
            source, landing = r.keep.at[unit, 1, 0], r.z_in.at[PLAIN_UNITS.index(unit), 2]
        else:
            source, landing = r.keep.at[unit, 1], r.y_in.at[Y_PLACES[unit]]
        return pltpu.make_async_remote_copy(
            src_ref=source,
            dst_ref=landing,
            send_sem=r.y_sent.at[int(unit in TURNED_UNITS)],
            recv_sem=r.y_got.at[Y_PLACES.get(unit, len(Y_PLACES))],
            device_id=self.at(2),
            device_id_type=pl.DeviceIdType.MESH,
        )

    def z_place(self, unit):
        if unit in PLAIN_UNITS:
            return PLAIN_UNITS.index(unit)
        return len(PLAIN_UNITS) + DOWN_STEPS[DOWN_UNITS.index(unit)] // 2

    def near_copy(self, unit, arriving=False):
        r = self.r
        if unit in DOWN_UNITS:
            step = DOWN_STEPS[DOWN_UNITS.index(unit)]
            if (step in NEAR_STEPS) == arriving:
                return None
            target = unit if arriving else DOWN_UNITS[DOWN_STEPS.index(step ^ 1)]
            source, landing = r.keep.at[unit], r.near_down.at[step // 2]
        elif unit in TURNED_UNITS:
            target = unit
            source = r.keep.at[unit, :, pl.ds(2, 2)]
            landing = r.turned_in.at[TURNED_UNITS.index(unit)]
        else:
            target = unit
            if unit in UP_UNITS and not arriving:
                target = UP_UNITS[DOWN_STEPS.index(DOWN_STEPS[UP_UNITS.index(unit)] ^ 1)]
            source = r.keep.at[unit, 0, pl.ds(2, 2)]
            landing = r.z_in.at[PLAIN_UNITS.index(target), pl.ds(0, 2)]
        return pltpu.make_async_remote_copy(
            src_ref=source,
            dst_ref=landing,
            send_sem=r.near_sent.at[int(unit in TURNED_UNITS)],
            recv_sem=r.near_got.at[self.z_place(target)],
            device_id=self.at(4),
            device_id_type=pl.DeviceIdType.MESH,
        )

    def far_copy(self, unit, arriving=False):
        r = self.r
        if unit in DOWN_UNITS:
            step = DOWN_STEPS[DOWN_UNITS.index(unit)]
            if step != (0 if arriving else 3):
                return None
            target = DOWN_UNITS[DOWN_STEPS.index(0)]
            source, landing = r.keep.at[unit, 0], r.far_down
        elif unit in TURNED_UNITS:
            target = unit
            source, landing = r.keep.at[unit, :, 1], r.z_in.at[PLAIN_UNITS.index(unit), pl.ds(0, 2)]
        else:
            target = unit
            if unit in UP_UNITS and not arriving:
                target = UP_UNITS[DOWN_STEPS.index(DOWN_STEPS[UP_UNITS.index(unit)] ^ 3)]
            source, landing = r.keep.at[unit, 0, 1], r.z_in.at[PLAIN_UNITS.index(target), 2]
        return pltpu.make_async_remote_copy(
            src_ref=source,
            dst_ref=landing,
            send_sem=r.far_sent.at[int(unit in TURNED_UNITS)],
            recv_sem=r.far_got.at[self.z_place(target)],
            device_id=self.at(12),
            device_id_type=pl.DeviceIdType.MESH,
        )

    def produce(self, unit, left, *rights):
        r = self.r
        first = 0
        for right in rights:
            last = first + right.shape[1]
            r.sums[:, first:last] = contract(left, right, 0, 0).astype(BF)
            first = last
        self.tick(1.2)
        if unit >= RING:
            self.core_copy(unit - RING).wait_send()
        core = lax.rem(self.me, 2)
        y = lax.rem(lax.div(self.me, 2), 2)
        z = lax.div(self.me, 4)
        for rel_y in range(2):
            for rel_z in range(4):
                y_at = flip(y, rel_y)
                if unit in DOWN_UNITS:
                    first = y_at * 8 * ROWS
                    mine = first + core * 4 * ROWS + rel_z * ROWS
                    other = first + (1 - core) * 4 * ROWS + rel_z * ROWS
                else:
                    first = flip(z, rel_z) * 4 * ROWS + y_at * 2 * ROWS
                    mine = first + core * ROWS
                    other = first + (1 - core) * ROWS
                slot = rel_y * 4 + (rel_z if unit in DOWN_UNITS else SLOT_OF[rel_z])
                r.ring[unit % RING, rel_y, slot - 4 * rel_y] = r.sums[pl.ds(pl.multiple_of(other, 16), ROWS), :]
                r.keep[unit, rel_y, slot - 4 * rel_y] = r.sums[pl.ds(pl.multiple_of(mine, 16), ROWS), :]
        if unit >= LANDINGS:
            pl.semaphore_wait(r.credit.at[unit - LANDINGS], 1)
        self.core_copy(unit).start()
        self.now += 0.5
        self.pending.append([unit, CORE, self.now + CORE_US])

    def advance(self, entry):
        self.plan(entry)()

    def near_busy(self, blocks):
        self.z_free = max(self.now, self.z_free) + blocks * LINK_US / 4
        return self.z_free + LATENCY_US

    def far_busy(self, blocks):
        self.z_free = max(self.now, self.z_free) + blocks * LINK_US / 4
        self.middle_free = max(self.now, self.middle_free) + blocks * LINK_US / 2
        return max(self.z_free, self.middle_free) + LATENCY_US

    def y_busy(self, us):
        self.y_free = max(self.now, self.y_free) + us
        return self.y_free + 0.3

    def plan(self, entry):
        unit, stage, _ = entry
        step = None
        if unit in WEIGHTS:
            if stage < 3:
                entry[1:] = [stage + 1, self.now + (3.8, 8.0, 2.5)[stage]]
            else:
                entry[1] = DONE
            return functools.partial(self.run, unit, stage)
        if unit in DOWN_UNITS:
            step = DOWN_STEPS[DOWN_UNITS.index(unit)]
        if unit == KV:
            entry[1] = DONE
        elif unit == SMALL:
            free = max(self.now, self.y_free if stage == CORE else self.z_free)
            following = {CORE: Y, Y: Z, Z: DONE}[stage]
            entry[1:] = [following, free + (1.0 if stage == CORE else 7.0)]
        elif unit in TURNED_UNITS:
            if stage == CORE:
                entry[1:] = [NEAR, self.near_busy(4)]
            elif stage == NEAR:
                entry[1:] = [FAR, self.far_busy(2)]
            elif stage == FAR:
                entry[1:] = [LAST, self.y_busy(LINK_US / 4) + LATE_US]
            else:
                entry[1] = DONE
        elif stage == CORE:
            if step in NEAR_STEPS:
                self.near_done[step ^ 1] = self.near_busy(8)
                entry[1] = DONE
            elif step is not None:
                entry[1:] = [JOIN, self.near_done[step]]
            else:
                entry[1:] = [Y, self.y_busy(LINK_US)]
        elif stage == JOIN:
            entry[1:] = [Y, self.y_busy(LINK_US)]
        elif stage == Y:
            if step is not None:
                done = self.far_busy(4) if step == 3 else self.z_free + LATE_US
                entry[1:] = [DONE, 0.0] if step == 3 else [FAR, done + LATE_US]
            else:
                entry[1:] = [NEAR, self.near_busy(2)]
                if unit in UP_UNITS:
                    self.meet(entry, [unit, UP_UNITS[DOWN_STEPS.index(DOWN_STEPS[UP_UNITS.index(unit)] ^ 1)]])
        elif stage == NEAR:
            entry[1:] = [FAR, self.far_busy(1) + (8.0 if unit in KV_UNITS else LATE_US)]
            if unit in UP_UNITS:
                self.meet(entry, UP_UNITS)
        else:
            entry[1] = DONE
            if unit == KV_UNITS[1]:
                self.pending.append([KV, CORE, self.now + LATE_US])
        return functools.partial(self.run, unit, stage)

    def meet(self, entry, units):
        due, entry[2] = entry[2], float("inf")
        waiting = [e for e in self.pending if e[0] in units and e[1] == entry[1]]
        if len(waiting) == len(units):
            for other in waiting:
                other[2] = due

    def join(self, unit, half, places, arrived):
        r = self.r
        for place in places:
            total = r.keep[unit, half, place].astype(F32) + arrived[place].astype(F32)
            r.keep[unit, half, place] = total.astype(BF)

    def run(self, unit, stage):
        r = self.r
        if unit in WEIGHTS:
            self.weight_arrival(WEIGHTS.index(unit), stage).wait_recv()
            if stage < 3:
                self.weight_copy(WEIGHTS.index(unit), stage + 1).start()
            return
        if unit == KV:
            self.kv_copy().wait_recv()
            self.store(KV)
            return
        if unit == SMALL:
            self.run_small((CORE, Y, Z).index(stage))
            return
        step = None
        if unit in DOWN_UNITS:
            step = DOWN_STEPS[DOWN_UNITS.index(unit)]
        turned = unit in TURNED_UNITS
        if stage == CORE:
            self.core_copy(unit).wait_recv()
            arrived = r.core_in.at[unit % LANDINGS]
            self.join(unit, 1, (0, 1, 2, 3), arrived.at[1])
            if step is None and not turned:
                self.y_copy(unit).start()
            self.join(unit, 0, (0, 1, 2, 3), arrived.at[0])
            if turned or step in NEAR_STEPS:
                self.near_copy(unit).start()
            if unit < UNITS - LANDINGS:
                pl.semaphore_signal(
                    r.credit.at[unit], 1, device_id=self.at(1), device_id_type=pl.DeviceIdType.MESH
                )
        elif stage == JOIN:
            self.near_copy(unit, arriving=True).wait_recv()
            arrived = r.near_down.at[step // 2]
            self.join(unit, 1, (0, 1, 2, 3), arrived.at[1])
            self.y_copy(unit).start()
            self.join(unit, 0, (0, 1, 2, 3), arrived.at[0])
        elif stage == Y:
            self.y_copy(unit).wait_recv()
            self.join(unit, 0, (2, 3, 0, 1), r.y_in.at[Y_PLACES[unit]])
            if step is None:
                self.near_copy(unit).start()
            elif step == 3:
                self.far_copy(unit).start()
        elif stage == NEAR:
            self.near_copy(unit, arriving=True).wait_recv()
            if turned:
                arrived = r.turned_in.at[TURNED_UNITS.index(unit)]
                for half in (0, 1):
                    self.join(unit, half, (1, 0), arrived.at[half])
            else:
                self.join(unit, 0, (1, 0), r.z_in.at[PLAIN_UNITS.index(unit)])
            self.far_copy(unit).start()
        elif turned and stage == FAR:
            self.far_copy(unit, arriving=True).wait_recv()
            arrived = r.z_in.at[PLAIN_UNITS.index(unit)]
            for half in (1, 0):
                total = r.keep[unit, half, 0].astype(F32) + arrived[half].astype(F32)
                r.keep[unit, half, 0] = total.astype(BF)
                if half:
                    self.y_copy(unit).start()
        elif turned:
            self.y_copy(unit).wait_recv()
            self.finish(unit)
        else:
            self.far_copy(unit, arriving=True).wait_recv()
            self.finish(unit)

    def small_copies(self, stage):
        r = self.r
        return [
            pltpu.make_async_remote_copy(
                src_ref=r.small_in.at[5 + stage],
                dst_ref=r.small_in.at[place],
                send_sem=r.small_sent.at[0],
                recv_sem=r.small_got.at[place],
                device_id=self.at(mask),
                device_id_type=pl.DeviceIdType.MESH,
            )
            for place, mask in SMALL_STEPS[stage]
        ]

    def kv_copy(self):
        r = self.r
        return pltpu.make_async_remote_copy(
            src_ref=r.kv_out,
            dst_ref=r.kv_in,
            send_sem=r.kv_sent.at[0],
            recv_sem=r.kv_got.at[0],
            device_id={STREAM: 1 - self.side},
            device_id_type=pl.DeviceIdType.MESH,
        )

    def weight_copy(self, half, stage):
        r = self.r
        core, y, z = lax.rem(self.me, 2), lax.rem(lax.div(self.me, 2), 2), lax.rem(lax.div(self.me, 4), 2)
        share = r.other_w.shape[-2]
        target, device = r.other_w.at[half, z, y, core], {STREAM: 1 - self.side}
        source = target
        if stage == 0:
            first = pl.multiple_of((z * 4 + y * 2 + core) * share, 16)
            source = r.w_ckv.at[pl.ds(first, share), half * WIDTH : (half + 1) * WIDTH]
        elif stage == 1:
            device = self.at(4)
        elif stage == 2:
            source = target = r.other_w.at[half, :, y, core]
            device = self.at(2)
        else:
            source = target = r.other_w.at[half, :, :, core]
            device = self.at(1)
        return pltpu.make_async_remote_copy(
            src_ref=source,
            dst_ref=target,
            send_sem=r.weight_sent.at[0],
            recv_sem=r.weight_got.at[half, stage],
            device_id=device,
            device_id_type=pl.DeviceIdType.MESH,
        )

    def weight_arrival(self, half, stage):
        r = self.r
        core, y, z = lax.rem(self.me, 2), lax.rem(lax.div(self.me, 2), 2), lax.rem(lax.div(self.me, 4), 2)
        target = (
            r.other_w.at[half, z, y, core],
            r.other_w.at[half, 1 - z, y, core],
            r.other_w.at[half, :, 1 - y, core],
            r.other_w.at[half, :, :, 1 - core],
        )[stage]
        return pltpu.make_async_remote_copy(
            src_ref=target,
            dst_ref=target,
            send_sem=r.weight_sent.at[0],
            recv_sem=r.weight_got.at[half, stage],
            device_id=self.at(1),
            device_id_type=pl.DeviceIdType.MESH,
        )

    def start_weights(self):
        for half in range(2):
            self.weight_copy(half, 0).start()
            self.pending.append([WEIGHTS[half], 0, self.now + 4.0 + 3.0 * half])

    def finish_weights(self):
        while True:
            left = [e for e in self.pending if e[0] in WEIGHTS]
            if not left:
                return
            entry = min(left, key=lambda e: e[2])
            self.now = max(self.now, entry[2])
            self.advance(entry)
            self.pending = [e for e in self.pending if e[1] != DONE]

    def start_small(self):
        r = self.r
        r.small_in[5] = r.small_sum[...]
        for copy in self.small_copies(0):
            copy.start()
        self.pending.append([SMALL, CORE, self.now + CORE_US + 1.0])

    def run_small(self, stage):
        r = self.r
        for copy in self.small_copies(stage):
            copy.wait_recv()
        for place, _ in SMALL_STEPS[stage]:
            r.small_sum[...] += r.small_in[place]
        if stage < 2:
            r.small_in[6 + stage] = r.small_sum[...]
            for copy in self.small_copies(stage + 1):
                copy.start()

    def due(self):
        while True:
            ready = [e for e in self.pending if e[2] <= self.now]
            if not ready:
                return
            entry = min(ready, key=lambda e: e[2])
            yield entry
            self.pending = [e for e in self.pending if e[1] != DONE]

    def tick(self, us):
        self.now += us
        for entry in self.due():
            self.advance(entry)

    def drain(self):
        while self.pending:
            self.now = max(self.now, min(e[2] for e in self.pending))
            for entry in self.due():
                self.advance(entry)
        for unit in range(UNITS - RING, UNITS):
            self.core_copy(unit).wait_send()
        r = self.r
        for whole, sent in (
            (r.y_in, r.y_sent),
            (r.s.at[pl.ds(0, 3), pl.ds(0, 608)], r.near_sent),
            (r.z_in.at[pl.ds(0, 5)], r.far_sent),
            (r.small_in.at[pl.ds(0, 5)], r.small_sent),
            (r.other_w, r.weight_sent),
            (r.s.at[Slot.normed], r.normed_sent),
        ):
            pltpu.make_async_copy(whole, whole, sent.at[0]).wait()
        for unit in TURNED_UNITS:
            for copy in (self.near_copy(unit), self.far_copy(unit), self.y_copy(unit)):
                copy.wait_send()
        self.kv_copy().wait_send()
        for place in range(max(0, len(self.stores) - STORES), len(self.stores)):
            self.store_copy(place).wait()

    def store_copy(self, place):
        r = self.r
        unit, part = self.stores[place]
        if unit == KV:
            pairs = [(r.kv_in, r.ckv_out)]
        elif unit in DOWN_UNITS:
            pairs = [(r.done.at[pl.ds(0, 4)], r.down_out)]
        elif unit in UP_UNITS:
            tile = flip(lax.div(self.me, 4), DOWN_STEPS[UP_UNITS.index(unit)])
            columns = pl.ds(pl.multiple_of(tile * WIDTH, WIDE), WIDTH)
            pairs = [(r.done.at[self.done_at(unit)], r.up_out.at[:, columns])]
        elif unit in THIRD_UNITS:
            third = WIDTH // 3
            first = third * THIRD_UNITS.index(unit)
            source = r.done.at[self.done_at(unit)]
            pairs = [
                (source.at[:, pl.ds(i * third, third)], r.qkv_out.at[:, pl.ds(i * WIDTH + first, third)])
                for i in range(3)
            ]
        else:
            pairs = [(r.done.at[self.done_at(unit)], {8: r.cout_out, 11: r.cq_out, 12: r.out_out}[unit])]
        return pltpu.make_async_copy(*pairs[part], r.stored_sums.at[place % STORES])

    def done_at(self, unit):
        return 4 + PLAIN_UNITS.index(unit)

    def store(self, unit):
        for part in range(3 if unit in THIRD_UNITS else 1):
            place = len(self.stores)
            if place >= STORES:
                self.store_copy(place - STORES).wait()
            self.stores.append((unit, part))
            self.store_copy(place).start()

    def finish(self, unit):
        r = self.r
        if unit in DOWN_UNITS:
            r.done[0:4] = r.keep[unit, 0].astype(F32) + r.far_down[...].astype(F32)
            self.store(unit)
            return
        total = r.keep[unit, 0, 0].astype(F32) + r.z_in[PLAIN_UNITS.index(unit), 2].astype(F32)
        if unit in KV_UNITS:
            half = KV_UNITS.index(unit)
            r.kv_out[:, half * WIDTH : (half + 1) * WIDTH] = total
            if half:
                self.kv_copy().start()
            return
        r.done[self.done_at(unit)] = total
        self.store(unit)


WIDTH = 768
ROWS = 48
DOWN_UNITS = (1, 3, 5, 7)
TURNED_UNITS = (13,)
UP_UNITS = (0, 2, 4, 6)
DOWN_STEPS = (1, 2, 3, 0)
NEAR_STEPS = (1, 2)
SLOT_OF = (0, 2, 3, 1)
PLAIN_UNITS = (0, 2, 4, 6, 8, 9, 10, 11, 12, 13, 14, 15)
UNITS = 16
Y_PLACES = {unit: at for at, unit in enumerate((0, 2, 4, 5, 6, 7, 8, 9, 10, 11, 12, 14, 15))}
KV_UNITS = (9, 10)
THIRD_UNITS = (13, 14, 15)


class Fetch:
    def __init__(self, source, target, semaphores, free):
        self.free = free
        self.place = free.pop(0)
        self.copy = pltpu.make_async_copy(source, target, semaphores.at[self.place])
        self.copy.start()

    def wait(self):
        self.copy.wait()
        self.free.append(self.place)


class Refs(NamedTuple):
    states: Any
    cotangent: Any
    w_qkv: Any
    w_out: Any
    w_cq: Any
    w_ckv: Any
    w_cout: Any
    w_up: Any
    w_down: Any
    counts: Any
    box_x: Any
    box_y: Any
    gain1: Any
    gain2: Any
    table_in: Any
    result_out: Any
    states_out: Any
    held_out: Any
    down_out: Any
    up_out: Any
    cout_out: Any
    cq_out: Any
    out_out: Any
    qkv_out: Any
    ckv_out: Any
    gain1_out: Any
    gain2_out: Any
    table_out: Any
    s: Any
    f: Any
    w: Any
    fetched: Any
    stored: Any
    sums: Any
    keep: Any
    ring: Any
    core_in: Any
    y_in: Any
    z_in: Any
    near_down: Any
    far_down: Any
    turned_in: Any
    core_sent: Any
    core_got: Any
    y_sent: Any
    y_got: Any
    near_sent: Any
    near_got: Any
    far_sent: Any
    far_got: Any
    credit: Any
    normed_sent: Any
    normed_got: Any
    back_sent: Any
    back_got: Any
    weight_sent: Any
    weight_got: Any
    other_w: Any
    done: Any
    stored_sums: Any
    kv_out: Any
    kv_in: Any
    kv_sent: Any
    kv_got: Any
    self_lse: Any
    cross_lse: Any
    bands: Any
    onehot: Any
    flipped: Any
    small_sum: Any
    table: Any
    gain_sums: Any
    table_sum: Any
    small_in: Any
    small_sent: Any
    small_got: Any
    d_bands: Any


INPUTS, SMALL_INPUTS, OUTPUTS, KEPT_OUTPUTS = 9, 6, 13, 0


def layer_kernel(scale, *refs):
    r = Refs(*refs)
    me = lax.axis_index(PAGE)
    side = lax.axis_index(STREAM)
    flow = Flow(r, me, side)
    count, width = r.states.shape
    pairs = width // WIDE
    half_rows = count // 2
    core, y, z = lax.rem(me, 2), lax.rem(lax.div(me, 2), 2), lax.div(me, 4)
    partner = {STREAM: 1 - side}

    free = list(range(FETCHES))

    def fetch(source, target):
        return Fetch(source, target, r.fetched, free)

    def slot(name):
        return r.s.at[name]

    def tile_of(step):
        return pl.ds(pl.multiple_of(flip(z, DOWN_STEPS[step]) * width, WIDE), width)

    def columns(ref, first):
        return ref.at[:, width * first : width * (first + 1)]

    got_states = fetch(r.states, slot(Slot.second))
    got_q, got_k, got_v = [fetch(columns(r.w_qkv, i), r.w.at[i]) for i in range(3)]
    got_out = fetch(r.w_out, r.w.at[3])
    got_cq = fetch(r.w_cq, r.w.at[4])
    got_grad = fetch(r.cotangent, slot(Slot.low_grad))

    barrier = pltpu.get_barrier_semaphore()
    others = [{PAGE: flip(me, mask)} for mask in (1, 2, 4, 8, 12)] + [partner]
    for other in others:
        pl.semaphore_signal(barrier, 1, device_id=other, device_id_type=pl.DeviceIdType.MESH)

    own_count, other_count = r.counts[side], r.counts[1 - side]
    slots_row = lax.broadcasted_iota(jnp.int32, (1, count), 1)
    mask_own = jnp.where(slots_row < own_count, 0.0, MASKED).astype(F32)
    mask_other = jnp.where(slots_row < other_count, 0.0, MASKED).astype(F32)
    slots_column = lax.broadcasted_iota(jnp.int32, (count, 1), 0)
    valid = jnp.where(slots_column < own_count, 1.0, 0.0).astype(F32)
    buckets = WIDE // 2
    small = own_count <= GRID_SMALL * GRID_SMALL
    tall = [jnp.floor((slots_row.astype(F32) + 0.5) * (1.0 / grid)).astype(jnp.int32) for grid in (GRID_SMALL, GRID_LARGE)]
    grid_top = jnp.where(small, tall[0], tall[1])
    grid_left = slots_row - jnp.where(small, tall[0] * GRID_SMALL, tall[1] * GRID_LARGE)
    left = jnp.where(side == 0, r.box_x[...], grid_left)
    top = jnp.where(side == 0, r.box_y[...], grid_top)
    index = lax.broadcasted_iota(jnp.int32, (buckets, count), 0)

    def marks(first, second):
        both = [jnp.where(index == first, 1.0, 0.0), jnp.where(index == second, 1.0, 0.0)]
        return jnp.concatenate(both, 0).astype(BF)

    r.onehot[...] = marks(left, top)
    r.flipped[...] = marks(buckets - 1 - left, buckets - 1 - top)
    keep = same_block((WIDE, WIDE))
    lower = lax.broadcasted_iota(jnp.int32, (WIDE, WIDE), 0) >= buckets
    heads = 2 * pairs
    for head in range(heads):
        across = jnp.broadcast_to(r.table_in[head : head + 1, :], (WIDE, WIDE))
        down = jnp.broadcast_to(r.table_in[heads + head : heads + head + 1, :], (WIDE, WIDE))
        rolled = pltpu.roll(jnp.where(lower, down, across), buckets, 1, stride=1, stride_axis=0)
        r.bands[head // 2, head % 2] = jnp.where(keep, rolled, 0.0).astype(BF)

    def normed_copy(part):
        rows = pl.ds(part * half_rows, half_rows)
        return pltpu.make_async_remote_copy(
            src_ref=slot(Slot.normed).at[rows],
            dst_ref=slot(Slot.other).at[rows],
            send_sem=r.normed_sent.at[0],
            recv_sem=r.normed_got.at[part],
            device_id=partner,
            device_id_type=pl.DeviceIdType.MESH,
        )

    got_states.wait()
    for part in range(2):
        rows = slice(part * half_rows, (part + 1) * half_rows)
        inputs = r.s[Slot.second, rows, :].astype(F32)
        r.f[2, rows, :] = inputs
        r.s[Slot.normed, rows, :] = norm_rows(inputs, r.gain1[...]).astype(BF)
    pl.semaphore_wait(barrier, len(others))

    flow.start_weights()
    for part in range(2):
        normed_copy(part).start()
    flow.tick(0.1)
    for name, copy, at in ((Slot.query, got_q, 0), (Slot.key, got_k, 1), (Slot.value, got_v, 2)):
        copy.wait()
        slot(name)[...] = contract(slot(Slot.normed)[...], r.w[at], 1, 0).astype(BF)
        flow.tick(1.0)
    held = [pltpu.make_async_copy(slot(name), r.held_out.at[i], r.stored.at[2 + i]) for i, name in enumerate((Slot.query, Slot.key, Slot.value))]
    for copy in held:
        copy.start()
    got_cout = fetch(r.w_cout, r.w.at[0])
    got_down = [fetch(r.w_down.at[tile_of(step)], r.w.at[1 + step]) for step in range(2)]

    def pair_loop(us, step, first=0, last=pairs):
        events = []
        for pair in range(first, last):
            flow.now += us
            events.append([])
            for entry in flow.due():
                events[-1].append(flow.plan(entry))

        @pl.loop(first, last)
        def _(pair):
            step(pair)
            for place, steps in enumerate(events, first):
                if steps:

                    @pl.when(pair == place)
                    def _(steps=steps):
                        for run in steps:
                            run()

    def lanes_of(pair):
        return pl.ds(pl.multiple_of(pair * WIDE, WIDE), WIDE)

    def self_forward(pair):
        lanes = lanes_of(pair)
        output, lse = forward_pair(
            scale,
            r.s[Slot.query, :, lanes],
            r.s[Slot.key, :, lanes],
            r.s[Slot.value, :, lanes],
            mask_own,
            (r.bands[pair], r.onehot[...]),
        )
        r.s[Slot.attended, :, lanes] = output
        r.self_lse[pair] = lse

    pair_loop(1.95, self_forward)

    got_out.wait()
    r.f[2] = r.f[2] + contract(slot(Slot.attended)[...], r.w[3], 1, 0)
    slot(Slot.low_middle)[...] = r.f[2].astype(BF)
    got_down.append(fetch(r.w_down.at[tile_of(2)], r.w.at[3]))
    got_cq.wait()
    slot(Slot.cross_query)[...] = contract(slot(Slot.low_middle)[...], r.w[4], 1, 0).astype(BF)
    got_down.append(fetch(r.w_down.at[tile_of(3)], r.w.at[4]))
    flow.tick(2.2)
    got_grad.wait()
    slot(Slot.low_grad)[...] = (slot(Slot.low_grad)[...].astype(F32) * valid).astype(BF)
    flow.tick(0.5)

    back_slots = (Slot.back0, Slot.back1, Slot.back2, Slot.back3)
    hidden_slots = (Slot.query, Slot.key, Slot.value, Slot.hidden3)
    got_up = []
    for step in range(4):
        got_down[step].wait()
        r.s[back_slots[step]] = contract(slot(Slot.low_grad)[...], r.w[1 + step], 1, 1).astype(BF)
        got_up.append(fetch(r.w_up.at[:, tile_of(step)], r.w.at[1 + step]))
        flow.tick(1.05)
    flow.finish_weights()
    for copy in held:
        copy.wait()
    for part in range(2):
        normed_copy(part).wait_recv()
    flow.now = max(flow.now, 30.0)
    for at, name in enumerate((Slot.cross_key, Slot.cross_value)):
        slot(name)[...] = contract(slot(Slot.other)[...], r.other_w[at].reshape(width, width), 1, 0).astype(BF)
    flow.tick(2.0)

    def cross_forward(pair):
        lanes = lanes_of(pair)
        output, lse = forward_pair(
            scale,
            r.s[Slot.cross_query, :, lanes],
            r.s[Slot.cross_key, :, lanes],
            r.s[Slot.cross_value, :, lanes],
            mask_other,
            None,
        )
        r.s[Slot.crossed, :, lanes] = output
        r.cross_lse[pair] = lse

    pair_loop(1.8, cross_forward)
    got_cout.wait()
    r.f[2] = r.f[2] + contract(slot(Slot.crossed)[...], r.w[0], 1, 0)
    for part in range(2):
        rows = slice(part * half_rows, (part + 1) * half_rows)
        r.s[Slot.second, rows, :] = norm_rows(r.f[2, rows, :], r.gain2[...]).astype(BF)
    flow.tick(2.0)

    second_at, grad_at = Slot.second, Slot.low_grad
    for step in range(4):
        hidden_at, d_up_at, up_at = hidden_slots[step], back_slots[step], 1 + step
        got_up[step].wait()

        for part in range(4):
            rows = slice(part * (count // 4), (part + 1) * (count // 4))
            hidden, slope = gelu_pair(contract(r.s[second_at, rows, :], r.w[up_at], 1, 0))
            r.s[hidden_at, rows, :] = hidden.astype(BF)
            r.s[d_up_at, rows, :] = (slope * r.s[d_up_at, rows, :].astype(F32)).astype(BF)

        flow.tick(2.0)
        flow.produce(UP_UNITS[step], r.s[second_at], r.s[d_up_at])
        flow.tick(0.1)
        flow.produce(DOWN_UNITS[step], r.s[hidden_at], r.s[grad_at])
        flow.tick(0.2)
    for step in range(4):
        for part in range(2):
            rows = slice(part * half_rows, (part + 1) * half_rows)
            back = contract(r.s[back_slots[step], rows, :], r.w[1 + step], 1, 1)
            r.f[0, rows, :] = back if step == 0 else r.f[0, rows, :] + back
        flow.tick(1.2)
    got_cq, got_out = fetch(r.w_cq, r.w.at[1]), fetch(r.w_out, r.w.at[2])
    got_q, got_k = [fetch(columns(r.w_qkv, i), r.w.at[3 + i]) for i in range(2)]

    low_after_at, d_crossed_at = Slot.back0, Slot.second
    r.small_sum[6:12, :] = fold(norm_back(r.f.at[2], r.f, 0, r.gain2, r.s, grad_at, low_after_at))
    flow.tick(1.7)
    r.s[d_crossed_at] = contract(r.s[low_after_at], r.w[0], 1, 1).astype(BF)
    got_v = fetch(columns(r.w_qkv, 2), r.w.at[0])
    flow.tick(1.1)
    flow.produce(8, slot(Slot.crossed)[...], r.s[low_after_at])
    flow.tick(0.1)

    d_query_at, d_key_at, d_value_at = Slot.back1, Slot.low_grad, Slot.d_value

    def cross_backward(pair):
        lanes = lanes_of(pair)
        d_query, d_key, d_value = backward_pair(
            scale,
            r.s[Slot.cross_query, :, lanes],
            r.s[Slot.cross_key, :, lanes],
            r.s[Slot.cross_value, :, lanes],
            r.s[d_crossed_at, :, lanes],
            r.s[Slot.crossed, :, lanes],
            r.cross_lse[pair],
            mask_other,
            None,
        )
        r.s[d_query_at, :, lanes] = d_query
        r.s[d_key_at, :, lanes] = d_key
        r.s[d_value_at, :, lanes] = d_value

    pair_loop(2.45, cross_backward)

    flow.produce(9, slot(Slot.other)[...], r.s[d_key_at])
    flow.tick(0.1)
    flow.produce(10, slot(Slot.other)[...], r.s[d_value_at])
    flow.tick(0.1)
    back_at = Slot.crossed
    r.s[back_at] = (
        contract(r.s[d_key_at], r.other_w[0].reshape(width, width), 1, 1)
        + contract(r.s[d_value_at], r.other_w[1].reshape(width, width), 1, 1)
    ).astype(BF)
    back_copy = pltpu.make_async_remote_copy(
        src_ref=r.s.at[back_at],
        dst_ref=slot(Slot.returned),
        send_sem=r.back_sent.at[0],
        recv_sem=r.back_got.at[0],
        device_id=partner,
        device_id_type=pl.DeviceIdType.MESH,
    )
    back_copy.start()
    flow.tick(2.0)
    got_states = fetch(r.states, r.s.at[d_key_at])

    query_at, key_at, value_at = Slot.back3, Slot.back0, Slot.d_value
    got_held = [fetch(r.held_out.at[i], r.s.at[at]) for i, at in enumerate((query_at, key_at, value_at))]

    flow.produce(11, slot(Slot.low_middle)[...], r.s[d_query_at])
    got_cq.wait()
    r.f[0] = r.f[0] + contract(r.s[d_query_at], r.w[1], 1, 1)
    d_middle_at, d_attended_at = Slot.cross_key, Slot.cross_value
    r.s[d_middle_at] = r.f[0].astype(BF)
    flow.tick(1.5)
    flow.produce(12, slot(Slot.attended)[...], r.s[d_middle_at])
    got_out.wait()
    r.s[d_attended_at] = contract(r.s[d_middle_at], r.w[2], 1, 1).astype(BF)
    got_down = [fetch(r.w_down.at[tile_of(step)], r.w.at[1 + step]) for step in range(2)]
    flow.tick(1.2)

    dq_at, dk_at, dv_at = Slot.cross_query, Slot.back2, Slot.second
    for copy in got_held:
        copy.wait()

    def self_backward(pair):
        lanes = lanes_of(pair)
        d_query, d_key, d_value, d_bands = backward_pair(
            scale,
            r.s[query_at, :, lanes],
            r.s[key_at, :, lanes],
            r.s[value_at, :, lanes],
            r.s[d_attended_at, :, lanes],
            r.s[Slot.attended, :, lanes],
            r.self_lse[pair],
            mask_own,
            (r.bands[pair], r.onehot[...], r.flipped[...]),
        )
        r.s[dq_at, :, lanes] = d_query
        r.s[dk_at, :, lanes] = d_key
        r.s[dv_at, :, lanes] = d_value
        r.d_bands[pair] = d_bands

    third = width // 3
    normed_at = Slot.normed
    for part in range(3):
        pair_loop(3.2, self_backward, part * pairs // 3, (part + 1) * pairs // 3)
        wanted = slice(part * third, (part + 1) * third)
        flow.produce(13 + part, r.s[normed_at], r.s[dq_at, :, wanted], r.s[dk_at, :, wanted], r.s[dv_at, :, wanted])
    for copy in (got_q, got_k, got_v):
        copy.wait()
    r.f[1] = (
        contract(r.s[dq_at], r.w[3], 1, 1)
        + contract(r.s[dk_at], r.w[4], 1, 1)
        + contract(r.s[dv_at], r.w[0], 1, 1)
    )
    got_down += [fetch(r.w_down.at[tile_of(step)], r.w.at[1 + step]) for step in range(2, 4)]
    flow.tick(3.2)
    for head in range(heads):
        across, down = unband(r.d_bands[head // 2, head % 2])
        r.small_sum[16 + head : 17 + head, :] = across
        r.small_sum[16 + heads + head : 17 + heads + head, :] = down
    flow.tick(1.0)
    got_states.wait()
    back_copy.wait_recv()
    for part in range(2):
        rows = slice(part * half_rows, (part + 1) * half_rows)
        r.f[1, rows, :] += r.s[Slot.returned, rows, :].astype(F32)
    gain1_grad = norm_back(r.s.at[d_key_at], r.f, 1, r.gain1, None, None, None)
    sent_states = pltpu.make_async_copy(r.f.at[0], r.states_out, r.stored.at[1])
    sent_states.start()
    r.small_sum[0:6, :] = fold(gain1_grad)
    r.small_sum[12:16, :] = jnp.zeros((4, WIDE), F32)
    flow.tick(2.0)

    flow.start_small()
    flow.tick(0.2)

    result_at = Slot.back3
    for step in range(4):
        got_down[step].wait()
        r.f[2] = r.f[2] + contract(r.s[hidden_slots[step]], r.w[1 + step], 1, 0)
        flow.tick(1.3)
    r.s[result_at] = (r.f[2] * valid).astype(BF)
    sent_result = pltpu.make_async_copy(r.s.at[result_at], r.result_out, r.stored.at[0])
    sent_result.start()
    flow.tick(0.4)
    flow.drain()
    gains = r.small_sum[...]
    shift = width - me * ROWS
    for place in range(2):
        row = jnp.concatenate([gains[6 * place + i : 6 * place + i + 1] for i in range(width // WIDE)], 1)
        r.gain_sums[place] = pltpu.roll(row, lax.rem(shift, width), 1)[:, :ROWS]
    flat = jnp.concatenate([gains[16:], jnp.zeros((WIDE - 2 * heads, WIDE), F32)], 0)
    r.table[...] = flat.T
    table_rows = r.table_out.shape[0]
    r.table_sum[...] = r.table[pl.ds(pl.multiple_of(me * table_rows, 8), table_rows), 0 : 2 * heads]
    last = [
        pltpu.make_async_copy(source, target, r.stored.at[5 + i])
        for i, (source, target) in enumerate(
            ((r.gain_sums.at[0], r.gain1_out), (r.gain_sums.at[1], r.gain2_out), (r.table_sum, r.table_out))
        )
    ]
    for copy in last:
        copy.start()
    for copy in last:
        copy.wait()
    back_copy.wait_send()
    sent_result.wait()
    sent_states.wait()


class Slot:
    (
        normed,
        other,
        query,
        key,
        value,
        attended,
        low_middle,
        cross_query,
        cross_key,
        cross_value,
        crossed,
        second,
        low_grad,
        hidden3,
        back0,
        back1,
        back2,
        back3,
        d_value,
        returned,
    ) = range(20)


SMALL = 99
SMALL_STEPS = (((0, 1),), ((1, 2),), ((2, 4), (3, 8), (4, 12)))


def fold(row):
    return jnp.concatenate([row[:, WIDE * i : WIDE * (i + 1)] for i in range(row.shape[1] // WIDE)], 0)


def norm_back(source, f, grad_at, gain, s, s_grad_at, s_out_at):
    count = f.shape[1]
    chunk = count // 4
    gain_grad = jnp.zeros((1, f.shape[2]), F32)
    for part in range(4):
        rows = slice(part * chunk, (part + 1) * chunk)
        inputs = source[rows, :].astype(F32)
        grad = f[grad_at, rows, :]
        centre = inputs - jnp.mean(inputs, axis=-1, keepdims=True)
        spread = lax.rsqrt(jnp.mean(centre * centre, axis=-1, keepdims=True) + EPSILON)
        normed = centre * spread
        gain_grad = gain_grad + jnp.sum(grad * normed, axis=0, keepdims=True)
        scaled = grad * gain[...]
        back = spread * (
            scaled
            - jnp.mean(scaled, axis=-1, keepdims=True)
            - normed * jnp.mean(scaled * normed, axis=-1, keepdims=True)
        )
        if s is not None:
            total = s[s_grad_at, rows, :].astype(F32) + back
            s[s_out_at, rows, :] = total.astype(BF)
        else:
            total = f[0, rows, :] + back
        f[0, rows, :] = total
    return gain_grad


def unband(grad):
    half = WIDE // 2
    rolled = pltpu.roll(jnp.where(same_block((WIDE, WIDE)), grad, 0.0), 1, 1, stride=1, stride_axis=0)
    return jnp.sum(rolled[:half], axis=0, keepdims=True), jnp.sum(rolled[half:], axis=0, keepdims=True)


def deliver_kernel(*refs):
    number = (len(refs) - 2) // 3
    sources, targets, held = refs[:number], refs[number : 2 * number], refs[2 * number : 3 * number]
    came, went = refs[-2:]
    arrivals = [pltpu.make_async_copy(sources[i], held[i], came.at[i]) for i in range(number)]
    departures = [pltpu.make_async_copy(held[i], targets[i], went.at[i]) for i in range(number)]
    for copy in arrivals:
        copy.start()
    for arrival, departure in zip(arrivals, departures):
        arrival.wait()
        departure.start()
    for copy in departures:
        copy.wait()


def deliver(arrays):
    anywhere = pl.BlockSpec(memory_space=pl.ANY)
    return pl.pallas_call(
        deliver_kernel,
        in_specs=[anywhere] * len(arrays),
        out_specs=[anywhere] * len(arrays),
        out_shape=[jax.ShapeDtypeStruct(array.shape, array.dtype) for array in arrays],
        scratch_shapes=[pltpu.VMEM(array.shape, array.dtype) for array in arrays]
        + [pltpu.SemaphoreType.DMA((len(arrays),))] * 2,
        compiler_params=params(63),
        cost_estimate=cost(3),
    )(*arrays)


def whole_layer(operands, scale):
    count, width = operands[0].shape
    hidden_width = operands[7].shape[1]
    heads = operands[-1].shape[0] // 2
    pairs = heads // 2
    rows = width // 16
    outs = [
        jax.ShapeDtypeStruct((count, width), BF),
        jax.ShapeDtypeStruct((count, width), F32),
        jax.ShapeDtypeStruct((3, count, width), BF),
        jax.ShapeDtypeStruct((4, rows, width), F32),
        jax.ShapeDtypeStruct((rows, hidden_width), F32),
        jax.ShapeDtypeStruct((rows, width), F32),
        jax.ShapeDtypeStruct((rows, width), F32),
        jax.ShapeDtypeStruct((rows, width), F32),
        jax.ShapeDtypeStruct((rows, 3 * width), F32),
        jax.ShapeDtypeStruct((rows, 2 * width), F32),
        jax.ShapeDtypeStruct((1, rows), F32),
        jax.ShapeDtypeStruct((1, rows), F32),
        jax.ShapeDtypeStruct((WIDE // 16, 2 * heads), F32),
    ]
    anywhere = pl.BlockSpec(memory_space=pl.ANY)
    inside = pl.BlockSpec(memory_space=pltpu.VMEM)
    scalars = pl.BlockSpec(memory_space=pltpu.SMEM)
    dma = pltpu.SemaphoreType.DMA
    small = (16 + 2 * heads, WIDE)
    scratch = [
        pltpu.VMEM((20, count, width), BF),
        pltpu.VMEM((3, count, width), F32),
        pltpu.VMEM((5, width, width), BF),
        dma((FETCHES,)),
        dma((8,)),
        pltpu.VMEM((width, width), BF),
        pltpu.VMEM((UNITS, 2, 4, rows, width), BF),
        pltpu.VMEM((RING, 2, 4, rows, width), BF),
        pltpu.VMEM((LANDINGS, 2, 4, rows, width), BF),
        pltpu.VMEM((len(Y_PLACES), 4, rows, width), BF),
        pltpu.VMEM((len(PLAIN_UNITS), 3, rows, width), BF),
        pltpu.VMEM((2, 2, 4, rows, width), BF),
        pltpu.VMEM((4, rows, width), BF),
        pltpu.VMEM((max(1, len(TURNED_UNITS)), 2, 2, 16 if not TURNED_UNITS else rows, width), BF),
        dma((RING,)),
        dma((LANDINGS,)),
        dma((2,)),
        dma((len(Y_PLACES) + 1,)),
        dma((2,)),
        dma((len(PLAIN_UNITS) + 2,)),
        dma((2,)),
        dma((len(PLAIN_UNITS) + 1,)),
        pltpu.SemaphoreType.REGULAR((UNITS - LANDINGS,)),
        dma((1,)),
        dma((2,)),
        dma((1,)),
        dma((1,)),
        dma((1,)),
        dma((2, 4)),
        pltpu.VMEM((2, 2, 2, 2, width // 8, width), BF),
        pltpu.VMEM((4 + len(PLAIN_UNITS), rows, width), F32),
        dma((STORES,)),
        pltpu.VMEM((rows, 2 * width), F32),
        pltpu.VMEM((rows, 2 * width), F32),
        dma((1,)),
        dma((1,)),
        pltpu.VMEM((pairs, 2, count), F32),
        pltpu.VMEM((pairs, 2, count), F32),
        pltpu.VMEM((pairs, 2, WIDE, WIDE), BF),
        pltpu.VMEM((WIDE, count), BF),
        pltpu.VMEM((WIDE, count), BF),
        pltpu.VMEM(small, F32),
        pltpu.VMEM((WIDE, WIDE), F32),
        pltpu.VMEM((2, 1, rows), F32),
        pltpu.VMEM((WIDE // 16, 2 * heads), F32),
        pltpu.VMEM((8, *small), F32),
        dma((1,)),
        dma((5,)),
        pltpu.VMEM((pairs, 2, WIDE, WIDE), F32),
    ]
    outputs = pl.pallas_call(
        functools.partial(layer_kernel, scale),
        in_specs=[anywhere] * INPUTS + [scalars] + [inside] * (SMALL_INPUTS - 1),
        out_specs=[anywhere] * OUTPUTS + [inside] * KEPT_OUTPUTS,
        out_shape=outs,
        scratch_shapes=scratch,
        compiler_params=pltpu.CompilerParams(
            collective_id=0, has_side_effects=True, vmem_limit_bytes=(64 << 20) - (256 << 10)
        ),
        cost_estimate=cost(150),
    )(*operands)
    down = outputs[3].reshape(4 * rows, width)
    return [*outputs[:2], down, *outputs[4:]]


def norm_rows(inputs, gain_row):
    centre = inputs - jnp.mean(inputs, axis=-1, keepdims=True)
    spread = jnp.mean(centre * centre, axis=-1, keepdims=True)
    return centre * lax.rsqrt(spread + EPSILON) * gain_row


def matmul(left, right):
    return contract(left, right, 1, 0)


def matmul_back(left, weight):
    return contract(left, weight, 1, 1)


def onehots(left, top, buckets):
    index = jnp.arange(buckets)[:, None]
    return jnp.concatenate([left[None, :] == index, top[None, :] == index], 0).astype(BF)


def body(
    states,
    counts,
    box_x,
    box_y,
    ln1_gain,
    ln2_gain,
    box_table,
    w_qkv,
    w_out,
    w_cq,
    w_ckv,
    w_cout,
    w_up,
    w_down,
    cotangent,
):
    slot_count, width = states.shape[2], states.shape[3]
    heads = box_table.shape[2] // 2
    buckets = box_table.shape[1] // 2
    scale = (width // heads) ** (-0.5)
    pairs = heads // 2
    parts = lax.axis_size(PAGE)
    side = lax.axis_index(STREAM)
    me = lax.axis_index(PAGE).astype(jnp.int32).reshape(1)
    own_count = jnp.take(counts[:, 0], side)
    other_count = jnp.take(counts[:, 0], 1 - side)
    slots = jnp.arange(slot_count)
    grid_side = jnp.where(own_count > GRID_SMALL * GRID_SMALL, GRID_LARGE, GRID_SMALL)
    left = jnp.where(side == 0, box_x[0], slots % grid_side)
    top = jnp.where(side == 0, box_y[0], slots // grid_side)
    onehot = onehots(left, top, buckets)
    flipped = onehots(buckets - 1 - left, buckets - 1 - top, buckets)
    mask_own = jnp.where(slots < own_count, 0.0, MASKED).astype(F32)[None]
    mask_other = jnp.where(slots < other_count, 0.0, MASKED).astype(F32)[None]
    valid = (slots < own_count).astype(F32)[:, None]
    bands = make_bands(box_table[0])
    weights = [w[0] for w in (w_qkv, w_out, w_cq, w_ckv, w_cout, w_up, w_down)]
    w_qkv, w_out, w_cq, w_ckv, w_cout, w_up, w_down = weights

    if parts == 16 and width == WIDTH and w_up.shape[1] == 4 * width:
        operands = [
            states[0, 0],
            cotangent[0, 0],
            w_qkv,
            w_out,
            w_cq,
            w_ckv,
            w_cout,
            w_up,
            w_down,
            counts[:, 0],
            box_x,
            box_y,
            ln1_gain,
            ln2_gain,
            box_table[0].T,
        ]
        result, states_grad, down, up, cout, cq, out, qkv, ckv, gain1, gain2, table = deliver(
            whole_layer(operands, scale)
        )
        return (
            result[None, None],
            states_grad[None, None],
            gain1,
            gain2,
            table[None],
            qkv[None],
            out[None],
            cq[None],
            ckv[None],
            cout[None],
            up[None],
            down[None],
        )

    inputs = states[0, 0].astype(F32)
    normed, norm_pull = jax.vjp(norm_rows, inputs, ln1_gain[0])
    normed = normed.astype(BF)
    cross_kv = matmul(normed, w_ckv).astype(BF)
    partner = swapped(cross_kv, STREAM, 1)
    joined = matmul(normed, w_qkv).astype(BF)
    attended, self_lse = attend_forward(joined, joined, pairs, mask_own, (bands, onehot), scale, 18)
    middle = inputs + matmul(attended, w_out)
    low_middle = middle.astype(BF)
    cross_query = matmul(low_middle, w_cq).astype(BF)
    crossed, cross_lse = attend_forward(cross_query, partner, 0, mask_other, None, scale, 16)
    after_cross = middle + matmul(crossed, w_cout)
    second, second_pull = jax.vjp(norm_rows, after_cross, ln2_gain[0])
    second = second.astype(BF)
    out_grad = cotangent[0, 0].astype(F32) * valid
    low_grad = out_grad.astype(BF)
    hidden, d_up, *down_parts = feed_forward(me, second, low_grad, w_up, w_down, parts)
    down_sum = reduce_parts(*down_parts)
    up_sum = reduce_parts(*outer_products(me, [(second, d_up)], parts, 6))
    d_after, ln2_grad = second_pull(matmul_back(d_up, w_up))
    d_after = d_after + out_grad
    low_after = d_after.astype(BF)
    d_crossed = matmul_back(low_after, w_cout).astype(BF)
    d_cross_query, d_partner = attend_backward(
        cross_query, partner, 0, d_crossed, crossed, cross_lse, mask_other, None, scale, 26
    )
    returned = swapped(d_partner, STREAM, 1)
    d_middle = d_after + matmul_back(d_cross_query, w_cq)
    low_d_middle = d_middle.astype(BF)
    d_attended = matmul_back(low_d_middle, w_out).astype(BF)
    mid_sum = reduce_parts(
        *outer_products(
            me, [(crossed, low_after), (low_middle, d_cross_query), (attended, low_d_middle)], parts, 6
        )
    )
    d_query, d_pair, d_bands = attend_backward(
        joined, joined, pairs, d_attended, attended, self_lse, mask_own, (bands, onehot, flipped), scale, 29
    )
    table_grad = gather_bands(d_bands)
    d_normed = (
        matmul_back(d_query, w_qkv[:, :width])
        + matmul_back(d_pair[0], w_qkv[:, width : 2 * width])
        + matmul_back(d_pair[1], w_qkv[:, 2 * width :])
        + matmul_back(returned[0], w_ckv[:, :width])
        + matmul_back(returned[1], w_ckv[:, width:])
    )
    d_inputs, ln1_grad = norm_pull(d_normed)
    states_grad = d_inputs + d_middle
    last_send, last_keep = outer_products(
        me,
        [
            (normed, d_query),
            (normed, d_pair[0]),
            (normed, d_pair[1]),
            (normed, returned[0]),
            (normed, returned[1]),
        ],
        parts,
        10,
    )
    last_sum = reduce_parts(last_send, last_keep)
    small = jnp.concatenate(
        [ln1_grad.reshape(parts, -1), ln2_grad.reshape(parts, -1), table_grad.reshape(parts, -1)], 1
    )
    small_sum = reduce_small(me[0], small)
    result = ((after_cross + matmul(hidden, w_down)) * valid).astype(BF)

    rows = width // parts
    table_rows = 2 * buckets // parts

    def wide(block):
        return block.reshape(-1, rows, width).transpose(1, 0, 2).reshape(1, rows, -1)

    return (
        result[None, None],
        states_grad[None, None],
        small_sum[None, :rows],
        small_sum[None, rows : 2 * rows],
        small_sum[2 * rows :].reshape(1, table_rows, 2 * heads),
        wide(last_sum[: 3 * rows]),
        wide(mid_sum[2 * rows :]),
        wide(mid_sum[rows : 2 * rows]),
        wide(last_sum[3 * rows :]),
        wide(mid_sum[:rows]),
        wide(up_sum),
        down_sum[None],
    )


def reduce_small(me, small):
    parts = small.shape[0]
    order = jnp.arange(parts) ^ me
    small = jnp.take(small, order, axis=0).reshape(parts // 4, 2, 2, -1)
    small = small[:, :, 0] + swapped(small[:, :, 1], PAGE, 1)
    small = small[:, 0] + swapped(small[:, 1], PAGE, 2)
    total = small[0]
    for step in range(1, parts // 4):
        total = total + swapped(small[step], PAGE, 4 * step)
    return total


def solution(mesh):
    placed = (
        P(STREAM, PAGE, None, None),
        P(None, PAGE),
        P(PAGE, None),
        P(PAGE, None),
        P(STREAM, None),
        P(STREAM, None),
        P(STREAM, None, None),
        P(STREAM, None, None),
        P(STREAM, None, None),
        P(STREAM, None, None),
        P(STREAM, None, None),
        P(STREAM, None, None),
        P(STREAM, None, None),
        P(STREAM, None, None),
        P(STREAM, PAGE, None, None),
    )
    return jax.shard_map(
        body,
        mesh=mesh,
        in_specs=placed,
        out_specs=(
            P(STREAM, PAGE, None, None),
            P(STREAM, PAGE, None, None),
            P(STREAM, PAGE),
            P(STREAM, PAGE),
            P(STREAM, PAGE, None),
            P(STREAM, PAGE, None),
            P(STREAM, PAGE, None),
            P(STREAM, PAGE, None),
            P(STREAM, PAGE, None),
            P(STREAM, PAGE, None),
            P(STREAM, PAGE, None),
            P(STREAM, PAGE, None),
        ),
        check_vma=False,
    )
```

```python
import functools
from typing import Any, NamedTuple

import jax
import jax.numpy as jnp
from jax import lax
from jax.experimental import pallas as pl
from jax.experimental.pallas import tpu as pltpu
from jax.sharding import PartitionSpec as P

GRID_SMALL = 16
GRID_LARGE = 24
EPSILON = 1e-05
MASKED = -1000000000.0
PAGE = "page"
STREAM = "stream"
BF = jnp.bfloat16
F32 = jnp.float32
WIDE = 128


def contract(left, right, left_dim, right_dim):
    return lax.dot_general(
        left, right, (((left_dim,), (right_dim,)), ((), ())), preferred_element_type=F32
    )


def params(mib=48):
    return pltpu.CompilerParams(vmem_limit_bytes=mib << 20)


def cost(us):
    return pl.CostEstimate(flops=int(us * 1.1e9), bytes_accessed=1 << 20, transcendentals=0)


def swapped(shard, axis, mask):
    return lax.ppermute(shard, axis, [(i, i ^ mask) for i in range(lax.axis_size(axis))])


def pieces(row):
    high = row.astype(BF).astype(F32)
    rest = row - high
    middle = rest.astype(BF).astype(F32)
    return high, middle, rest - middle


def extra_rows(rows, count):
    index = lax.broadcasted_iota(jnp.int32, (16, count), 0)
    block = jnp.zeros((16, count), F32)
    for place, row in enumerate(rows):
        block = jnp.where(index == place, row, block)
    return block.astype(BF)


def forward_pair(scale, queries, key_rows, values, mask, bias):
    count = queries.shape[0]
    half = WIDE // 2
    queries = (queries * scale).T
    key_rows = key_rows.T
    values = values.T
    ones = jnp.ones((1, count), F32)
    query_extra = extra_rows([ones], count)
    key_extra = extra_rows([mask], count)
    outs, logs = [], []
    for side in range(2):
        part = slice(half * side, half * side + half)
        if bias is not None:
            bands, onehot = bias
            band = contract(bands[side], onehot, 1, 0).astype(BF)
            left = jnp.concatenate([key_rows[part], onehot, key_extra], 0)
            right = jnp.concatenate([queries[part], band, query_extra], 0)
        else:
            left = jnp.concatenate([key_rows[part], key_extra], 0)
            right = jnp.concatenate([queries[part], query_extra], 0)
        scores = contract(left, right, 0, 0)
        top = jnp.max(scores, axis=0, keepdims=True)
        weights = jnp.exp(scores - top).astype(BF)
        output = contract(jnp.concatenate([values[part], query_extra], 0), weights, 1, 0)
        total = output[half : half + 1]
        outs.append(output[:half] * (1.0 / total))
        logs.append(top + jnp.log(total))
    return jnp.concatenate(outs, 0).astype(BF).T, jnp.concatenate(logs, 0)


def forward_kernel(has_bias, scale, *refs):
    q_ref, k_ref, v_ref, mask_ref = refs[:4]
    bias = (refs[4][...], refs[5][...]) if has_bias else None
    o_ref, lse_ref = refs[-2:]
    o_ref[...], lse_ref[0] = forward_pair(scale, q_ref[...], k_ref[...], v_ref[...], mask_ref[...], bias)


def backward_pair(scale, queries, key_rows, values, grad_out, output, lse, mask, bias):
    if bias is not None:
        bands, onehot, flipped = bias
    count = queries.shape[0]
    half = WIDE // 2
    queries = (queries * scale).T
    key_rows = key_rows.T
    values = values.T
    grad_out = grad_out.T
    product = grad_out.astype(F32) * output.T.astype(F32)
    ones = jnp.ones((1, count), F32)
    key_extra = extra_rows([ones, ones, ones, mask], count)
    value_extra = extra_rows([ones, ones, ones], count)
    d_queries, d_keys, d_values, d_bands = [], [], [], []
    for side in range(2):
        part = slice(half * side, half * side + half)
        lse_rows = extra_rows([*pieces(-lse[side : side + 1, :]), ones], count)
        delta = jnp.sum(product[part], axis=0, keepdims=True)
        delta_rows = extra_rows(list(pieces(-delta)), count)
        if bias is not None:
            band = contract(bands[side], onehot, 1, 0).astype(BF)
            left = jnp.concatenate([queries[part], band, lse_rows], 0)
            right = jnp.concatenate([key_rows[part], onehot, key_extra], 0)
        else:
            left = jnp.concatenate([queries[part], lse_rows], 0)
            right = jnp.concatenate([key_rows[part], key_extra], 0)
        weights = jnp.exp(contract(left, right, 0, 0))
        d_weights = contract(
            jnp.concatenate([grad_out[part], delta_rows], 0),
            jnp.concatenate([values[part], value_extra], 0),
            0,
            0,
        )
        d_scores = (weights * d_weights).astype(BF)
        d_values.append(contract(grad_out[part], weights.astype(BF), 1, 0))
        d_keys.append(contract(queries[part], d_scores, 1, 0))
        scaled = key_rows[part] * scale
        if bias is not None:
            both = contract(jnp.concatenate([scaled, flipped], 0), d_scores, 1, 1)
            d_queries.append(both[:half])
            d_bands.append(contract(onehot, both[half:].astype(BF), 1, 1))
        else:
            d_queries.append(contract(scaled, d_scores, 1, 1))
    out = tuple(jnp.concatenate(each, 0).astype(BF).T for each in (d_queries, d_keys, d_values))
    return out if bias is None else (*out, jnp.stack(d_bands))


def backward_kernel(has_bias, scale, *refs):
    q_ref, k_ref, v_ref, do_ref, o_ref, lse_ref, mask_ref = refs[:7]
    bias = tuple(ref[...] for ref in refs[7:10]) if has_bias else None
    outs = refs[10:] if has_bias else refs[7:]
    grads = backward_pair(
        scale, q_ref[...], k_ref[...], v_ref[...], do_ref[...], o_ref[...], lse_ref[0], mask_ref[...], bias
    )
    outs[0][...] = grads[0]
    outs[1][0] = grads[1]
    outs[1][1] = grads[2]
    if has_bias:
        outs[2][...] = grads[3]


def column(first):
    return lambda i: (0, first + i)


def attend_forward(query_rows, key_value_rows, first, mask, bias, scale, us):
    count = query_rows.shape[0]
    pairs = key_value_rows.shape[1] // WIDE // (3 if first else 2)
    block = lambda start: pl.BlockSpec((count, WIDE), column(start))
    row = pl.BlockSpec((1, count), lambda i: (0, 0))
    wide = pl.BlockSpec((WIDE, count), lambda i: (0, 0))
    specs = [block(0), block(first), block(first + pairs), row]
    operands = [query_rows, key_value_rows, key_value_rows, mask]
    if bias is not None:
        specs += [pl.BlockSpec((2, WIDE, WIDE), lambda i: (i, 0, 0)), wide]
        operands += [bias[0], bias[1]]
    return pl.pallas_call(
        functools.partial(forward_kernel, bias is not None, scale),
        grid=(pairs,),
        in_specs=specs,
        out_specs=[block(0), pl.BlockSpec((1, 2, count), lambda i: (i, 0, 0))],
        out_shape=[
            jax.ShapeDtypeStruct((count, pairs * WIDE), BF),
            jax.ShapeDtypeStruct((pairs, 2, count), F32),
        ],
        compiler_params=params(),
        cost_estimate=cost(us),
    )(*operands)


def attend_backward(query_rows, key_value_rows, first, grad_out, output, lse, mask, bias, scale, us):
    count = query_rows.shape[0]
    pairs = lse.shape[0]
    block = lambda start: pl.BlockSpec((count, WIDE), column(start))
    row = pl.BlockSpec((1, count), lambda i: (0, 0))
    wide = pl.BlockSpec((WIDE, count), lambda i: (0, 0))
    band = pl.BlockSpec((2, WIDE, WIDE), lambda i: (i, 0, 0))
    specs = [
        block(0),
        block(first),
        block(first + pairs),
        block(0),
        block(0),
        pl.BlockSpec((1, 2, count), lambda i: (i, 0, 0)),
        row,
    ]
    operands = [query_rows, key_value_rows, key_value_rows, grad_out, output, lse, mask]
    out_specs = [block(0), pl.BlockSpec((2, count, WIDE), lambda i: (0, 0, i))]
    out_shape = [
        jax.ShapeDtypeStruct((count, pairs * WIDE), BF),
        jax.ShapeDtypeStruct((2, count, pairs * WIDE), BF),
    ]
    if bias is not None:
        specs += [band, wide, wide]
        operands += list(bias)
        out_specs.append(band)
        out_shape.append(jax.ShapeDtypeStruct((2 * pairs, WIDE, WIDE), F32))
    return pl.pallas_call(
        functools.partial(backward_kernel, bias is not None, scale),
        grid=(pairs,),
        in_specs=specs,
        out_specs=out_specs,
        out_shape=out_shape,
        compiler_params=params(),
        cost_estimate=cost(us),
    )(*operands)


def same_block(shape):
    rows = lax.broadcasted_iota(jnp.int32, shape, 0) // (WIDE // 2)
    columns = lax.broadcasted_iota(jnp.int32, shape, 1) // (WIDE // 2)
    return rows == columns


def band_kernel(table_ref, band_ref):
    heads = band_ref.shape[0]
    shape = (WIDE, WIDE)
    keep = same_block(shape)
    lower = lax.broadcasted_iota(jnp.int32, shape, 0) >= WIDE // 2
    for head in range(heads):
        across = jnp.broadcast_to(table_ref[head : head + 1, :], shape)
        down = jnp.broadcast_to(table_ref[heads + head : heads + head + 1, :], shape)
        rolled = pltpu.roll(jnp.where(lower, down, across), WIDE // 2, 1, stride=1, stride_axis=0)
        band_ref[head] = jnp.where(keep, rolled, 0.0).astype(BF)


def make_bands(table):
    heads = table.shape[1] // 2
    return pl.pallas_call(
        band_kernel,
        out_shape=jax.ShapeDtypeStruct((heads, WIDE, WIDE), BF),
        compiler_params=params(),
        cost_estimate=cost(3),
    )(table.T)


def unband_kernel(grad_ref, table_ref):
    heads = grad_ref.shape[0]
    half = WIDE // 2
    shape = (WIDE, WIDE)
    keep = same_block(shape)
    for head in range(heads):
        rolled = pltpu.roll(jnp.where(keep, grad_ref[head], 0.0), 1, 1, stride=1, stride_axis=0)
        table_ref[head : head + 1, :] = jnp.sum(rolled[:half], axis=0, keepdims=True)
        table_ref[heads + head : heads + head + 1, :] = jnp.sum(rolled[half:], axis=0, keepdims=True)


def gather_bands(grads):
    heads = grads.shape[0]
    table = pl.pallas_call(
        unband_kernel,
        out_shape=jax.ShapeDtypeStruct((2 * heads, WIDE), F32),
        compiler_params=params(),
        cost_estimate=cost(3),
    )(grads)
    return table.T


def gelu_pair(value):
    density = jnp.exp(value * value * -0.5) * 0.3989422804014327
    t = 1.0 / (1.0 + 0.2316419 * jnp.abs(value))
    poly = t * (0.319381530 + t * (-0.356563782 + t * (1.781477937 + t * (-1.821255978 + t * 1.330274429))))
    tail = poly * density
    phi = jnp.where(value >= 0, 1.0 - tail, tail)
    return value * phi, phi + value * density


def feed_kernel(me_ref, second_ref, grad_ref, up_ref, down_ref, hidden_ref, d_up_ref, send_ref, keep_ref, sums_ref):
    tile = pl.program_id(0)
    grad = grad_ref[...]
    value = contract(second_ref[...], up_ref[...], 1, 0)
    hidden, slope = gelu_pair(value)
    hidden = hidden.astype(BF)
    hidden_ref[...] = hidden
    back = contract(grad, down_ref[...], 1, 1)
    d_up_ref[...] = (slope * back).astype(BF)
    sums_ref[...] = contract(hidden, grad, 0, 0)
    rows = send_ref.shape[1]
    per_tile = sums_ref.shape[0] // rows
    place_rows(me_ref[0], tile * per_tile, per_tile, rows, sums_ref, send_ref, keep_ref, 0)


def place_rows(me, first, number, rows, sums_ref, send_ref, keep_ref, offset):
    halves = send_ref.shape[0]
    quarters = halves // 2
    for local in range(number):
        relative = (first + local) ^ me
        slot = ((relative >> 1) & 1) * quarters + (relative >> 2)
        block = sums_ref[local * rows : local * rows + rows, :].astype(BF)

        @pl.when(relative & 1 == 1)
        def _():
            send_ref[slot, offset : offset + rows, :] = block

        @pl.when(relative & 1 == 0)
        def _():
            keep_ref[slot, offset : offset + rows, :] = block


def feed_forward(me, second, grad, w_up, w_down, parts):
    count, width = second.shape
    hidden_width = w_up.shape[1]
    rows = hidden_width // parts
    tiles = hidden_width // width
    whole = pl.BlockSpec((count, width), lambda i, me: (0, 0))
    tile = pl.BlockSpec((count, width), lambda i, me: (0, i))
    slots = pl.BlockSpec((parts // 2, rows, width), lambda i, me: (0, 0, 0))
    return pl.pallas_call(
        feed_kernel,
        grid_spec=pltpu.PrefetchScalarGridSpec(
            num_scalar_prefetch=1,
            grid=(tiles,),
            in_specs=[
                whole,
                whole,
                pl.BlockSpec((width, width), lambda i, me: (0, i)),
                pl.BlockSpec((width, width), lambda i, me: (i, 0)),
            ],
            out_specs=[tile, tile, slots, slots],
            scratch_shapes=[pltpu.VMEM((width, width), F32)],
        ),
        out_shape=[
            jax.ShapeDtypeStruct((count, hidden_width), BF),
            jax.ShapeDtypeStruct((count, hidden_width), BF),
            jax.ShapeDtypeStruct((parts // 2, rows, width), BF),
            jax.ShapeDtypeStruct((parts // 2, rows, width), BF),
        ],
        compiler_params=params(56),
        cost_estimate=cost(22),
    )(me, second, grad, w_up, w_down)


def outer_kernel(plan, rows, me_ref, *refs):
    tile = pl.program_id(0)
    lefts, rights = refs[: len(plan)], refs[len(plan) : 2 * len(plan)]
    send_ref, keep_ref, sums_ref = refs[2 * len(plan) :]
    number = 2 * send_ref.shape[0]
    first = 0
    for (tiles,), left_ref, right_ref in zip(plan, lefts, rights):
        for step in range(tiles):

            @pl.when(tile == first + step)
            def _(left_ref=left_ref, right_ref=right_ref, offset=(first + step) * rows):
                sums_ref[...] = contract(left_ref[...], right_ref[...], 0, 0)
                place_rows(me_ref[0], 0, number, rows, sums_ref, send_ref, keep_ref, offset)

        first += tiles


def outer_products(me, pairs, parts, us, extra=None):
    count, width = pairs[0][0].shape
    rows = width // parts
    plan, specs_left, specs_right = [], [], []
    first = 0
    for left, right in pairs:
        tiles = right.shape[1] // width
        plan.append((tiles,))
        specs_left.append(pl.BlockSpec((count, width), lambda i, me: (0, 0)))
        specs_right.append(
            pl.BlockSpec(
                (count, width),
                lambda i, me, first=first, tiles=tiles: (0, jnp.clip(i - first, 0, tiles - 1)),
            )
        )
        first += tiles
    slots = pl.BlockSpec((parts // 2, first * rows, width), lambda i, me: (0, 0, 0))
    shape = jax.ShapeDtypeStruct((parts // 2, first * rows, width), BF)
    return pl.pallas_call(
        functools.partial(outer_kernel, plan, rows),
        grid_spec=pltpu.PrefetchScalarGridSpec(
            num_scalar_prefetch=1,
            grid=(first,),
            in_specs=specs_left + specs_right,
            out_specs=[slots, slots],
            scratch_shapes=[pltpu.VMEM((width, width), F32)],
        ),
        out_shape=[shape, shape],
        compiler_params=params(56),
        cost_estimate=cost(us),
    )(me, *[left for left, _ in pairs], *[right for _, right in pairs])


def reduce_parts(send, keep):
    half = send.shape[0] // 2
    arrived = swapped(send, PAGE, 1).astype(F32)
    away = (arrived[half:] + keep[half:].astype(F32)).astype(BF)
    mine = arrived[:half] + keep[:half].astype(F32)
    mine = mine + swapped(away, PAGE, 2).astype(F32)
    total = mine[0]
    for step in range(1, half):
        total = total + swapped(mine[step].astype(BF), PAGE, 4 * step).astype(F32)
    return total


def flip(position, mask):
    out = position
    bit = 1
    while bit <= mask:
        if mask & bit:
            out = out + bit * (1 - 2 * lax.rem(lax.div(position, bit), 2))
        bit *= 2
    return out


RING = 2
STORES = 8
FETCHES = 14
LANDINGS = 3
LINK_US = 6.6
CORE_US = 1.7
LATE_US = 30.0
LATENCY_US = 4.5


CORE, NEAR, FAR, JOIN, LAST, DONE, Y, Z = range(8)
KV = 98
WEIGHTS = (96, 97)


class Flow:
    def __init__(self, refs, me, side):
        self.r = refs
        self.me = me
        self.side = side
        self.now = 0.0
        self.y_free = 0.0
        self.z_free = 0.0
        self.middle_free = 0.0
        self.pending = []
        self.near_done = {}
        self.stores = []

    def at(self, mask):
        return {PAGE: flip(self.me, mask)}

    def core_copy(self, unit):
        r = self.r
        return pltpu.make_async_remote_copy(
            src_ref=r.ring.at[unit % RING],
            dst_ref=r.core_in.at[unit % LANDINGS],
            send_sem=r.core_sent.at[unit % RING],
            recv_sem=r.core_got.at[unit % LANDINGS],
            device_id=self.at(1),
            device_id_type=pl.DeviceIdType.MESH,
        )

    def y_copy(self, unit):
        r = self.r
        if unit in TURNED_UNITS:
            source, landing = r.keep.at[unit, 1, 0], r.z_in.at[PLAIN_UNITS.index(unit), 2]
        else:
            source, landing = r.keep.at[unit, 1], r.y_in.at[Y_PLACES[unit]]
        return pltpu.make_async_remote_copy(
            src_ref=source,
            dst_ref=landing,
            send_sem=r.y_sent.at[int(unit in TURNED_UNITS)],
            recv_sem=r.y_got.at[Y_PLACES.get(unit, len(Y_PLACES))],
            device_id=self.at(2),
            device_id_type=pl.DeviceIdType.MESH,
        )

    def z_place(self, unit):
        if unit in PLAIN_UNITS:
            return PLAIN_UNITS.index(unit)
        return len(PLAIN_UNITS) + DOWN_STEPS[DOWN_UNITS.index(unit)] // 2

    def near_copy(self, unit, arriving=False):
        r = self.r
        if unit in DOWN_UNITS:
            step = DOWN_STEPS[DOWN_UNITS.index(unit)]
            if (step in NEAR_STEPS) == arriving:
                return None
            target = unit if arriving else DOWN_UNITS[DOWN_STEPS.index(step ^ 1)]
            source, landing = r.keep.at[unit], r.near_down.at[step // 2]
        elif unit in TURNED_UNITS:
            target = unit
            source = r.keep.at[unit, :, pl.ds(2, 2)]
            landing = r.turned_in.at[TURNED_UNITS.index(unit)]
        else:
            target = unit
            if unit in UP_UNITS and not arriving:
                target = UP_UNITS[DOWN_STEPS.index(DOWN_STEPS[UP_UNITS.index(unit)] ^ 1)]
            source = r.keep.at[unit, 0, pl.ds(2, 2)]
            landing = r.z_in.at[PLAIN_UNITS.index(target), pl.ds(0, 2)]
        return pltpu.make_async_remote_copy(
            src_ref=source,
            dst_ref=landing,
            send_sem=r.near_sent.at[int(unit in TURNED_UNITS)],
            recv_sem=r.near_got.at[self.z_place(target)],
            device_id=self.at(4),
            device_id_type=pl.DeviceIdType.MESH,
        )

    def far_copy(self, unit, arriving=False):
        r = self.r
        if unit in DOWN_UNITS:
            step = DOWN_STEPS[DOWN_UNITS.index(unit)]
            if step != (0 if arriving else 3):
                return None
            target = DOWN_UNITS[DOWN_STEPS.index(0)]
            source, landing = r.keep.at[unit, 0], r.far_down
        elif unit in TURNED_UNITS:
            target = unit
            source, landing = r.keep.at[unit, :, 1], r.z_in.at[PLAIN_UNITS.index(unit), pl.ds(0, 2)]
        else:
            target = unit
            if unit in UP_UNITS and not arriving:
                target = UP_UNITS[DOWN_STEPS.index(DOWN_STEPS[UP_UNITS.index(unit)] ^ 3)]
            source, landing = r.keep.at[unit, 0, 1], r.z_in.at[PLAIN_UNITS.index(target), 2]
        return pltpu.make_async_remote_copy(
            src_ref=source,
            dst_ref=landing,
            send_sem=r.far_sent.at[int(unit in TURNED_UNITS)],
            recv_sem=r.far_got.at[self.z_place(target)],
            device_id=self.at(12),
            device_id_type=pl.DeviceIdType.MESH,
        )

    def produce(self, unit, left, *rights):
        r = self.r
        first = 0
        for right in rights:
            last = first + right.shape[1]
            r.sums[:, first:last] = contract(left, right, 0, 0).astype(BF)
            first = last
        self.tick(1.2)
        if unit >= RING:
            self.core_copy(unit - RING).wait_send()
        core = lax.rem(self.me, 2)
        y = lax.rem(lax.div(self.me, 2), 2)
        z = lax.div(self.me, 4)
        for rel_y in range(2):
            for rel_z in range(4):
                y_at = flip(y, rel_y)
                if unit in DOWN_UNITS:
                    first = y_at * 8 * ROWS
                    mine = first + core * 4 * ROWS + rel_z * ROWS
                    other = first + (1 - core) * 4 * ROWS + rel_z * ROWS
                else:
                    first = flip(z, rel_z) * 4 * ROWS + y_at * 2 * ROWS
                    mine = first + core * ROWS
                    other = first + (1 - core) * ROWS
                slot = rel_y * 4 + (rel_z if unit in DOWN_UNITS else SLOT_OF[rel_z])
                r.ring[unit % RING, rel_y, slot - 4 * rel_y] = r.sums[pl.ds(pl.multiple_of(other, 16), ROWS), :]
                r.keep[unit, rel_y, slot - 4 * rel_y] = r.sums[pl.ds(pl.multiple_of(mine, 16), ROWS), :]
        if unit >= LANDINGS:
            pl.semaphore_wait(r.credit.at[unit - LANDINGS], 1)
        self.core_copy(unit).start()
        self.now += 0.5
        self.pending.append([unit, CORE, self.now + CORE_US])

    def advance(self, entry):
        self.plan(entry)()

    def near_busy(self, blocks):
        self.z_free = max(self.now, self.z_free) + blocks * LINK_US / 4
        return self.z_free + LATENCY_US

    def far_busy(self, blocks):
        self.z_free = max(self.now, self.z_free) + blocks * LINK_US / 4
        self.middle_free = max(self.now, self.middle_free) + blocks * LINK_US / 2
        return max(self.z_free, self.middle_free) + LATENCY_US

    def y_busy(self, us):
        self.y_free = max(self.now, self.y_free) + us
        return self.y_free + 0.3

    def plan(self, entry):
        unit, stage, _ = entry
        step = None
        if unit in WEIGHTS:
            if stage < 3:
                entry[1:] = [stage + 1, self.now + (3.8, 8.0, 2.5)[stage]]
            else:
                entry[1] = DONE
            return functools.partial(self.run, unit, stage)
        if unit in DOWN_UNITS:
            step = DOWN_STEPS[DOWN_UNITS.index(unit)]
        if unit == KV:
            entry[1] = DONE
        elif unit == SMALL:
            free = max(self.now, self.y_free if stage == CORE else self.z_free)
            following = {CORE: Y, Y: Z, Z: DONE}[stage]
            entry[1:] = [following, free + (1.0 if stage == CORE else 7.0)]
        elif unit in TURNED_UNITS:
            if stage == CORE:
                entry[1:] = [NEAR, self.near_busy(4)]
            elif stage == NEAR:
                entry[1:] = [FAR, self.far_busy(2)]
            elif stage == FAR:
                entry[1:] = [LAST, self.y_busy(LINK_US / 4) + LATE_US]
            else:
                entry[1] = DONE
        elif stage == CORE:
            if step in NEAR_STEPS:
                self.near_done[step ^ 1] = self.near_busy(8)
                entry[1] = DONE
            elif step is not None:
                entry[1:] = [JOIN, self.near_done[step]]
            else:
                entry[1:] = [Y, self.y_busy(LINK_US)]
        elif stage == JOIN:
            entry[1:] = [Y, self.y_busy(LINK_US)]
        elif stage == Y:
            if step is not None:
                done = self.far_busy(4) if step == 3 else self.z_free + LATE_US
                entry[1:] = [DONE, 0.0] if step == 3 else [FAR, done + LATE_US]
            else:
                entry[1:] = [NEAR, self.near_busy(2)]
                if unit in UP_UNITS:
                    self.meet(entry, [unit, UP_UNITS[DOWN_STEPS.index(DOWN_STEPS[UP_UNITS.index(unit)] ^ 1)]])
        elif stage == NEAR:
            entry[1:] = [FAR, self.far_busy(1) + (8.0 if unit in KV_UNITS else LATE_US)]
            if unit in UP_UNITS:
                self.meet(entry, UP_UNITS)
        else:
            entry[1] = DONE
            if unit == KV_UNITS[1]:
                self.pending.append([KV, CORE, self.now + LATE_US])
        return functools.partial(self.run, unit, stage)

    def meet(self, entry, units):
        due, entry[2] = entry[2], float("inf")
        waiting = [e for e in self.pending if e[0] in units and e[1] == entry[1]]
        if len(waiting) == len(units):
            for other in waiting:
                other[2] = due

    def join(self, unit, half, places, arrived):
        r = self.r
        for place in places:
            total = r.keep[unit, half, place].astype(F32) + arrived[place].astype(F32)
            r.keep[unit, half, place] = total.astype(BF)

    def run(self, unit, stage):
        r = self.r
        if unit in WEIGHTS:
            self.weight_arrival(WEIGHTS.index(unit), stage).wait_recv()
            if stage < 3:
                self.weight_copy(WEIGHTS.index(unit), stage + 1).start()
            return
        if unit == KV:
            self.kv_copy().wait_recv()
            self.store(KV)
            return
        if unit == SMALL:
            self.run_small((CORE, Y, Z).index(stage))
            return
        step = None
        if unit in DOWN_UNITS:
            step = DOWN_STEPS[DOWN_UNITS.index(unit)]
        turned = unit in TURNED_UNITS
        if stage == CORE:
            self.core_copy(unit).wait_recv()
            arrived = r.core_in.at[unit % LANDINGS]
            self.join(unit, 1, (0, 1, 2, 3), arrived.at[1])
            if step is None and not turned:
                self.y_copy(unit).start()
            self.join(unit, 0, (0, 1, 2, 3), arrived.at[0])
            if turned or step in NEAR_STEPS:
                self.near_copy(unit).start()
            if unit < UNITS - LANDINGS:
                pl.semaphore_signal(
                    r.credit.at[unit], 1, device_id=self.at(1), device_id_type=pl.DeviceIdType.MESH
                )
        elif stage == JOIN:
            self.near_copy(unit, arriving=True).wait_recv()
            arrived = r.near_down.at[step // 2]
            self.join(unit, 1, (0, 1, 2, 3), arrived.at[1])
            self.y_copy(unit).start()
            self.join(unit, 0, (0, 1, 2, 3), arrived.at[0])
        elif stage == Y:
            self.y_copy(unit).wait_recv()
            self.join(unit, 0, (2, 3, 0, 1), r.y_in.at[Y_PLACES[unit]])
            if step is None:
                self.near_copy(unit).start()
            elif step == 3:
                self.far_copy(unit).start()
        elif stage == NEAR:
            self.near_copy(unit, arriving=True).wait_recv()
            if turned:
                arrived = r.turned_in.at[TURNED_UNITS.index(unit)]
                for half in (0, 1):
                    self.join(unit, half, (1, 0), arrived.at[half])
            else:
                self.join(unit, 0, (1, 0), r.z_in.at[PLAIN_UNITS.index(unit)])
            self.far_copy(unit).start()
        elif turned and stage == FAR:
            self.far_copy(unit, arriving=True).wait_recv()
            arrived = r.z_in.at[PLAIN_UNITS.index(unit)]
            for half in (1, 0):
                total = r.keep[unit, half, 0].astype(F32) + arrived[half].astype(F32)
                r.keep[unit, half, 0] = total.astype(BF)
                if half:
                    self.y_copy(unit).start()
        elif turned:
            self.y_copy(unit).wait_recv()
            self.finish(unit)
        else:
            self.far_copy(unit, arriving=True).wait_recv()
            self.finish(unit)

    def small_copies(self, stage):
        r = self.r
        return [
            pltpu.make_async_remote_copy(
                src_ref=r.small_in.at[5 + stage],
                dst_ref=r.small_in.at[place],
                send_sem=r.small_sent.at[0],
                recv_sem=r.small_got.at[place],
                device_id=self.at(mask),
                device_id_type=pl.DeviceIdType.MESH,
            )
            for place, mask in SMALL_STEPS[stage]
        ]

    def kv_copy(self):
        r = self.r
        return pltpu.make_async_remote_copy(
            src_ref=r.kv_out,
            dst_ref=r.kv_in,
            send_sem=r.kv_sent.at[0],
            recv_sem=r.kv_got.at[0],
            device_id={STREAM: 1 - self.side},
            device_id_type=pl.DeviceIdType.MESH,
        )

    def weight_copy(self, half, stage):
        r = self.r
        core, y, z = lax.rem(self.me, 2), lax.rem(lax.div(self.me, 2), 2), lax.rem(lax.div(self.me, 4), 2)
        share = r.other_w.shape[-2]
        target, device = r.other_w.at[half, z, y, core], {STREAM: 1 - self.side}
        source = target
        if stage == 0:
            first = pl.multiple_of((z * 4 + y * 2 + core) * share, 16)
            source = r.w_ckv.at[pl.ds(first, share), half * WIDTH : (half + 1) * WIDTH]
        elif stage == 1:
            device = self.at(4)
        elif stage == 2:
            source = target = r.other_w.at[half, :, y, core]
            device = self.at(2)
        else:
            source = target = r.other_w.at[half, :, :, core]
            device = self.at(1)
        return pltpu.make_async_remote_copy(
            src_ref=source,
            dst_ref=target,
            send_sem=r.weight_sent.at[0],
            recv_sem=r.weight_got.at[half, stage],
            device_id=device,
            device_id_type=pl.DeviceIdType.MESH,
        )

    def weight_arrival(self, half, stage):
        r = self.r
        core, y, z = lax.rem(self.me, 2), lax.rem(lax.div(self.me, 2), 2), lax.rem(lax.div(self.me, 4), 2)
        target = (
            r.other_w.at[half, z, y, core],
            r.other_w.at[half, 1 - z, y, core],
            r.other_w.at[half, :, 1 - y, core],
            r.other_w.at[half, :, :, 1 - core],
        )[stage]
        return pltpu.make_async_remote_copy(
            src_ref=target,
            dst_ref=target,
            send_sem=r.weight_sent.at[0],
            recv_sem=r.weight_got.at[half, stage],
            device_id=self.at(1),
            device_id_type=pl.DeviceIdType.MESH,
        )

    def start_weights(self):
        for half in range(2):
            self.weight_copy(half, 0).start()
            self.pending.append([WEIGHTS[half], 0, self.now + 4.0 + 3.0 * half])

    def finish_weights(self):
        while True:
            left = [e for e in self.pending if e[0] in WEIGHTS]
            if not left:
                return
            entry = min(left, key=lambda e: e[2])
            self.now = max(self.now, entry[2])
            self.advance(entry)
            self.pending = [e for e in self.pending if e[1] != DONE]

    def start_small(self):
        r = self.r
        r.small_in[5] = r.small_sum[...]
        for copy in self.small_copies(0):
            copy.start()
        self.pending.append([SMALL, CORE, self.now + CORE_US + 1.0])

    def run_small(self, stage):
        r = self.r
        for copy in self.small_copies(stage):
            copy.wait_recv()
        for place, _ in SMALL_STEPS[stage]:
            r.small_sum[...] += r.small_in[place]
        if stage < 2:
            r.small_in[6 + stage] = r.small_sum[...]
            for copy in self.small_copies(stage + 1):
                copy.start()

    def due(self):
        while True:
            ready = [e for e in self.pending if e[2] <= self.now]
            if not ready:
                return
            entry = min(ready, key=lambda e: e[2])
            yield entry
            self.pending = [e for e in self.pending if e[1] != DONE]

    def tick(self, us):
        self.now += us
        for entry in self.due():
            self.advance(entry)

    def drain(self):
        while self.pending:
            self.now = max(self.now, min(e[2] for e in self.pending))
            for entry in self.due():
                self.advance(entry)
        for unit in range(UNITS - RING, UNITS):
            self.core_copy(unit).wait_send()
        r = self.r
        for whole, sent in (
            (r.y_in, r.y_sent),
            (r.s.at[pl.ds(0, 3), pl.ds(0, 608)], r.near_sent),
            (r.z_in.at[pl.ds(0, 5)], r.far_sent),
            (r.small_in.at[pl.ds(0, 5)], r.small_sent),
            (r.other_w, r.weight_sent),
            (r.s.at[Slot.normed], r.normed_sent),
        ):
            pltpu.make_async_copy(whole, whole, sent.at[0]).wait()
        for unit in TURNED_UNITS:
            for copy in (self.near_copy(unit), self.far_copy(unit), self.y_copy(unit)):
                copy.wait_send()
        self.kv_copy().wait_send()
        for place in range(max(0, len(self.stores) - STORES), len(self.stores)):
            self.store_copy(place).wait()

    def store_copy(self, place):
        r = self.r
        unit, part = self.stores[place]
        if unit == KV:
            pairs = [(r.kv_in, r.ckv_out)]
        elif unit in DOWN_UNITS:
            pairs = [(r.done.at[pl.ds(0, 4)], r.down_out)]
        elif unit in UP_UNITS:
            tile = flip(lax.div(self.me, 4), DOWN_STEPS[UP_UNITS.index(unit)])
            columns = pl.ds(pl.multiple_of(tile * WIDTH, WIDE), WIDTH)
            pairs = [(r.done.at[self.done_at(unit)], r.up_out.at[:, columns])]
        elif unit in THIRD_UNITS:
            third = WIDTH // 3
            first = third * THIRD_UNITS.index(unit)
            source = r.done.at[self.done_at(unit)]
            pairs = [
                (source.at[:, pl.ds(i * third, third)], r.qkv_out.at[:, pl.ds(i * WIDTH + first, third)])
                for i in range(3)
            ]
        else:
            pairs = [(r.done.at[self.done_at(unit)], {8: r.cout_out, 11: r.cq_out, 12: r.out_out}[unit])]
        return pltpu.make_async_copy(*pairs[part], r.stored_sums.at[place % STORES])

    def done_at(self, unit):
        return 4 + PLAIN_UNITS.index(unit)

    def store(self, unit):
        for part in range(3 if unit in THIRD_UNITS else 1):
            place = len(self.stores)
            if place >= STORES:
                self.store_copy(place - STORES).wait()
            self.stores.append((unit, part))
            self.store_copy(place).start()

    def finish(self, unit):
        r = self.r
        if unit in DOWN_UNITS:
            r.done[0:4] = r.keep[unit, 0].astype(F32) + r.far_down[...].astype(F32)
            self.store(unit)
            return
        total = r.keep[unit, 0, 0].astype(F32) + r.z_in[PLAIN_UNITS.index(unit), 2].astype(F32)
        if unit in KV_UNITS:
            half = KV_UNITS.index(unit)
            r.kv_out[:, half * WIDTH : (half + 1) * WIDTH] = total
            if half:
                self.kv_copy().start()
            return
        r.done[self.done_at(unit)] = total
        self.store(unit)


WIDTH = 768
ROWS = 48
DOWN_UNITS = (1, 3, 5, 7)
TURNED_UNITS = (13,)
UP_UNITS = (0, 2, 4, 6)
DOWN_STEPS = (1, 2, 3, 0)
NEAR_STEPS = (1, 2)
SLOT_OF = (0, 2, 3, 1)
PLAIN_UNITS = (0, 2, 4, 6, 8, 9, 10, 11, 12, 13, 14, 15)
UNITS = 16
Y_PLACES = {unit: at for at, unit in enumerate((0, 2, 4, 5, 6, 7, 8, 9, 10, 11, 12, 14, 15))}
KV_UNITS = (9, 10)
THIRD_UNITS = (13, 14, 15)


class Fetch:
    def __init__(self, source, target, semaphores, free):
        self.free = free
        self.place = free.pop(0)
        self.copy = pltpu.make_async_copy(source, target, semaphores.at[self.place])
        self.copy.start()

    def wait(self):
        self.copy.wait()
        self.free.append(self.place)


class Refs(NamedTuple):
    states: Any
    cotangent: Any
    w_qkv: Any
    w_out: Any
    w_cq: Any
    w_ckv: Any
    w_cout: Any
    w_up: Any
    w_down: Any
    counts: Any
    box_x: Any
    box_y: Any
    gain1: Any
    gain2: Any
    table_in: Any
    result_out: Any
    states_out: Any
    held_out: Any
    down_out: Any
    up_out: Any
    cout_out: Any
    cq_out: Any
    out_out: Any
    qkv_out: Any
    ckv_out: Any
    gain1_out: Any
    gain2_out: Any
    table_out: Any
    s: Any
    f: Any
    w: Any
    fetched: Any
    stored: Any
    sums: Any
    keep: Any
    ring: Any
    core_in: Any
    y_in: Any
    z_in: Any
    near_down: Any
    far_down: Any
    turned_in: Any
    core_sent: Any
    core_got: Any
    y_sent: Any
    y_got: Any
    near_sent: Any
    near_got: Any
    far_sent: Any
    far_got: Any
    credit: Any
    normed_sent: Any
    normed_got: Any
    back_sent: Any
    back_got: Any
    weight_sent: Any
    weight_got: Any
    other_w: Any
    done: Any
    stored_sums: Any
    kv_out: Any
    kv_in: Any
    kv_sent: Any
    kv_got: Any
    self_lse: Any
    cross_lse: Any
    bands: Any
    onehot: Any
    flipped: Any
    small_sum: Any
    table: Any
    gain_sums: Any
    table_sum: Any
    small_in: Any
    small_sent: Any
    small_got: Any
    d_bands: Any


INPUTS, SMALL_INPUTS, OUTPUTS, KEPT_OUTPUTS = 9, 6, 13, 0


def layer_kernel(scale, *refs):
    r = Refs(*refs)
    me = lax.axis_index(PAGE)
    side = lax.axis_index(STREAM)
    flow = Flow(r, me, side)
    count, width = r.states.shape
    pairs = width // WIDE
    half_rows = count // 2
    core, y, z = lax.rem(me, 2), lax.rem(lax.div(me, 2), 2), lax.div(me, 4)
    partner = {STREAM: 1 - side}

    free = list(range(FETCHES))

    def fetch(source, target):
        return Fetch(source, target, r.fetched, free)

    def slot(name):
        return r.s.at[name]

    def tile_of(step):
        return pl.ds(pl.multiple_of(flip(z, DOWN_STEPS[step]) * width, WIDE), width)

    def columns(ref, first):
        return ref.at[:, width * first : width * (first + 1)]

    got_states = fetch(r.states, slot(Slot.second))
    got_q, got_k, got_v = [fetch(columns(r.w_qkv, i), r.w.at[i]) for i in range(3)]
    got_out = fetch(r.w_out, r.w.at[3])
    got_cq = fetch(r.w_cq, r.w.at[4])
    got_grad = fetch(r.cotangent, slot(Slot.low_grad))

    barrier = pltpu.get_barrier_semaphore()
    others = [{PAGE: flip(me, mask)} for mask in (1, 2, 4, 8, 12)] + [partner]
    for other in others:
        pl.semaphore_signal(barrier, 1, device_id=other, device_id_type=pl.DeviceIdType.MESH)

    own_count, other_count = r.counts[side], r.counts[1 - side]
    slots_row = lax.broadcasted_iota(jnp.int32, (1, count), 1)
    mask_own = jnp.where(slots_row < own_count, 0.0, MASKED).astype(F32)
    mask_other = jnp.where(slots_row < other_count, 0.0, MASKED).astype(F32)
    slots_column = lax.broadcasted_iota(jnp.int32, (count, 1), 0)
    valid = jnp.where(slots_column < own_count, 1.0, 0.0).astype(F32)
    buckets = WIDE // 2
    small = own_count <= GRID_SMALL * GRID_SMALL
    tall = [jnp.floor((slots_row.astype(F32) + 0.5) * (1.0 / grid)).astype(jnp.int32) for grid in (GRID_SMALL, GRID_LARGE)]
    grid_top = jnp.where(small, tall[0], tall[1])
    grid_left = slots_row - jnp.where(small, tall[0] * GRID_SMALL, tall[1] * GRID_LARGE)
    left = jnp.where(side == 0, r.box_x[...], grid_left)
    top = jnp.where(side == 0, r.box_y[...], grid_top)
    index = lax.broadcasted_iota(jnp.int32, (buckets, count), 0)

    def marks(first, second):
        both = [jnp.where(index == first, 1.0, 0.0), jnp.where(index == second, 1.0, 0.0)]
        return jnp.concatenate(both, 0).astype(BF)

    r.onehot[...] = marks(left, top)
    r.flipped[...] = marks(buckets - 1 - left, buckets - 1 - top)
    keep = same_block((WIDE, WIDE))
    lower = lax.broadcasted_iota(jnp.int32, (WIDE, WIDE), 0) >= buckets
    heads = 2 * pairs
    for head in range(heads):
        across = jnp.broadcast_to(r.table_in[head : head + 1, :], (WIDE, WIDE))
        down = jnp.broadcast_to(r.table_in[heads + head : heads + head + 1, :], (WIDE, WIDE))
        rolled = pltpu.roll(jnp.where(lower, down, across), buckets, 1, stride=1, stride_axis=0)
        r.bands[head // 2, head % 2] = jnp.where(keep, rolled, 0.0).astype(BF)

    def normed_copy(part):
        rows = pl.ds(part * half_rows, half_rows)
        return pltpu.make_async_remote_copy(
            src_ref=slot(Slot.normed).at[rows],
            dst_ref=slot(Slot.other).at[rows],
            send_sem=r.normed_sent.at[0],
            recv_sem=r.normed_got.at[part],
            device_id=partner,
            device_id_type=pl.DeviceIdType.MESH,
        )

    got_states.wait()
    for part in range(2):
        rows = slice(part * half_rows, (part + 1) * half_rows)
        inputs = r.s[Slot.second, rows, :].astype(F32)
        r.f[2, rows, :] = inputs
        r.s[Slot.normed, rows, :] = norm_rows(inputs, r.gain1[...]).astype(BF)
    pl.semaphore_wait(barrier, len(others))

    flow.start_weights()
    normed_copy(0).start()
    flow.tick(0.1)
    for name, copy, at in ((Slot.query, got_q, 0), (Slot.key, got_k, 1), (Slot.value, got_v, 2)):
        copy.wait()
        slot(name)[...] = contract(slot(Slot.normed)[...], r.w[at], 1, 0).astype(BF)
        flow.tick(1.0)
    held = [pltpu.make_async_copy(slot(name), r.held_out.at[i], r.stored.at[2 + i]) for i, name in enumerate((Slot.query, Slot.key, Slot.value))]
    for copy in held:
        copy.start()
    got_cout = fetch(r.w_cout, r.w.at[0])
    got_down = [fetch(r.w_down.at[tile_of(step)], r.w.at[1 + step]) for step in range(2)]

    def pair_loop(us, step, first=0, last=pairs):
        events = []
        for pair in range(first, last):
            flow.now += us
            events.append([])
            for entry in flow.due():
                events[-1].append(flow.plan(entry))

        @pl.loop(first, last)
        def _(pair):
            step(pair)
            for place, steps in enumerate(events, first):
                if steps:

                    @pl.when(pair == place)
                    def _(steps=steps):
                        for run in steps:
                            run()

    def lanes_of(pair):
        return pl.ds(pl.multiple_of(pair * WIDE, WIDE), WIDE)

    def self_forward(pair):
        lanes = lanes_of(pair)
        output, lse = forward_pair(
            scale,
            r.s[Slot.query, :, lanes],
            r.s[Slot.key, :, lanes],
            r.s[Slot.value, :, lanes],
            mask_own,
            (r.bands[pair], r.onehot[...]),
        )
        r.s[Slot.attended, :, lanes] = output
        r.self_lse[pair] = lse

        @pl.when(pair == pairs // 2)
        def _():
            normed_copy(1).start()

    pair_loop(1.95, self_forward)

    got_out.wait()
    r.f[2] = r.f[2] + contract(slot(Slot.attended)[...], r.w[3], 1, 0)
    slot(Slot.low_middle)[...] = r.f[2].astype(BF)
    got_down.append(fetch(r.w_down.at[tile_of(2)], r.w.at[3]))
    got_cq.wait()
    slot(Slot.cross_query)[...] = contract(slot(Slot.low_middle)[...], r.w[4], 1, 0).astype(BF)
    got_down.append(fetch(r.w_down.at[tile_of(3)], r.w.at[4]))
    flow.tick(2.2)
    got_grad.wait()
    slot(Slot.low_grad)[...] = (slot(Slot.low_grad)[...].astype(F32) * valid).astype(BF)
    flow.tick(0.5)

    back_slots = (Slot.back0, Slot.back1, Slot.back2, Slot.back3)
    hidden_slots = (Slot.query, Slot.key, Slot.value, Slot.hidden3)
    got_up = []
    for step in range(4):
        got_down[step].wait()
        r.s[back_slots[step]] = contract(slot(Slot.low_grad)[...], r.w[1 + step], 1, 1).astype(BF)
        got_up.append(fetch(r.w_up.at[:, tile_of(step)], r.w.at[1 + step]))
        flow.tick(1.05)
    flow.finish_weights()
    for copy in held:
        copy.wait()
    flow.now = max(flow.now, 30.0)
    for part in range(2):
        normed_copy(part).wait_recv()
        rows = slice(part * half_rows, (part + 1) * half_rows)
        for at, name in enumerate((Slot.cross_key, Slot.cross_value)):
            weight = r.other_w[at].reshape(width, width)
            r.s[name, rows, :] = contract(r.s[Slot.other, rows, :], weight, 1, 0).astype(BF)
    flow.tick(2.0)

    def cross_forward(pair):
        lanes = lanes_of(pair)
        output, lse = forward_pair(
            scale,
            r.s[Slot.cross_query, :, lanes],
            r.s[Slot.cross_key, :, lanes],
            r.s[Slot.cross_value, :, lanes],
            mask_other,
            None,
        )
        r.s[Slot.crossed, :, lanes] = output
        r.cross_lse[pair] = lse

    pair_loop(1.8, cross_forward)
    got_cout.wait()
    r.f[2] = r.f[2] + contract(slot(Slot.crossed)[...], r.w[0], 1, 0)
    for part in range(2):
        rows = slice(part * half_rows, (part + 1) * half_rows)
        r.s[Slot.second, rows, :] = norm_rows(r.f[2, rows, :], r.gain2[...]).astype(BF)
    flow.tick(2.0)

    second_at, grad_at = Slot.second, Slot.low_grad
    for step in range(4):
        hidden_at, d_up_at, up_at = hidden_slots[step], back_slots[step], 1 + step
        got_up[step].wait()

        for part in range(4):
            rows = slice(part * (count // 4), (part + 1) * (count // 4))
            hidden, slope = gelu_pair(contract(r.s[second_at, rows, :], r.w[up_at], 1, 0))
            r.s[hidden_at, rows, :] = hidden.astype(BF)
            r.s[d_up_at, rows, :] = (slope * r.s[d_up_at, rows, :].astype(F32)).astype(BF)

        flow.tick(2.0)
        flow.produce(UP_UNITS[step], r.s[second_at], r.s[d_up_at])
        flow.tick(0.1)
        flow.produce(DOWN_UNITS[step], r.s[hidden_at], r.s[grad_at])
        flow.tick(0.2)
    for step in range(4):
        for part in range(2):
            rows = slice(part * half_rows, (part + 1) * half_rows)
            back = contract(r.s[back_slots[step], rows, :], r.w[1 + step], 1, 1)
            r.f[0, rows, :] = back if step == 0 else r.f[0, rows, :] + back
        flow.tick(1.2)
    got_cq, got_out = fetch(r.w_cq, r.w.at[1]), fetch(r.w_out, r.w.at[2])
    got_q, got_k = [fetch(columns(r.w_qkv, i), r.w.at[3 + i]) for i in range(2)]

    low_after_at, d_crossed_at = Slot.back0, Slot.second
    r.small_sum[6:12, :] = fold(norm_back(r.f.at[2], r.f, 0, r.gain2, r.s, grad_at, low_after_at))
    flow.tick(1.7)
    r.s[d_crossed_at] = contract(r.s[low_after_at], r.w[0], 1, 1).astype(BF)
    got_v = fetch(columns(r.w_qkv, 2), r.w.at[0])
    flow.tick(1.1)
    flow.produce(8, slot(Slot.crossed)[...], r.s[low_after_at])
    flow.tick(0.1)

    d_query_at, d_key_at, d_value_at = Slot.back1, Slot.low_grad, Slot.d_value

    def cross_backward(pair):
        lanes = lanes_of(pair)
        d_query, d_key, d_value = backward_pair(
            scale,
            r.s[Slot.cross_query, :, lanes],
            r.s[Slot.cross_key, :, lanes],
            r.s[Slot.cross_value, :, lanes],
            r.s[d_crossed_at, :, lanes],
            r.s[Slot.crossed, :, lanes],
            r.cross_lse[pair],
            mask_other,
            None,
        )
        r.s[d_query_at, :, lanes] = d_query
        r.s[d_key_at, :, lanes] = d_key
        r.s[d_value_at, :, lanes] = d_value

    pair_loop(2.45, cross_backward)

    flow.produce(9, slot(Slot.other)[...], r.s[d_key_at])
    flow.tick(0.1)
    flow.produce(10, slot(Slot.other)[...], r.s[d_value_at])
    flow.tick(0.1)
    back_at = Slot.crossed
    r.s[back_at] = (
        contract(r.s[d_key_at], r.other_w[0].reshape(width, width), 1, 1)
        + contract(r.s[d_value_at], r.other_w[1].reshape(width, width), 1, 1)
    ).astype(BF)
    back_copy = pltpu.make_async_remote_copy(
        src_ref=r.s.at[back_at],
        dst_ref=slot(Slot.returned),
        send_sem=r.back_sent.at[0],
        recv_sem=r.back_got.at[0],
        device_id=partner,
        device_id_type=pl.DeviceIdType.MESH,
    )
    back_copy.start()
    flow.tick(2.0)
    got_states = fetch(r.states, r.s.at[d_key_at])

    query_at, key_at, value_at = Slot.back3, Slot.back0, Slot.d_value
    got_held = [fetch(r.held_out.at[i], r.s.at[at]) for i, at in enumerate((query_at, key_at, value_at))]

    flow.produce(11, slot(Slot.low_middle)[...], r.s[d_query_at])
    got_cq.wait()
    r.f[0] = r.f[0] + contract(r.s[d_query_at], r.w[1], 1, 1)
    d_middle_at, d_attended_at = Slot.cross_key, Slot.cross_value
    r.s[d_middle_at] = r.f[0].astype(BF)
    flow.tick(1.5)
    flow.produce(12, slot(Slot.attended)[...], r.s[d_middle_at])
    got_out.wait()
    r.s[d_attended_at] = contract(r.s[d_middle_at], r.w[2], 1, 1).astype(BF)
    got_down = [fetch(r.w_down.at[tile_of(step)], r.w.at[1 + step]) for step in range(2)]
    flow.tick(1.2)

    dq_at, dk_at, dv_at = Slot.cross_query, Slot.back2, Slot.second
    for copy in got_held:
        copy.wait()

    def self_backward(pair):
        lanes = lanes_of(pair)
        d_query, d_key, d_value, d_bands = backward_pair(
            scale,
            r.s[query_at, :, lanes],
            r.s[key_at, :, lanes],
            r.s[value_at, :, lanes],
            r.s[d_attended_at, :, lanes],
            r.s[Slot.attended, :, lanes],
            r.self_lse[pair],
            mask_own,
            (r.bands[pair], r.onehot[...], r.flipped[...]),
        )
        r.s[dq_at, :, lanes] = d_query
        r.s[dk_at, :, lanes] = d_key
        r.s[dv_at, :, lanes] = d_value
        r.d_bands[pair] = d_bands

    third = width // 3
    normed_at = Slot.normed
    for part in range(3):
        pair_loop(3.2, self_backward, part * pairs // 3, (part + 1) * pairs // 3)
        wanted = slice(part * third, (part + 1) * third)
        flow.produce(13 + part, r.s[normed_at], r.s[dq_at, :, wanted], r.s[dk_at, :, wanted], r.s[dv_at, :, wanted])
    for copy in (got_q, got_k, got_v):
        copy.wait()
    r.f[1] = (
        contract(r.s[dq_at], r.w[3], 1, 1)
        + contract(r.s[dk_at], r.w[4], 1, 1)
        + contract(r.s[dv_at], r.w[0], 1, 1)
    )
    got_down += [fetch(r.w_down.at[tile_of(step)], r.w.at[1 + step]) for step in range(2, 4)]
    flow.tick(3.2)
    for head in range(heads):
        across, down = unband(r.d_bands[head // 2, head % 2])
        r.small_sum[16 + head : 17 + head, :] = across
        r.small_sum[16 + heads + head : 17 + heads + head, :] = down
    flow.tick(1.0)
    got_states.wait()
    back_copy.wait_recv()
    for part in range(2):
        rows = slice(part * half_rows, (part + 1) * half_rows)
        r.f[1, rows, :] += r.s[Slot.returned, rows, :].astype(F32)
    gain1_grad = norm_back(r.s.at[d_key_at], r.f, 1, r.gain1, None, None, None)
    sent_states = pltpu.make_async_copy(r.f.at[0], r.states_out, r.stored.at[1])
    sent_states.start()
    r.small_sum[0:6, :] = fold(gain1_grad)
    r.small_sum[12:16, :] = jnp.zeros((4, WIDE), F32)
    flow.tick(2.0)

    flow.start_small()
    flow.tick(0.2)

    result_at = Slot.back3
    for step in range(4):
        got_down[step].wait()
        r.f[2] = r.f[2] + contract(r.s[hidden_slots[step]], r.w[1 + step], 1, 0)
        flow.tick(1.3)
    r.s[result_at] = (r.f[2] * valid).astype(BF)
    sent_result = pltpu.make_async_copy(r.s.at[result_at], r.result_out, r.stored.at[0])
    sent_result.start()
    flow.tick(0.4)
    flow.drain()
    gains = r.small_sum[...]
    shift = width - me * ROWS
    for place in range(2):
        row = jnp.concatenate([gains[6 * place + i : 6 * place + i + 1] for i in range(width // WIDE)], 1)
        r.gain_sums[place] = pltpu.roll(row, lax.rem(shift, width), 1)[:, :ROWS]
    flat = jnp.concatenate([gains[16:], jnp.zeros((WIDE - 2 * heads, WIDE), F32)], 0)
    r.table[...] = flat.T
    table_rows = r.table_out.shape[0]
    r.table_sum[...] = r.table[pl.ds(pl.multiple_of(me * table_rows, 8), table_rows), 0 : 2 * heads]
    last = [
        pltpu.make_async_copy(source, target, r.stored.at[5 + i])
        for i, (source, target) in enumerate(
            ((r.gain_sums.at[0], r.gain1_out), (r.gain_sums.at[1], r.gain2_out), (r.table_sum, r.table_out))
        )
    ]
    for copy in last:
        copy.start()
    for copy in last:
        copy.wait()
    back_copy.wait_send()
    sent_result.wait()
    sent_states.wait()


class Slot:
    (
        normed,
        other,
        query,
        key,
        value,
        attended,
        low_middle,
        cross_query,
        cross_key,
        cross_value,
        crossed,
        second,
        low_grad,
        hidden3,
        back0,
        back1,
        back2,
        back3,
        d_value,
        returned,
    ) = range(20)


SMALL = 99
SMALL_STEPS = (((0, 1),), ((1, 2),), ((2, 4), (3, 8), (4, 12)))


def fold(row):
    return jnp.concatenate([row[:, WIDE * i : WIDE * (i + 1)] for i in range(row.shape[1] // WIDE)], 0)


def norm_back(source, f, grad_at, gain, s, s_grad_at, s_out_at):
    count = f.shape[1]
    chunk = count // 4
    gain_grad = jnp.zeros((1, f.shape[2]), F32)
    for part in range(4):
        rows = slice(part * chunk, (part + 1) * chunk)
        inputs = source[rows, :].astype(F32)
        grad = f[grad_at, rows, :]
        centre = inputs - jnp.mean(inputs, axis=-1, keepdims=True)
        spread = lax.rsqrt(jnp.mean(centre * centre, axis=-1, keepdims=True) + EPSILON)
        normed = centre * spread
        gain_grad = gain_grad + jnp.sum(grad * normed, axis=0, keepdims=True)
        scaled = grad * gain[...]
        back = spread * (
            scaled
            - jnp.mean(scaled, axis=-1, keepdims=True)
            - normed * jnp.mean(scaled * normed, axis=-1, keepdims=True)
        )
        if s is not None:
            total = s[s_grad_at, rows, :].astype(F32) + back
            s[s_out_at, rows, :] = total.astype(BF)
        else:
            total = f[0, rows, :] + back
        f[0, rows, :] = total
    return gain_grad


def unband(grad):
    half = WIDE // 2
    rolled = pltpu.roll(jnp.where(same_block((WIDE, WIDE)), grad, 0.0), 1, 1, stride=1, stride_axis=0)
    return jnp.sum(rolled[:half], axis=0, keepdims=True), jnp.sum(rolled[half:], axis=0, keepdims=True)


def deliver_kernel(*refs):
    number = (len(refs) - 2) // 3
    sources, targets, held = refs[:number], refs[number : 2 * number], refs[2 * number : 3 * number]
    came, went = refs[-2:]
    arrivals = [pltpu.make_async_copy(sources[i], held[i], came.at[i]) for i in range(number)]
    departures = [pltpu.make_async_copy(held[i], targets[i], went.at[i]) for i in range(number)]
    for copy in arrivals:
        copy.start()
    for arrival, departure in zip(arrivals, departures):
        arrival.wait()
        departure.start()
    for copy in departures:
        copy.wait()


def deliver(arrays):
    anywhere = pl.BlockSpec(memory_space=pl.ANY)
    return pl.pallas_call(
        deliver_kernel,
        in_specs=[anywhere] * len(arrays),
        out_specs=[anywhere] * len(arrays),
        out_shape=[jax.ShapeDtypeStruct(array.shape, array.dtype) for array in arrays],
        scratch_shapes=[pltpu.VMEM(array.shape, array.dtype) for array in arrays]
        + [pltpu.SemaphoreType.DMA((len(arrays),))] * 2,
        compiler_params=params(63),
        cost_estimate=cost(3),
    )(*arrays)


def whole_layer(operands, scale):
    count, width = operands[0].shape
    hidden_width = operands[7].shape[1]
    heads = operands[-1].shape[0] // 2
    pairs = heads // 2
    rows = width // 16
    outs = [
        jax.ShapeDtypeStruct((count, width), BF),
        jax.ShapeDtypeStruct((count, width), F32),
        jax.ShapeDtypeStruct((3, count, width), BF),
        jax.ShapeDtypeStruct((4, rows, width), F32),
        jax.ShapeDtypeStruct((rows, hidden_width), F32),
        jax.ShapeDtypeStruct((rows, width), F32),
        jax.ShapeDtypeStruct((rows, width), F32),
        jax.ShapeDtypeStruct((rows, width), F32),
        jax.ShapeDtypeStruct((rows, 3 * width), F32),
        jax.ShapeDtypeStruct((rows, 2 * width), F32),
        jax.ShapeDtypeStruct((1, rows), F32),
        jax.ShapeDtypeStruct((1, rows), F32),
        jax.ShapeDtypeStruct((WIDE // 16, 2 * heads), F32),
    ]
    anywhere = pl.BlockSpec(memory_space=pl.ANY)
    inside = pl.BlockSpec(memory_space=pltpu.VMEM)
    scalars = pl.BlockSpec(memory_space=pltpu.SMEM)
    dma = pltpu.SemaphoreType.DMA
    small = (16 + 2 * heads, WIDE)
    scratch = [
        pltpu.VMEM((20, count, width), BF),
        pltpu.VMEM((3, count, width), F32),
        pltpu.VMEM((5, width, width), BF),
        dma((FETCHES,)),
        dma((8,)),
        pltpu.VMEM((width, width), BF),
        pltpu.VMEM((UNITS, 2, 4, rows, width), BF),
        pltpu.VMEM((RING, 2, 4, rows, width), BF),
        pltpu.VMEM((LANDINGS, 2, 4, rows, width), BF),
        pltpu.VMEM((len(Y_PLACES), 4, rows, width), BF),
        pltpu.VMEM((len(PLAIN_UNITS), 3, rows, width), BF),
        pltpu.VMEM((2, 2, 4, rows, width), BF),
        pltpu.VMEM((4, rows, width), BF),
        pltpu.VMEM((max(1, len(TURNED_UNITS)), 2, 2, 16 if not TURNED_UNITS else rows, width), BF),
        dma((RING,)),
        dma((LANDINGS,)),
        dma((2,)),
        dma((len(Y_PLACES) + 1,)),
        dma((2,)),
        dma((len(PLAIN_UNITS) + 2,)),
        dma((2,)),
        dma((len(PLAIN_UNITS) + 1,)),
        pltpu.SemaphoreType.REGULAR((UNITS - LANDINGS,)),
        dma((1,)),
        dma((2,)),
        dma((1,)),
        dma((1,)),
        dma((1,)),
        dma((2, 4)),
        pltpu.VMEM((2, 2, 2, 2, width // 8, width), BF),
        pltpu.VMEM((4 + len(PLAIN_UNITS), rows, width), F32),
        dma((STORES,)),
        pltpu.VMEM((rows, 2 * width), F32),
        pltpu.VMEM((rows, 2 * width), F32),
        dma((1,)),
        dma((1,)),
        pltpu.VMEM((pairs, 2, count), F32),
        pltpu.VMEM((pairs, 2, count), F32),
        pltpu.VMEM((pairs, 2, WIDE, WIDE), BF),
        pltpu.VMEM((WIDE, count), BF),
        pltpu.VMEM((WIDE, count), BF),
        pltpu.VMEM(small, F32),
        pltpu.VMEM((WIDE, WIDE), F32),
        pltpu.VMEM((2, 1, rows), F32),
        pltpu.VMEM((WIDE // 16, 2 * heads), F32),
        pltpu.VMEM((8, *small), F32),
        dma((1,)),
        dma((5,)),
        pltpu.VMEM((pairs, 2, WIDE, WIDE), F32),
    ]
    outputs = pl.pallas_call(
        functools.partial(layer_kernel, scale),
        in_specs=[anywhere] * INPUTS + [scalars] + [inside] * (SMALL_INPUTS - 1),
        out_specs=[anywhere] * OUTPUTS + [inside] * KEPT_OUTPUTS,
        out_shape=outs,
        scratch_shapes=scratch,
        compiler_params=pltpu.CompilerParams(
            collective_id=0, has_side_effects=True, vmem_limit_bytes=(64 << 20) - (256 << 10)
        ),
        cost_estimate=cost(150),
    )(*operands)
    down = outputs[3].reshape(4 * rows, width)
    return [*outputs[:2], down, *outputs[4:]]


def norm_rows(inputs, gain_row):
    centre = inputs - jnp.mean(inputs, axis=-1, keepdims=True)
    spread = jnp.mean(centre * centre, axis=-1, keepdims=True)
    return centre * lax.rsqrt(spread + EPSILON) * gain_row


def matmul(left, right):
    return contract(left, right, 1, 0)


def matmul_back(left, weight):
    return contract(left, weight, 1, 1)


def onehots(left, top, buckets):
    index = jnp.arange(buckets)[:, None]
    return jnp.concatenate([left[None, :] == index, top[None, :] == index], 0).astype(BF)


def body(
    states,
    counts,
    box_x,
    box_y,
    ln1_gain,
    ln2_gain,
    box_table,
    w_qkv,
    w_out,
    w_cq,
    w_ckv,
    w_cout,
    w_up,
    w_down,
    cotangent,
):
    slot_count, width = states.shape[2], states.shape[3]
    heads = box_table.shape[2] // 2
    buckets = box_table.shape[1] // 2
    scale = (width // heads) ** (-0.5)
    pairs = heads // 2
    parts = lax.axis_size(PAGE)
    side = lax.axis_index(STREAM)
    me = lax.axis_index(PAGE).astype(jnp.int32).reshape(1)
    own_count = jnp.take(counts[:, 0], side)
    other_count = jnp.take(counts[:, 0], 1 - side)
    slots = jnp.arange(slot_count)
    grid_side = jnp.where(own_count > GRID_SMALL * GRID_SMALL, GRID_LARGE, GRID_SMALL)
    left = jnp.where(side == 0, box_x[0], slots % grid_side)
    top = jnp.where(side == 0, box_y[0], slots // grid_side)
    onehot = onehots(left, top, buckets)
    flipped = onehots(buckets - 1 - left, buckets - 1 - top, buckets)
    mask_own = jnp.where(slots < own_count, 0.0, MASKED).astype(F32)[None]
    mask_other = jnp.where(slots < other_count, 0.0, MASKED).astype(F32)[None]
    valid = (slots < own_count).astype(F32)[:, None]
    bands = make_bands(box_table[0])
    weights = [w[0] for w in (w_qkv, w_out, w_cq, w_ckv, w_cout, w_up, w_down)]
    w_qkv, w_out, w_cq, w_ckv, w_cout, w_up, w_down = weights

    if parts == 16 and width == WIDTH and w_up.shape[1] == 4 * width:
        operands = [
            states[0, 0],
            cotangent[0, 0],
            w_qkv,
            w_out,
            w_cq,
            w_ckv,
            w_cout,
            w_up,
            w_down,
            counts[:, 0],
            box_x,
            box_y,
            ln1_gain,
            ln2_gain,
            box_table[0].T,
        ]
        result, states_grad, down, up, cout, cq, out, qkv, ckv, gain1, gain2, table = deliver(
            whole_layer(operands, scale)
        )
        return (
            result[None, None],
            states_grad[None, None],
            gain1,
            gain2,
            table[None],
            qkv[None],
            out[None],
            cq[None],
            ckv[None],
            cout[None],
            up[None],
            down[None],
        )

    inputs = states[0, 0].astype(F32)
    normed, norm_pull = jax.vjp(norm_rows, inputs, ln1_gain[0])
    normed = normed.astype(BF)
    cross_kv = matmul(normed, w_ckv).astype(BF)
    partner = swapped(cross_kv, STREAM, 1)
    joined = matmul(normed, w_qkv).astype(BF)
    attended, self_lse = attend_forward(joined, joined, pairs, mask_own, (bands, onehot), scale, 18)
    middle = inputs + matmul(attended, w_out)
    low_middle = middle.astype(BF)
    cross_query = matmul(low_middle, w_cq).astype(BF)
    crossed, cross_lse = attend_forward(cross_query, partner, 0, mask_other, None, scale, 16)
    after_cross = middle + matmul(crossed, w_cout)
    second, second_pull = jax.vjp(norm_rows, after_cross, ln2_gain[0])
    second = second.astype(BF)
    out_grad = cotangent[0, 0].astype(F32) * valid
    low_grad = out_grad.astype(BF)
    hidden, d_up, *down_parts = feed_forward(me, second, low_grad, w_up, w_down, parts)
    down_sum = reduce_parts(*down_parts)
    up_sum = reduce_parts(*outer_products(me, [(second, d_up)], parts, 6))
    d_after, ln2_grad = second_pull(matmul_back(d_up, w_up))
    d_after = d_after + out_grad
    low_after = d_after.astype(BF)
    d_crossed = matmul_back(low_after, w_cout).astype(BF)
    d_cross_query, d_partner = attend_backward(
        cross_query, partner, 0, d_crossed, crossed, cross_lse, mask_other, None, scale, 26
    )
    returned = swapped(d_partner, STREAM, 1)
    d_middle = d_after + matmul_back(d_cross_query, w_cq)
    low_d_middle = d_middle.astype(BF)
    d_attended = matmul_back(low_d_middle, w_out).astype(BF)
    mid_sum = reduce_parts(
        *outer_products(
            me, [(crossed, low_after), (low_middle, d_cross_query), (attended, low_d_middle)], parts, 6
        )
    )
    d_query, d_pair, d_bands = attend_backward(
        joined, joined, pairs, d_attended, attended, self_lse, mask_own, (bands, onehot, flipped), scale, 29
    )
    table_grad = gather_bands(d_bands)
    d_normed = (
        matmul_back(d_query, w_qkv[:, :width])
        + matmul_back(d_pair[0], w_qkv[:, width : 2 * width])
        + matmul_back(d_pair[1], w_qkv[:, 2 * width :])
        + matmul_back(returned[0], w_ckv[:, :width])
        + matmul_back(returned[1], w_ckv[:, width:])
    )
    d_inputs, ln1_grad = norm_pull(d_normed)
    states_grad = d_inputs + d_middle
    last_send, last_keep = outer_products(
        me,
        [
            (normed, d_query),
            (normed, d_pair[0]),
            (normed, d_pair[1]),
            (normed, returned[0]),
            (normed, returned[1]),
        ],
        parts,
        10,
    )
    last_sum = reduce_parts(last_send, last_keep)
    small = jnp.concatenate(
        [ln1_grad.reshape(parts, -1), ln2_grad.reshape(parts, -1), table_grad.reshape(parts, -1)], 1
    )
    small_sum = reduce_small(me[0], small)
    result = ((after_cross + matmul(hidden, w_down)) * valid).astype(BF)

    rows = width // parts
    table_rows = 2 * buckets // parts

    def wide(block):
        return block.reshape(-1, rows, width).transpose(1, 0, 2).reshape(1, rows, -1)

    return (
        result[None, None],
        states_grad[None, None],
        small_sum[None, :rows],
        small_sum[None, rows : 2 * rows],
        small_sum[2 * rows :].reshape(1, table_rows, 2 * heads),
        wide(last_sum[: 3 * rows]),
        wide(mid_sum[2 * rows :]),
        wide(mid_sum[rows : 2 * rows]),
        wide(last_sum[3 * rows :]),
        wide(mid_sum[:rows]),
        wide(up_sum),
        down_sum[None],
    )


def reduce_small(me, small):
    parts = small.shape[0]
    order = jnp.arange(parts) ^ me
    small = jnp.take(small, order, axis=0).reshape(parts // 4, 2, 2, -1)
    small = small[:, :, 0] + swapped(small[:, :, 1], PAGE, 1)
    small = small[:, 0] + swapped(small[:, 1], PAGE, 2)
    total = small[0]
    for step in range(1, parts // 4):
        total = total + swapped(small[step], PAGE, 4 * step)
    return total


def solution(mesh):
    placed = (
        P(STREAM, PAGE, None, None),
        P(None, PAGE),
        P(PAGE, None),
        P(PAGE, None),
        P(STREAM, None),
        P(STREAM, None),
        P(STREAM, None, None),
        P(STREAM, None, None),
        P(STREAM, None, None),
        P(STREAM, None, None),
        P(STREAM, None, None),
        P(STREAM, None, None),
        P(STREAM, None, None),
        P(STREAM, None, None),
        P(STREAM, PAGE, None, None),
    )
    return jax.shard_map(
        body,
        mesh=mesh,
        in_specs=placed,
        out_specs=(
            P(STREAM, PAGE, None, None),
            P(STREAM, PAGE, None, None),
            P(STREAM, PAGE),
            P(STREAM, PAGE),
            P(STREAM, PAGE, None),
            P(STREAM, PAGE, None),
            P(STREAM, PAGE, None),
            P(STREAM, PAGE, None),
            P(STREAM, PAGE, None),
            P(STREAM, PAGE, None),
            P(STREAM, PAGE, None),
            P(STREAM, PAGE, None),
        ),
        check_vma=False,
    )
```
